32 devices in a mesh: ctx: 8 (over z, x), tp: 4 (over y, core).
Axes of the slice: x: 2, y: 2, z: 4, core: 2. Of those that a mesh axis runs over, the one named last changes fastest.
Arguments:
- trace_q: bfloat16 [1024, 5120], P(('ctx', 'tp')), may hold values from -120 to 120
- trace_key_value: bfloat16 [1024, 2048], P(('ctx', 'tp')), may hold values from -6 to 6
- suffix_q: bfloat16 [8, 128, 5120], P('ctx', 'tp'), may hold values from -120 to 120
- suffix_key_value: bfloat16 [8, 128, 2048], P('ctx', 'tp'), may hold values from -6 to 6
- prefix_len: int32 [8], P('ctx'), may hold values from 256 to 1024, as said below
- del_start: int32 [8], P('ctx'), may hold values from 0 to 1023, as said below
- del_end: int32 [8], P('ctx'), may hold values from 1 to 1024, as said below
Outputs:
- trace_out: bfloat16 [1024, 5120], P(('ctx', 'tp'))
- suffix_out: bfloat16 [8, 128, 5120], P('ctx', 'tp')
The draws below stay inside these ranges and needn't reach their ends.
Inputs may be any that keep to these rules, and one draw needn't show every extreme that they name: `prefix_len`: one variant keeps the whole trace as prefix and deletes only its last position. del_start < prefix_len of the same variant. del_start < del_end <= prefix_len of the same variant, and del_end - del_start <= 128.
All inputs are finite; a program needn't handle non-finite values.
Results may differ from the reference program's by a relative error of at most 0.0075.
Values may be sent and summed in bfloat16 or wider, within the bound.
No kernel may reach another device: no remote copies, remote signals or barrier semaphores. Data moves between devices by JAX's collectives and lax.ppermute only.
A program may use at most 192 MiB of HBM per device.

```python
import jax
import jax.numpy as jnp
from jax import lax

QUERY_HEADS = 40
KEY_VALUE_HEADS = 8
HEAD_SIZE = 128
TOK_DEV = 128
SUFFIX_LENGTH = 128
TRACE_LENGTH = 1024
VARIANT_COUNT = 8
N_CTX = 8


def bounded_normal_draw(key, shape):
    return jnp.clip(jax.random.normal(key, shape, jnp.float32), -6.0, 6.0)


def drawn_queries(key, shape, salt):
    query_matrix = bounded_normal_draw(jax.random.fold_in(key, salt), shape)
    return query_matrix


def value_portion(key, shape, salt):
    return bounded_normal_draw(jax.random.fold_in(key, salt), shape)


def starting_trace_keys(key):
    return bounded_normal_draw(jax.random.fold_in(key, 101), (TRACE_LENGTH, KEY_VALUE_HEADS, HEAD_SIZE))


def starting_suffix_keys(key):
    return bounded_normal_draw(jax.random.fold_in(key, 111), (VARIANT_COUNT, SUFFIX_LENGTH, KEY_VALUE_HEADS, HEAD_SIZE))


def draw_trace_key_value(key, part):
    stacked_pairs = jnp.stack([starting_trace_keys(key), value_portion(key, (TRACE_LENGTH, KEY_VALUE_HEADS, HEAD_SIZE), 102)], axis=2)
    return stacked_pairs.reshape(TRACE_LENGTH, KEY_VALUE_HEADS * 2 * HEAD_SIZE).astype(jnp.bfloat16)


def draw_trace_q(key, part):
    query_matrix = drawn_queries(key, (TRACE_LENGTH, QUERY_HEADS, HEAD_SIZE), 103)
    return query_matrix.reshape(TRACE_LENGTH, QUERY_HEADS * HEAD_SIZE).astype(jnp.bfloat16)


def draw_suffix_key_value(key, part):
    stacked_pairs = jnp.stack([starting_suffix_keys(key), value_portion(key, (VARIANT_COUNT, SUFFIX_LENGTH, KEY_VALUE_HEADS, HEAD_SIZE), 112)], axis=3)
    return stacked_pairs.reshape(VARIANT_COUNT, SUFFIX_LENGTH, KEY_VALUE_HEADS * 2 * HEAD_SIZE).astype(jnp.bfloat16)


def draw_suffix_q(key, part):
    query_matrix = drawn_queries(key, (VARIANT_COUNT, SUFFIX_LENGTH, QUERY_HEADS, HEAD_SIZE), 113)
    return query_matrix.reshape(VARIANT_COUNT, SUFFIX_LENGTH, QUERY_HEADS * HEAD_SIZE).astype(jnp.bfloat16)


def deletion_spans(key):
    prefix = jax.random.randint(jax.random.fold_in(key, 201), (VARIANT_COUNT,), TRACE_LENGTH // 4, TRACE_LENGTH + 1)
    chosen_row = jax.random.randint(jax.random.fold_in(key, 202), (), 0, VARIANT_COUNT)
    is_chosen = jnp.arange(VARIANT_COUNT) == chosen_row
    prefix = jnp.where(is_chosen, TRACE_LENGTH, prefix).astype(jnp.int32)
    first = jax.random.randint(jax.random.fold_in(key, 203), (VARIANT_COUNT,), 0, prefix)
    span_size = jax.random.randint(jax.random.fold_in(key, 204), (VARIANT_COUNT,), 1, TRACE_LENGTH // 8 + 1)
    last = jnp.minimum(first + span_size, prefix)
    first = jnp.where(is_chosen, TRACE_LENGTH - 1, first)
    last = jnp.where(is_chosen, TRACE_LENGTH, last)
    return (prefix.astype(jnp.int32), first.astype(jnp.int32), last.astype(jnp.int32))


def draw_prefix_len(key, part):
    return deletion_spans(key)[0]


def draw_del_start(key, part):
    return deletion_spans(key)[1]


def draw_del_end(key, part):
    return deletion_spans(key)[2]


def setup_inputs(seed: int = 0) -> dict:
    arg_keys = jax.random.split(jax.random.key(seed), 8)
    return {
        "trace_q": draw_trace_q(jax.random.fold_in(arg_keys[7], 71), 0),
        "trace_key_value": draw_trace_key_value(jax.random.fold_in(arg_keys[7], 71), 0),
        "suffix_q": draw_suffix_q(jax.random.fold_in(arg_keys[7], 71), 0),
        "suffix_key_value": draw_suffix_key_value(jax.random.fold_in(arg_keys[7], 71), 0),
        "prefix_len": draw_prefix_len(jax.random.fold_in(arg_keys[7], 71), 0),
        "del_start": draw_del_start(jax.random.fold_in(arg_keys[7], 71), 0),
        "del_end": draw_del_end(jax.random.fold_in(arg_keys[7], 71), 0),
    }


def attend(query_matrix, key_rows, value_rows, allowed):
    element_count = query_matrix.shape[0]
    queries_per_group = QUERY_HEADS // KEY_VALUE_HEADS
    query_groups = query_matrix.reshape(element_count, KEY_VALUE_HEADS, queries_per_group, HEAD_SIZE).astype(jnp.float32)
    scores = jnp.einsum("qgjd,kgd->qgjk", query_groups, key_rows.astype(jnp.float32)) * (HEAD_SIZE ** -0.5)
    visible = allowed[:, None, None, :]
    largest = jnp.max(jnp.where(visible, scores, -1e30), axis=-1, keepdims=True)
    weights = jnp.where(visible, jnp.exp(scores - largest), 0.0)
    denominator = jnp.sum(weights, axis=-1)
    rounded = lax.optimization_barrier(weights.astype(jnp.bfloat16)).astype(jnp.float32)
    summed = jnp.einsum("qgjk,kgd->qgjd", rounded, value_rows.astype(jnp.float32))
    result = summed / denominator[..., None]
    return result.reshape(element_count, QUERY_HEADS * HEAD_SIZE).astype(jnp.bfloat16)


def reference(trace_q, trace_key_value, suffix_q, suffix_key_value, prefix_len, del_start, del_end):
    key_value_pairs = trace_key_value.reshape(TRACE_LENGTH, KEY_VALUE_HEADS, 2, HEAD_SIZE)
    trace_keys = key_value_pairs[:, :, 0]
    trace_values = key_value_pairs[:, :, 1]
    positions = jnp.arange(TRACE_LENGTH, dtype=jnp.int32)
    blocks = trace_q.reshape(N_CTX, TOK_DEV, QUERY_HEADS * HEAD_SIZE)

    def one_block(inputs):
        block_queries, number = inputs
        query_pos = number * TOK_DEV + jnp.arange(TOK_DEV, dtype=jnp.int32)
        allowed = positions[None, :] <= query_pos[:, None]
        return attend(block_queries, trace_keys, trace_values, allowed)

    trace_out = lax.map(one_block, (blocks, jnp.arange(N_CTX, dtype=jnp.int32))).reshape(TRACE_LENGTH, QUERY_HEADS * HEAD_SIZE)
    suffix_key_value_pairs = suffix_key_value.reshape(VARIANT_COUNT, SUFFIX_LENGTH, KEY_VALUE_HEADS, 2, HEAD_SIZE)
    own_rows = jnp.arange(SUFFIX_LENGTH, dtype=jnp.int32)

    def one_variant(inputs):
        query_matrix, variant_pairs, prefix, first, last = inputs
        key_rows = jnp.concatenate([trace_keys, variant_pairs[:, :, 0]], axis=0)
        value_rows = jnp.concatenate([trace_values, variant_pairs[:, :, 1]], axis=0)
        kept = (positions < prefix) & ((positions < first) | (positions >= last))
        prefix_ok = jnp.broadcast_to(kept[None, :], (SUFFIX_LENGTH, TRACE_LENGTH))
        self_ok = own_rows[None, :] <= own_rows[:, None]
        allowed = jnp.concatenate([prefix_ok, self_ok], axis=1)
        return attend(query_matrix, key_rows, value_rows, allowed)

    suffix_out = lax.map(one_variant, (suffix_q, suffix_key_value_pairs, prefix_len, del_start, del_end))
    return trace_out, suffix_out
```

```python
import functools

import jax
import jax.numpy as jnp
from jax import lax
from jax.experimental import pallas as pl
from jax.experimental.pallas import tpu as pltpu
from jax.sharding import PartitionSpec as P

QUERY_HEADS = 40
KEY_VALUE_HEADS = 8
HEAD_SIZE = 128
GROUP = QUERY_HEADS // KEY_VALUE_HEADS
PAIR = 2 * HEAD_SIZE
LOG2E = 1.4426950408889634
SCALE = HEAD_SIZE ** (-0.5) * LOG2E
MASKED = -1e30
CHUNK_ROWS = 1024


def dot_t(a, b):
    return lax.dot_general(a, b, (((1,), (1,)), ((), ())), preferred_element_type=jnp.float32)


def dot(a, b):
    return lax.dot_general(a, b, (((1,), (0,)), ((), ())), preferred_element_type=jnp.float32)


def attend_kernel(piece_rows, first_call, last_call, *refs):
    refs = list(refs)
    starts, place, span = refs[:3]
    tq, sq = refs[3:5]
    del refs[:5]
    own_pieces = []
    if first_call:
        own_pieces, refs = refs[:4], refs[4:]
    pieces, refs = refs[: len(piece_rows)], refs[len(piece_rows):]
    if not first_call:
        m_in, l_in, acc_in = refs[:3]
        del refs[:3]
    if last_call:
        t_out, s_out = refs[:2]
        del refs[:2]
    else:
        m_out, l_out, acc_out = refs[:3]
        del refs[:3]
    kv, sems = refs

    rows = tq.shape[0]
    total = sum(piece_rows)
    copies, at = [], 0
    for index, (piece, size) in enumerate(zip(pieces, piece_rows)):
        copies.append(pltpu.make_async_copy(piece, kv.at[pl.ds(at, size)], sems.at[index]))
        at += size
    for index, piece in enumerate(own_pieces):
        copies.append(
            pltpu.make_async_copy(piece, kv.at[pl.ds(at, rows)], sems.at[len(piece_rows) + index])
        )
        at += rows
    for copy in copies:
        copy.start()

    first_position = place[0]
    suffix_row = place[1]
    prefix, del_start, del_end = span[0], span[1], span[2]
    lanes = 128
    lane = lax.broadcasted_iota(jnp.int32, (rows, lanes), 1)
    row = lax.broadcasted_iota(jnp.int32, (rows, lanes), 0)
    q_trace_aug = jnp.where(lane == row, 1.0, 0.0).astype(jnp.bfloat16)
    q_suffix_aug = jnp.where((lane == rows) | (lane == rows + 1 + row), 1.0, 0.0).astype(jnp.bfloat16)
    q_aug = jnp.concatenate([q_trace_aug] * GROUP + [q_suffix_aug] * GROUP, axis=0)
    k_aug = []
    for index, size in enumerate(piece_rows):
        lane_k = lax.broadcasted_iota(jnp.int32, (size, lanes), 1)
        position = starts[index] + lax.broadcasted_iota(jnp.int32, (size, lanes), 0)
        hidden_trace = (lane_k < rows) & (position > first_position + lane_k)
        hidden_suffix = (lane_k == rows) & (
            (position >= prefix) | ((position >= del_start) & (position < del_end))
        )
        k_aug.append(jnp.where(hidden_trace | hidden_suffix, MASKED, 0.0).astype(jnp.bfloat16))
    k_aug = jnp.concatenate(k_aug, axis=0)
    if first_call:
        own_aug = []
        for index in range(len(own_pieces)):
            position = place[2 + index] + row
            hidden = (lane > rows) & (position > suffix_row + (lane - rows - 1))
            own_aug.append(jnp.where(hidden, MASKED, 0.0).astype(jnp.bfloat16))
        own_aug = jnp.concatenate(own_aug, axis=0)
        own_total = rows * len(own_pieces)
        own_ones = jnp.ones((own_total, HEAD_SIZE), jnp.bfloat16)
    ones = jnp.ones((total, HEAD_SIZE), jnp.bfloat16)
    for copy in copies:
        copy.wait()

    half = GROUP * rows
    for g in range(KEY_VALUE_HEADS):
        def heads(ref):
            return [ref[:, (g * GROUP + j) * HEAD_SIZE:(g * GROUP + j + 1) * HEAD_SIZE] for j in range(GROUP)]

        query = jnp.concatenate(heads(tq) + heads(sq), axis=0)
        query = jnp.concatenate([query, q_aug], axis=1)
        key = kv[0:total, g * PAIR:g * PAIR + HEAD_SIZE]
        value = kv[0:total, g * PAIR + HEAD_SIZE:(g + 1) * PAIR]
        scores = dot_t(query, jnp.concatenate([key, k_aug], axis=1))
        top = jnp.max(scores, axis=1, keepdims=True)
        if first_call:
            own_key = kv[total:total + own_total, g * PAIR:g * PAIR + HEAD_SIZE]
            own_value = kv[total:total + own_total, g * PAIR + HEAD_SIZE:(g + 1) * PAIR]
            own_scores = dot_t(query[half:], jnp.concatenate([own_key, own_aug], axis=1))
            own_top = jnp.maximum(top[half:], jnp.max(own_scores, axis=1, keepdims=True))
            top = jnp.concatenate([top[:half], own_top], axis=0)
        else:
            old = m_in[g * 2 * half:(g + 1) * 2 * half, :]
            top = jnp.maximum(old, top)
        weights = jnp.exp2((scores - top[:, 0:1]) * SCALE).astype(jnp.bfloat16)
        both = dot(weights, jnp.concatenate([value, ones], axis=1))
        summed, denominator = both[:, :HEAD_SIZE], both[:, HEAD_SIZE:]
        if first_call:
            own_weights = jnp.exp2((own_scores - top[half:]) * SCALE).astype(jnp.bfloat16)
            own_both = dot(own_weights, jnp.concatenate([own_value, own_ones], axis=1))
            summed = jnp.concatenate([summed[:half], summed[half:] + own_both[:, :HEAD_SIZE]], axis=0)
            denominator = jnp.concatenate(
                [denominator[:half], denominator[half:] + own_both[:, HEAD_SIZE:]], axis=0
            )
        else:
            here = slice(g * 2 * half, (g + 1) * 2 * half)
            rescale = jnp.exp2((old - top) * SCALE)
            summed = summed + acc_in[here, :] * rescale
            denominator = denominator + l_in[here, :] * rescale
        if last_call:
            result = (summed / denominator).astype(jnp.bfloat16)
            for j in range(GROUP):
                columns = slice((g * GROUP + j) * HEAD_SIZE, (g * GROUP + j + 1) * HEAD_SIZE)
                t_out[:, columns] = result[j * rows:(j + 1) * rows]
                s_out[:, columns] = result[half + j * rows:half + (j + 1) * rows]
        else:
            here = slice(g * 2 * half, (g + 1) * 2 * half)
            m_out[here, :] = jnp.broadcast_to(top, (2 * half, HEAD_SIZE))
            l_out[here, :] = denominator
            acc_out[here, :] = summed


def attend(starts, place, span, tq, sq, own_pieces, pieces, carry, last_call):
    first_call = carry is None
    piece_rows = tuple(p.shape[0] for p in pieces)
    rows = tq.shape[0]
    own_count = 4 if first_call else 0
    smem = pl.BlockSpec(memory_space=pltpu.SMEM)
    vmem = pl.BlockSpec(memory_space=pltpu.VMEM)
    hbm = pl.BlockSpec(memory_space=pl.ANY)
    operands = [starts, place, span, tq, sq]
    in_specs = [smem, smem, smem, vmem, vmem]
    if first_call:
        operands += list(own_pieces)
        in_specs += [hbm] * own_count
    operands += list(pieces)
    in_specs += [hbm] * len(pieces)
    if not first_call:
        operands += list(carry)
        in_specs += [vmem] * 3
    if last_call:
        out_shape = [jax.ShapeDtypeStruct(tq.shape, jnp.bfloat16)] * 2
    else:
        state = jax.ShapeDtypeStruct((2 * QUERY_HEADS * rows, HEAD_SIZE), jnp.float32)
        out_shape = [state] * 3
    all_rows = sum(piece_rows) + own_count * rows
    flops = 2 * 2 * QUERY_HEADS * rows * all_rows * PAIR * 2
    return pl.pallas_call(
        functools.partial(attend_kernel, piece_rows, first_call, last_call),
        out_shape=out_shape,
        in_specs=in_specs,
        out_specs=[vmem] * len(out_shape),
        scratch_shapes=[
            pltpu.VMEM((all_rows, tq.shape[1] // GROUP * 2), jnp.bfloat16),
            pltpu.SemaphoreType.DMA((len(pieces) + own_count,)),
        ],
        compiler_params=pltpu.CompilerParams(vmem_limit_bytes=48 * 1024 * 1024),
        cost_estimate=pl.CostEstimate(
            flops=flops, bytes_accessed=all_rows * 4096, transcendentals=2 * QUERY_HEADS * rows * all_rows
        ),
    )(*operands)


def swap(array, axis, bit, size):
    return lax.ppermute(array, axis, [(i, i ^ bit) for i in range(size)])


def local(ctx_size, tp_size, trace_q, trace_key_value, suffix_q, suffix_key_value, prefix_len, del_start, del_end):
    rows = trace_q.shape[0]
    ctx = lax.axis_index("ctx").astype(jnp.int32)
    tp = lax.axis_index("tp").astype(jnp.int32)
    span = jnp.concatenate([prefix_len, del_start, del_end])
    sq = suffix_q[0]
    suffix_own = suffix_key_value[0]

    core = lambda a: swap(a, "tp", 1, tp_size)
    across_y = lambda a: swap(a, "tp", 2, tp_size)
    across_x = lambda a: swap(a, "ctx", 1, ctx_size)

    suffix_y = across_y(suffix_own)
    suffix_pieces = [suffix_own, suffix_y, core(suffix_own), core(suffix_y)]
    suffix_tp = [tp, tp ^ 2, tp ^ 1, tp ^ 3]
    place = jnp.stack([(ctx * tp_size + tp) * rows, tp * rows] + [t * rows for t in suffix_tp])

    if ctx_size == 8:
        planes = ctx_size // 2
        pieces, starts = [], []

        def add(piece, piece_ctx, piece_tp):
            pieces.append(piece)
            starts.append((piece_ctx * tp_size + piece_tp) * rows)
            pieces.append(core(piece))
            starts.append((piece_ctx * tp_size + (piece_tp ^ 1)) * rows)

        for shift in (0, 1, 3, 2):
            if shift == 0:
                mine = trace_key_value
            else:
                mine = lax.ppermute(
                    trace_key_value, "ctx", [(i, (i + 2 * shift) % ctx_size) for i in range(ctx_size)]
                )
            source = (ctx - 2 * shift) % ctx_size
            from_x = across_x(mine)
            from_y = across_y(mine)
            diagonal = across_x(from_y) if shift in (0, 1) else across_y(from_x)
            add(mine, source, tp)
            add(from_x, source ^ 1, tp)
            add(from_y, source, tp ^ 2)
            add(diagonal, source ^ 1, tp ^ 2)
        groups = [(pieces, jnp.stack(starts))]
    else:
        gathered = lax.all_gather(trace_key_value, ("ctx", "tp"), axis=0, tiled=True)
        groups = [
            ([gathered[at:at + CHUNK_ROWS]], jnp.full((1,), at, jnp.int32))
            for at in range(0, gathered.shape[0], CHUNK_ROWS)
        ]

    carry = None
    for index, (group, group_starts) in enumerate(groups):
        carry = attend(
            group_starts, place, span, trace_q, sq, suffix_pieces, group, carry, index == len(groups) - 1
        )
    trace_out, suffix_out = carry
    return trace_out, suffix_out[None]


def solution(mesh):
    return jax.shard_map(
        functools.partial(local, mesh.shape["ctx"], mesh.shape["tp"]),
        mesh=mesh,
        in_specs=(
            P(("ctx", "tp"), None),
            P(("ctx", "tp"), None),
            P("ctx", "tp", None),
            P("ctx", "tp", None),
            P("ctx"),
            P("ctx"),
            P("ctx"),
        ),
        out_specs=(P(("ctx", "tp"), None), P("ctx", "tp", None)),
        check_vma=False,
    )
```

```python
import functools

import jax
import jax.numpy as jnp
from jax import lax
from jax.experimental import pallas as pl
from jax.experimental.pallas import tpu as pltpu
from jax.sharding import PartitionSpec as P

QUERY_HEADS = 40
KEY_VALUE_HEADS = 8
HEAD_SIZE = 128
GROUP = QUERY_HEADS // KEY_VALUE_HEADS
PAIR = 2 * HEAD_SIZE
LOG2E = 1.4426950408889634
SCALE = HEAD_SIZE ** (-0.5) * LOG2E
MASKED = -1e30
CHUNK_ROWS = 1024
OWN_ORDER = (0, 2, 1, 3)


def dot_t(a, b):
    return lax.dot_general(a, b, (((1,), (1,)), ((), ())), preferred_element_type=jnp.float32)


def dot(a, b):
    return lax.dot_general(a, b, (((1,), (0,)), ((), ())), preferred_element_type=jnp.float32)


def attend_kernel(slots, own_order, own_count, tp_size, first_call, last_call, *refs):
    refs = list(refs)
    prefix_ref, del_start_ref, del_end_ref, tq, sq = refs[:5]
    del refs[:5]
    own_pieces, refs = refs[:own_count], refs[own_count:]
    piece_count = len(refs) - 2 - (2 if not first_call else 0) - 2
    pieces, refs = refs[:piece_count], refs[piece_count:]
    if not first_call:
        stats_in, sum_in = refs[:2]
        del refs[:2]
    out_a, out_b, kv, sems = refs

    rows = tq.shape[0]
    copies, at = [], 0
    for index, piece in enumerate(list(pieces) + list(own_pieces)):
        size = piece.shape[0]
        copies.append(pltpu.make_async_copy(piece, kv.at[pl.ds(at, size)], sems.at[index]))
        at += size
    for copy in copies:
        copy.start()

    ctx = lax.axis_index("ctx").astype(jnp.int32)
    tp = lax.axis_index("tp").astype(jnp.int32)
    first_position = (ctx * tp_size + tp) * rows
    prefix, del_start, del_end = prefix_ref[0], del_start_ref[0], del_end_ref[0]
    lanes = 128
    lane = lax.broadcasted_iota(jnp.int32, (rows, lanes), 1)
    row = lax.broadcasted_iota(jnp.int32, (rows, lanes), 0)
    q_trace_aug = jnp.where(lane == row, 1.0, 0.0).astype(jnp.bfloat16)
    q_suffix_aug = jnp.where((lane == rows) | (lane == rows + 1 + row), 1.0, 0.0).astype(jnp.bfloat16)
    q_aug = jnp.concatenate([q_trace_aug] * GROUP + [q_suffix_aug] * GROUP, axis=0)
    k_aug = []
    for slot in slots:
        position = slot(ctx, tp) * rows + row
        hidden_trace = (lane < rows) & (position > first_position + lane)
        hidden_suffix = (lane == rows) & (
            (position >= prefix) | ((position >= del_start) & (position < del_end))
        )
        k_aug.append(jnp.where(hidden_trace | hidden_suffix, MASKED, 0.0).astype(jnp.bfloat16))
    k_aug = jnp.concatenate(k_aug, axis=0)
    total = rows * len(slots)
    if first_call:
        own_aug = []
        for flip in own_order:
            position = (tp ^ flip) * rows + row
            hidden = (lane > rows) & (position > tp * rows + (lane - rows - 1))
            own_aug.append(jnp.where(hidden, MASKED, 0.0).astype(jnp.bfloat16))
        own_aug = jnp.concatenate(own_aug, axis=0)
        own_total = rows * len(own_order)
        own_ones = jnp.ones((own_total, HEAD_SIZE), jnp.bfloat16)
    ones = jnp.ones((total, HEAD_SIZE), jnp.bfloat16)
    for copy in copies:
        copy.wait()

    half = GROUP * rows
    lane_out = lax.broadcasted_iota(jnp.int32, (2 * half, HEAD_SIZE), 1)
    for g in range(KEY_VALUE_HEADS):
        def heads(ref):
            return [ref[:, (g * GROUP + j) * HEAD_SIZE:(g * GROUP + j + 1) * HEAD_SIZE] for j in range(GROUP)]

        here = slice(g * 2 * half, (g + 1) * 2 * half)
        query = jnp.concatenate(heads(tq) + heads(sq), axis=0)
        query = jnp.concatenate([query, q_aug], axis=1)
        key = kv[0:total, g * PAIR:g * PAIR + HEAD_SIZE]
        value = kv[0:total, g * PAIR + HEAD_SIZE:(g + 1) * PAIR]
        scores = dot_t(query, jnp.concatenate([key, k_aug], axis=1))
        top = jnp.max(scores, axis=1, keepdims=True)
        if first_call:
            own_key = kv[total:total + own_total, g * PAIR:g * PAIR + HEAD_SIZE]
            own_value = kv[total:total + own_total, g * PAIR + HEAD_SIZE:(g + 1) * PAIR]
            own_scores = dot_t(query[half:], jnp.concatenate([own_key, own_aug], axis=1))
            own_top = jnp.maximum(top[half:], jnp.max(own_scores, axis=1, keepdims=True))
            top = jnp.concatenate([top[:half], own_top], axis=0)
        else:
            old_top = stats_in[here, 0:1]
            top = jnp.maximum(old_top, top)
        weights = jnp.exp2((scores - top) * SCALE).astype(jnp.bfloat16)
        both = dot(weights, jnp.concatenate([value, ones], axis=1))
        summed, denominator = both[:, :HEAD_SIZE], both[:, HEAD_SIZE:]
        if first_call:
            own_weights = jnp.exp2((own_scores - top[half:]) * SCALE).astype(jnp.bfloat16)
            own_both = dot(own_weights, jnp.concatenate([own_value, own_ones], axis=1))
            summed = jnp.concatenate([summed[:half], summed[half:] + own_both[:, :HEAD_SIZE]], axis=0)
            denominator = jnp.concatenate(
                [denominator[:half], denominator[half:] + own_both[:, HEAD_SIZE:]], axis=0
            )
        else:
            rescale = jnp.exp2((old_top - top) * SCALE)
            summed = summed + sum_in[here, :] * rescale
            denominator = denominator + stats_in[here, 1:2] * rescale
        if last_call:
            result = (summed / denominator).astype(jnp.bfloat16)
            for j in range(GROUP):
                columns = slice((g * GROUP + j) * HEAD_SIZE, (g * GROUP + j + 1) * HEAD_SIZE)
                out_a[:, columns] = result[j * rows:(j + 1) * rows]
                out_b[:, columns] = result[half + j * rows:half + (j + 1) * rows]
        else:
            out_a[here, :] = jnp.where(lane_out == 0, top, denominator)
            out_b[here, :] = summed


def attend(spans, tq, sq, own_pieces, pieces, slots, tp_size, carry, last_call):
    first_call = carry is None
    rows = tq.shape[0]
    own_pieces = list(own_pieces) if first_call else []
    smem = pl.BlockSpec(memory_space=pltpu.SMEM)
    vmem = pl.BlockSpec(memory_space=pltpu.VMEM)
    hbm = pl.BlockSpec(memory_space=pl.ANY)
    operands = [*spans, tq, sq, *own_pieces, *pieces]
    in_specs = [smem] * 3 + [vmem] * 2 + [hbm] * (len(own_pieces) + len(pieces))
    if not first_call:
        operands += list(carry)
        in_specs += [vmem] * 2
    if last_call:
        out_shape = [jax.ShapeDtypeStruct(tq.shape, jnp.bfloat16)] * 2
    else:
        out_shape = [jax.ShapeDtypeStruct((2 * QUERY_HEADS * rows, HEAD_SIZE), jnp.float32)] * 2
    all_rows = sum(p.shape[0] for p in pieces) + sum(p.shape[0] for p in own_pieces)
    flops = 2 * 2 * QUERY_HEADS * rows * all_rows * PAIR * 2
    return pl.pallas_call(
        functools.partial(
            attend_kernel, slots, OWN_ORDER, len(own_pieces), tp_size, first_call, last_call
        ),
        out_shape=out_shape,
        in_specs=in_specs,
        out_specs=[vmem] * len(out_shape),
        scratch_shapes=[
            pltpu.VMEM((all_rows, tq.shape[1] // GROUP * 2), jnp.bfloat16),
            pltpu.SemaphoreType.DMA((len(pieces) + len(own_pieces),)),
        ],
        compiler_params=pltpu.CompilerParams(vmem_limit_bytes=32 * 1024 * 1024),
        cost_estimate=pl.CostEstimate(
            flops=flops, bytes_accessed=all_rows * 4096, transcendentals=2 * QUERY_HEADS * rows * all_rows
        ),
    )(*operands)


def swap(array, axis, bit, size):
    return lax.ppermute(array, axis, [(i, i ^ bit) for i in range(size)])


def after(array, *others):
    return lax.optimization_barrier((array, *others))[0]


def local(ctx_size, tp_size, trace_q, trace_key_value, suffix_q, suffix_key_value, prefix_len, del_start, del_end):
    rows = trace_q.shape[0]
    spans = (prefix_len, del_start, del_end)
    sq = suffix_q[0]
    suffix_own = suffix_key_value[0]

    core = lambda a: swap(a, "tp", 1, tp_size)
    across_y = lambda a: swap(a, "tp", 2, tp_size)
    across_x = lambda a: swap(a, "ctx", 1, ctx_size)
    along_z = lambda a, shift: lax.ppermute(
        a, "ctx", [(i, (i + 2 * shift) % ctx_size) for i in range(ctx_size)]
    )

    def slot(shift, x, y, c=0):
        return lambda ctx, tp: (((ctx + ctx_size - 2 * shift) % ctx_size) ^ x) * tp_size + (tp ^ (2 * y + c))

    def absorb(pieces, slots, state, last_call):
        return attend(spans, trace_q, sq, suffix_pieces, pieces, slots, tp_size, state, last_call)

    def with_core(names):
        return [slot(*n) for n in names] + [slot(*n, 1) for n in names]

    if ctx_size == 8 and tp_size == 4:
        own = trace_key_value
        up, down = along_z(own, 1), along_z(own, 3)
        own_x, own_y = across_x(own), across_y(own)
        own_d = across_x(own_y)
        suffix_near = jnp.concatenate([suffix_own, across_y(suffix_own)], axis=0)
        suffix_pieces = [suffix_near, core(suffix_near)]
        plane = jnp.concatenate([own, own_x, own_y, own_d], axis=0)
        first = ([plane, core(plane)], with_core([(0, 0, 0), (0, 1, 0), (0, 0, 1), (0, 1, 1)]))

        far = along_z(after(own, up, down), 2)
        near = jnp.concatenate([up, down], axis=0)
        near_x, near_y = across_x(near), across_y(near)
        state = absorb(*first, None, False)
        near_x, near_y, state = lax.optimization_barrier((near_x, near_y, state))
        up_d, down_d = across_x(near_y[:rows]), across_y(near_x[rows:])
        far_x, far_y = across_x(far), across_y(far)
        planes = jnp.concatenate([near, near_x, near_y, up_d, down_d], axis=0)
        second = (
            [planes, core(planes)],
            with_core([(1, 0, 0), (3, 0, 0), (1, 1, 0), (3, 1, 0), (1, 0, 1), (3, 0, 1), (1, 1, 1), (3, 1, 1)]),
        )
        far_d = across_y(far_x)
        sides = jnp.concatenate([far, far_x, far_y], axis=0)
        sides_core = core(sides)
        state = absorb(*second, state, False)
        far_d, sides_core, state = lax.optimization_barrier((far_d, sides_core, state))
        third = (
            [sides, sides_core, far_d, core(far_d)],
            with_core([(2, 0, 0), (2, 1, 0), (2, 0, 1)]) + with_core([(2, 1, 1)]),
        )
        trace_out, suffix_out = absorb(*third, state, True)
    else:
        gathered = lax.all_gather(trace_key_value, ("ctx", "tp"), axis=0, tiled=True)
        own_parts = lax.all_gather(suffix_own, "tp", axis=0, tiled=False)
        tp = lax.axis_index("tp")
        suffix_pieces = [own_parts[tp ^ flip] for flip in OWN_ORDER]
        groups = [
            (
                [gathered[at:at + CHUNK_ROWS]],
                [lambda ctx, tp, number=number: number for number in range(at // rows, (at + CHUNK_ROWS) // rows)],
            )
            for at in range(0, gathered.shape[0], CHUNK_ROWS)
        ]

        state = None
        for index, (pieces, slots) in enumerate(groups):
            state = absorb(pieces, slots, state, index == len(groups) - 1)
        trace_out, suffix_out = state
    return trace_out, suffix_out[None]


def solution(mesh):
    return jax.shard_map(
        functools.partial(local, mesh.shape["ctx"], mesh.shape["tp"]),
        mesh=mesh,
        in_specs=(
            P(("ctx", "tp"), None),
            P(("ctx", "tp"), None),
            P("ctx", "tp", None),
            P("ctx", "tp", None),
            P("ctx"),
            P("ctx"),
            P("ctx"),
        ),
        out_specs=(P(("ctx", "tp"), None), P("ctx", "tp", None)),
        check_vma=False,
    )
```

```python
import functools

import jax
import jax.numpy as jnp
from jax import lax
from jax.experimental import pallas as pl
from jax.experimental.pallas import tpu as pltpu
from jax.sharding import PartitionSpec as P

QUERY_HEADS = 40
KEY_VALUE_HEADS = 8
HEAD_SIZE = 128
GROUP = QUERY_HEADS // KEY_VALUE_HEADS
PAIR = 2 * HEAD_SIZE
LOG2E = 1.4426950408889634
SCALE = HEAD_SIZE ** (-0.5) * LOG2E
MASKED = -1e30
CHUNK_ROWS = 1024
OWN_ORDER = (0, 2, 1, 3)


def dot_t(a, b):
    return lax.dot_general(a, b, (((1,), (1,)), ((), ())), preferred_element_type=jnp.float32)


def dot(a, b):
    return lax.dot_general(a, b, (((1,), (0,)), ((), ())), preferred_element_type=jnp.float32)


def attend_kernel(slots, own_order, own_count, tp_size, first_call, last_call, *refs):
    refs = list(refs)
    prefix_ref, del_start_ref, del_end_ref, tq, sq = refs[:5]
    del refs[:5]
    k_aug_ref, refs = refs[-1], refs[:-1]
    out_a, out_b = refs[-2:]
    del refs[-2:]
    if not first_call:
        stats_in, sum_in = refs[-2:]
        del refs[-2:]
    own_pieces, pieces = refs[:own_count], refs[own_count:]

    rows = tq.shape[0]
    ctx = lax.axis_index("ctx").astype(jnp.int32)
    tp = lax.axis_index("tp").astype(jnp.int32)
    first_position = (ctx * tp_size + tp) * rows
    prefix, del_start, del_end = prefix_ref[0], del_start_ref[0], del_end_ref[0]
    lanes = HEAD_SIZE
    lane = lax.broadcasted_iota(jnp.int32, (rows, lanes), 1)
    row = lax.broadcasted_iota(jnp.int32, (rows, lanes), 0)
    q_trace_aug = jnp.where(lane == row, 1.0, 0.0).astype(jnp.bfloat16)
    q_suffix_aug = jnp.where((lane == rows) | (lane == rows + 1 + row), 1.0, 0.0).astype(jnp.bfloat16)
    q_aug = jnp.concatenate([q_trace_aug] * GROUP + [q_suffix_aug] * GROUP, axis=0)
    for index, slot in enumerate(slots):
        position = slot(ctx, tp) * rows + row
        hidden_trace = (lane < rows) & (position > first_position + lane)
        hidden_suffix = (lane == rows) & (
            (position >= prefix) | ((position >= del_start) & (position < del_end))
        )
        bias = jnp.where(hidden_trace | hidden_suffix, MASKED, 0.0).astype(jnp.bfloat16)
        k_aug_ref[index * rows:(index + 1) * rows, :] = bias
    total = rows * len(slots)
    if first_call:
        for index, flip in enumerate(own_order):
            position = (tp ^ flip) * rows + row
            hidden = (lane > rows) & (position > tp * rows + (lane - rows - 1))
            bias = jnp.where(hidden, MASKED, 0.0).astype(jnp.bfloat16)
            k_aug_ref[total + index * rows:total + (index + 1) * rows, :] = bias
        own_total = rows * len(own_order)
        own_ones = jnp.ones((own_total, HEAD_SIZE), jnp.bfloat16)
    ones = jnp.ones((total, HEAD_SIZE), jnp.bfloat16)
    half = GROUP * rows
    lane_out = lax.broadcasted_iota(jnp.int32, (2 * half, HEAD_SIZE), 1)

    def one_head(g, _):
        def columns(index):
            return pl.ds(pl.multiple_of(index * HEAD_SIZE, HEAD_SIZE), HEAD_SIZE)

        def stacked(parts, index):
            return jnp.concatenate([part[:, columns(index)] for part in parts], axis=0)

        query = jnp.concatenate(
            [ref[:, columns(g * GROUP + j)] for ref in (tq, sq) for j in range(GROUP)], axis=0
        )
        query = jnp.concatenate([query, q_aug], axis=1)
        scores = dot_t(query, jnp.concatenate([stacked(pieces, 2 * g), k_aug_ref[0:total]], axis=1))
        top = jnp.max(scores, axis=1, keepdims=True)
        if first_call:
            own_key = jnp.concatenate(
                [stacked(own_pieces, 2 * g), k_aug_ref[total:total + own_total]], axis=1
            )
            own_scores = dot_t(query[half:], own_key)
            own_top = jnp.maximum(top[half:], jnp.max(own_scores, axis=1, keepdims=True))
            top = jnp.concatenate([top[:half], own_top], axis=0)
        else:
            old_top = stats_in[g, :, 0:1]
            top = jnp.maximum(old_top, top)
        weights = jnp.exp2((scores - top) * SCALE).astype(jnp.bfloat16)
        both = dot(weights, jnp.concatenate([stacked(pieces, 2 * g + 1), ones], axis=1))
        summed, denominator = both[:, :HEAD_SIZE], both[:, HEAD_SIZE:]
        if first_call:
            own_weights = jnp.exp2((own_scores - top[half:]) * SCALE).astype(jnp.bfloat16)
            own_both = dot(own_weights, jnp.concatenate([stacked(own_pieces, 2 * g + 1), own_ones], axis=1))
            summed = jnp.concatenate([summed[:half], summed[half:] + own_both[:, :HEAD_SIZE]], axis=0)
            denominator = jnp.concatenate(
                [denominator[:half], denominator[half:] + own_both[:, HEAD_SIZE:]], axis=0
            )
        else:
            rescale = jnp.exp2((old_top - top) * SCALE)
            summed = summed + sum_in[g] * rescale
            denominator = denominator + stats_in[g, :, 1:2] * rescale
        if last_call:
            inverse = pl.reciprocal(denominator, approx=True)
            inverse = inverse * (2.0 - denominator * inverse)
            result = (summed * inverse).astype(jnp.bfloat16)
            for j in range(GROUP):
                out_a[:, columns(g * GROUP + j)] = result[j * rows:(j + 1) * rows]
                out_b[:, columns(g * GROUP + j)] = result[half + j * rows:half + (j + 1) * rows]
        else:
            out_a[g] = jnp.where(lane_out == 0, top, denominator)
            out_b[g] = summed
        return 0

    lax.fori_loop(0, KEY_VALUE_HEADS, one_head, 0)


def attend(spans, tq, sq, own_pieces, pieces, slots, tp_size, carry, last_call):
    first_call = carry is None
    rows = tq.shape[0]
    own_pieces = list(own_pieces) if first_call else []
    smem = pl.BlockSpec(memory_space=pltpu.SMEM)
    vmem = pl.BlockSpec(memory_space=pltpu.VMEM)
    operands = [*spans, tq, sq, *own_pieces, *pieces]
    if not first_call:
        operands += list(carry)
    if last_call:
        out_shape = [jax.ShapeDtypeStruct(tq.shape, jnp.bfloat16)] * 2
    else:
        state = (KEY_VALUE_HEADS, 2 * GROUP * rows, HEAD_SIZE)
        out_shape = [jax.ShapeDtypeStruct(state, jnp.float32)] * 2
    all_rows = sum(p.shape[0] for p in pieces) + sum(p.shape[0] for p in own_pieces)
    flops = 2 * 2 * QUERY_HEADS * rows * all_rows * PAIR * 2
    return pl.pallas_call(
        functools.partial(
            attend_kernel, slots, OWN_ORDER, len(own_pieces), tp_size, first_call, last_call
        ),
        out_shape=out_shape,
        in_specs=[smem] * 3 + [vmem] * (len(operands) - 3),
        out_specs=[vmem] * len(out_shape),
        scratch_shapes=[pltpu.VMEM((all_rows, HEAD_SIZE), jnp.bfloat16)],
        compiler_params=pltpu.CompilerParams(vmem_limit_bytes=32 * 1024 * 1024),
        cost_estimate=pl.CostEstimate(
            flops=flops, bytes_accessed=all_rows * 4096, transcendentals=2 * QUERY_HEADS * rows * all_rows
        ),
    )(*operands)


def swap(array, axis, bit, size):
    return lax.ppermute(array, axis, [(i, i ^ bit) for i in range(size)])


def after(array, *others):
    return lax.optimization_barrier((array, *others))[0]


def local(ctx_size, tp_size, trace_q, trace_key_value, suffix_q, suffix_key_value, prefix_len, del_start, del_end):
    rows = trace_q.shape[0]
    spans = (prefix_len, del_start, del_end)
    sq = suffix_q[0]
    suffix_own = suffix_key_value[0]

    core = lambda a: swap(a, "tp", 1, tp_size)
    across_y = lambda a: swap(a, "tp", 2, tp_size)
    across_x = lambda a: swap(a, "ctx", 1, ctx_size)
    along_z = lambda a, shift: lax.ppermute(
        a, "ctx", [(i, (i + 2 * shift) % ctx_size) for i in range(ctx_size)]
    )

    across_both = lambda a: lax.ppermute(
        a,
        ("ctx", "tp"),
        [(i * tp_size + j, (i ^ 1) * tp_size + (j ^ 2)) for i in range(ctx_size) for j in range(tp_size)],
    )

    def slot(shift, x, y, c=0):
        return lambda ctx, tp: (((ctx + ctx_size - 2 * shift) % ctx_size) ^ x) * tp_size + (tp ^ (2 * y + c))

    def absorb(pieces, slots, state, last_call):
        return attend(spans, trace_q, sq, suffix_pieces, pieces, slots, tp_size, state, last_call)

    def with_core(names):
        return [slot(*n) for n in names] + [slot(*n, 1) for n in names]

    if ctx_size == 8 and tp_size == 4:
        own = trace_key_value
        up, down = along_z(own, 1), along_z(own, 3)
        own_x, own_y = across_x(own), across_y(own)
        far = along_z(own, 2)
        own_d = across_x(own_y)
        suffix_y = across_y(after(suffix_own, own_y))
        plane = jnp.concatenate([own, own_x, own_y, own_d, suffix_own, suffix_y], axis=0)
        plane_core = core(plane)
        here = 4 * rows
        suffix_pieces = [plane[here:], plane_core[here:]]
        first = [plane[:here], plane_core[:here]]
        first_slots = with_core([(0, 0, 0), (0, 1, 0), (0, 0, 1), (0, 1, 1)])

        near = jnp.concatenate([up, down], axis=0)
        near_x, near_y, near_d = across_x(near), across_y(near), across_both(near)
        state = absorb(first, first_slots, None, False)
        far_x, far_y, far_d = across_x(far), across_y(far), across_both(far)
        near_x, near_y, near_d, state = lax.optimization_barrier((near_x, near_y, near_d, state))
        planes = jnp.concatenate([near, near_x, near_y, near_d, far], axis=0)
        second = [planes, core(planes)]
        second_slots = with_core(
            [(z, x, y) for x, y in ((0, 0), (1, 0), (0, 1), (1, 1)) for z in (1, 3)] + [(2, 0, 0)]
        )
        state = absorb(second, second_slots, state, False)
        far_rest = jnp.concatenate([far_x, far_y, far_d], axis=0)
        third = [far_rest, core(far_rest)]
        third_slots = with_core([(2, 1, 0), (2, 0, 1), (2, 1, 1)])
        trace_out, suffix_out = absorb(third, third_slots, state, True)
    else:
        gathered = lax.all_gather(trace_key_value, ("ctx", "tp"), axis=0, tiled=True)
        own_parts = lax.all_gather(suffix_own, "tp", axis=0, tiled=False)
        tp = lax.axis_index("tp")
        suffix_pieces = [own_parts[tp ^ flip] for flip in OWN_ORDER]
        groups = [
            (
                [gathered[at:at + CHUNK_ROWS]],
                [lambda ctx, tp, number=number: number for number in range(at // rows, (at + CHUNK_ROWS) // rows)],
            )
            for at in range(0, gathered.shape[0], CHUNK_ROWS)
        ]

        state = None
        for index, (pieces, slots) in enumerate(groups):
            state = absorb(pieces, slots, state, index == len(groups) - 1)
        trace_out, suffix_out = state
    return trace_out, suffix_out[None]


def solution(mesh):
    return jax.shard_map(
        functools.partial(local, mesh.shape["ctx"], mesh.shape["tp"]),
        mesh=mesh,
        in_specs=(
            P(("ctx", "tp"), None),
            P(("ctx", "tp"), None),
            P("ctx", "tp", None),
            P("ctx", "tp", None),
            P("ctx"),
            P("ctx"),
            P("ctx"),
        ),
        out_specs=(P(("ctx", "tp"), None), P("ctx", "tp", None)),
        check_vma=False,
    )
```

```python
import functools

import jax
import jax.numpy as jnp
from jax import lax
from jax.experimental import pallas as pl
from jax.experimental.pallas import tpu as pltpu
from jax.sharding import PartitionSpec as P

QUERY_HEADS = 40
KEY_VALUE_HEADS = 8
HEAD_SIZE = 128
GROUP = QUERY_HEADS // KEY_VALUE_HEADS
PAIR = 2 * HEAD_SIZE
LOG2E = 1.4426950408889634
SCALE = HEAD_SIZE ** (-0.5) * LOG2E
MASKED = -1e30
CHUNK_ROWS = 1024
OWN_ORDER = (0, 2, 1, 3)


def dot_t(a, b):
    return lax.dot_general(a, b, (((1,), (1,)), ((), ())), preferred_element_type=jnp.float32)


def dot(a, b):
    return lax.dot_general(a, b, (((1,), (0,)), ((), ())), preferred_element_type=jnp.float32)


def attend_kernel(slots, own_order, own_count, tp_size, first_call, last_call, *refs):
    refs = list(refs)
    prefix_ref, del_start_ref, del_end_ref, tq, sq = refs[:5]
    del refs[:5]
    k_aug_ref, refs = refs[-1], refs[:-1]
    out_a, out_b = refs[-2:]
    del refs[-2:]
    if not first_call:
        stats_in, sum_in = refs[-2:]
        del refs[-2:]
    own_pieces, pieces = refs[:own_count], refs[own_count:]

    rows = tq.shape[0]
    ctx = lax.axis_index("ctx").astype(jnp.int32)
    tp = lax.axis_index("tp").astype(jnp.int32)
    first_position = (ctx * tp_size + tp) * rows
    prefix, del_start, del_end = prefix_ref[0], del_start_ref[0], del_end_ref[0]
    lanes = HEAD_SIZE
    lane = lax.broadcasted_iota(jnp.int32, (rows, lanes), 1)
    row = lax.broadcasted_iota(jnp.int32, (rows, lanes), 0)
    q_trace_aug = jnp.where(lane == row, 1.0, 0.0).astype(jnp.bfloat16)
    q_suffix_aug = jnp.where((lane == rows) | (lane == rows + 1 + row), 1.0, 0.0).astype(jnp.bfloat16)
    q_aug = jnp.concatenate([q_trace_aug] * GROUP + [q_suffix_aug] * GROUP, axis=0)
    for index, slot in enumerate(slots):
        position = slot(ctx, tp) * rows + row
        hidden_trace = (lane < rows) & (position > first_position + lane)
        hidden_suffix = (lane == rows) & (
            (position >= prefix) | ((position >= del_start) & (position < del_end))
        )
        bias = jnp.where(hidden_trace | hidden_suffix, MASKED, 0.0).astype(jnp.bfloat16)
        k_aug_ref[index * rows:(index + 1) * rows, :] = bias
    total = rows * len(slots)
    if own_count:
        for index, flip in enumerate(own_order):
            position = (tp ^ flip) * rows + row
            hidden = (lane > rows) & (position > tp * rows + (lane - rows - 1))
            bias = jnp.where(hidden, MASKED, 0.0).astype(jnp.bfloat16)
            k_aug_ref[total + index * rows:total + (index + 1) * rows, :] = bias
        own_total = rows * len(own_order)
        own_ones = jnp.ones((own_total, HEAD_SIZE), jnp.bfloat16)
    ones = jnp.ones((total, HEAD_SIZE), jnp.bfloat16)
    half = GROUP * rows
    lane_out = lax.broadcasted_iota(jnp.int32, (2 * half, HEAD_SIZE), 1)

    def columns(index):
        return slice(index * HEAD_SIZE, (index + 1) * HEAD_SIZE)

    def stacked(parts, index):
        return jnp.concatenate([part[:, columns(index)] for part in parts], axis=0)

    def scores_of(g):
        query = jnp.concatenate(
            [ref[:, columns(g * GROUP + j)] for ref in (tq, sq) for j in range(GROUP)], axis=0
        )
        query = jnp.concatenate([query, q_aug], axis=1)
        scores = dot_t(query, jnp.concatenate([stacked(pieces, 2 * g), k_aug_ref[0:total]], axis=1))
        if not own_count:
            return scores, None
        own_key = jnp.concatenate([stacked(own_pieces, 2 * g), k_aug_ref[total:total + own_total]], axis=1)
        return scores, dot_t(query[half:], own_key)

    def absorb_head(g, scores, own_scores):
        top = jnp.max(scores, axis=1, keepdims=True)
        if own_count:
            own_top = jnp.maximum(top[half:], jnp.max(own_scores, axis=1, keepdims=True))
            top = jnp.concatenate([top[:half], own_top], axis=0)
        if not first_call:
            old_top = stats_in[g, :, 0:1]
            top = jnp.maximum(old_top, top)
        weights = jnp.exp2((scores - top) * SCALE).astype(jnp.bfloat16)
        both = dot(weights, jnp.concatenate([stacked(pieces, 2 * g + 1), ones], axis=1))
        summed, denominator = both[:, :HEAD_SIZE], both[:, HEAD_SIZE:]
        if own_count:
            own_weights = jnp.exp2((own_scores - top[half:]) * SCALE).astype(jnp.bfloat16)
            own_both = dot(own_weights, jnp.concatenate([stacked(own_pieces, 2 * g + 1), own_ones], axis=1))
            summed = jnp.concatenate([summed[:half], summed[half:] + own_both[:, :HEAD_SIZE]], axis=0)
            denominator = jnp.concatenate(
                [denominator[:half], denominator[half:] + own_both[:, HEAD_SIZE:]], axis=0
            )
        if not first_call:
            rescale = jnp.exp2((old_top - top) * SCALE)
            summed = summed + sum_in[g] * rescale
            denominator = denominator + stats_in[g, :, 1:2] * rescale
        if last_call:
            inverse = pl.reciprocal(denominator, approx=True)
            inverse = inverse * (2.0 - denominator * inverse)
            result = (summed * inverse).astype(jnp.bfloat16)
            for j in range(GROUP):
                out_a[:, columns(g * GROUP + j)] = result[j * rows:(j + 1) * rows]
                out_b[:, columns(g * GROUP + j)] = result[half + j * rows:half + (j + 1) * rows]
        else:
            out_a[g] = jnp.where(lane_out == 0, top, denominator)
            out_b[g] = summed

    ahead = scores_of(0)
    for g in range(KEY_VALUE_HEADS):
        now, ahead = ahead, scores_of(g + 1) if g + 1 < KEY_VALUE_HEADS else None
        absorb_head(g, *now)


def attend(spans, tq, sq, own_pieces, pieces, slots, tp_size, carry, last_call):
    first_call = carry is None
    rows = tq.shape[0]
    smem = pl.BlockSpec(memory_space=pltpu.SMEM)
    vmem = pl.BlockSpec(memory_space=pltpu.VMEM)
    operands = [*spans, tq, sq, *own_pieces, *pieces]
    if not first_call:
        operands += list(carry)
    if last_call:
        out_shape = [jax.ShapeDtypeStruct(tq.shape, jnp.bfloat16)] * 2
    else:
        state = (KEY_VALUE_HEADS, 2 * GROUP * rows, HEAD_SIZE)
        out_shape = [jax.ShapeDtypeStruct(state, jnp.float32)] * 2
    all_rows = sum(p.shape[0] for p in pieces) + sum(p.shape[0] for p in own_pieces)
    flops = 2 * 2 * QUERY_HEADS * rows * all_rows * PAIR * 2
    return pl.pallas_call(
        functools.partial(
            attend_kernel, slots, OWN_ORDER, len(own_pieces), tp_size, first_call, last_call
        ),
        out_shape=out_shape,
        in_specs=[smem] * 3 + [vmem] * (len(operands) - 3),
        out_specs=[vmem] * len(out_shape),
        scratch_shapes=[pltpu.VMEM((all_rows, HEAD_SIZE), jnp.bfloat16)],
        compiler_params=pltpu.CompilerParams(vmem_limit_bytes=32 * 1024 * 1024),
        cost_estimate=pl.CostEstimate(
            flops=flops, bytes_accessed=all_rows * 4096, transcendentals=2 * QUERY_HEADS * rows * all_rows
        ),
    )(*operands)


def swap(array, axis, bit, size):
    return lax.ppermute(array, axis, [(i, i ^ bit) for i in range(size)])


def after(array, *others):
    return lax.optimization_barrier((array, *others))[0]


def local(ctx_size, tp_size, trace_q, trace_key_value, suffix_q, suffix_key_value, prefix_len, del_start, del_end):
    rows = trace_q.shape[0]
    spans = (prefix_len, del_start, del_end)
    sq = suffix_q[0]
    suffix_own = suffix_key_value[0]

    core = lambda a: swap(a, "tp", 1, tp_size)
    across_y = lambda a: swap(a, "tp", 2, tp_size)
    across_x = lambda a: swap(a, "ctx", 1, ctx_size)
    along_z = lambda a, shift: lax.ppermute(
        a, "ctx", [(i, (i + 2 * shift) % ctx_size) for i in range(ctx_size)]
    )

    across_both = lambda a: lax.ppermute(
        a,
        ("ctx", "tp"),
        [(i * tp_size + j, (i ^ 1) * tp_size + (j ^ 2)) for i in range(ctx_size) for j in range(tp_size)],
    )

    def slot(shift, x, y, c=0):
        return lambda ctx, tp: (((ctx + ctx_size - 2 * shift) % ctx_size) ^ x) * tp_size + (tp ^ (2 * y + c))

    def absorb(pieces, slots, state, last_call, suffix_pieces=()):
        return attend(spans, trace_q, sq, suffix_pieces, pieces, slots, tp_size, state, last_call)

    def with_core(names):
        return [slot(*n) for n in names] + [slot(*n, 1) for n in names]

    if ctx_size == 8 and tp_size == 4:
        up, down = along_z(trace_key_value, 1), along_z(trace_key_value, 3)
        own_x, own_y = across_x(trace_key_value), across_y(trace_key_value)
        own_d = across_both(trace_key_value)
        own, suffix_own, own_x, own_y = lax.optimization_barrier((trace_key_value, suffix_own, own_x, own_y))
        suffix_y = across_y(suffix_own)
        plane = jnp.concatenate([own, own_x, own_y, own_d], axis=0)
        first = [plane, core(plane)]
        first_slots = with_core([(0, 0, 0), (0, 1, 0), (0, 0, 1), (0, 1, 1)])

        far = along_z(up, 1)
        near = jnp.concatenate([up, down], axis=0)
        near_x, near_y = across_x(near), across_y(near)
        far_x, far_y = across_x(far), across_y(far)
        rest_d = across_both(jnp.concatenate([near, far], axis=0))
        far, first[0] = lax.optimization_barrier((far, first[0]))
        state = absorb(first, first_slots, None, False)
        near_x, near_y, suffix_y, state = lax.optimization_barrier((near_x, near_y, suffix_y, state))
        planes = jnp.concatenate([near, near_x, near_y, far, suffix_own, suffix_y], axis=0)
        planes_core = core(planes)
        here = 7 * rows
        second = [planes[:here], planes_core[:here]]
        second_slots = with_core([(z, x, y) for x, y in ((0, 0), (1, 0), (0, 1)) for z in (1, 3)] + [(2, 0, 0)])
        state = absorb(second, second_slots, state, False, [planes[here:], planes_core[here:]])
        rest = jnp.concatenate([far_x, far_y, rest_d], axis=0)
        third = [rest, core(rest)]
        third_slots = with_core([(2, 1, 0), (2, 0, 1), (1, 1, 1), (3, 1, 1), (2, 1, 1)])
        trace_out, suffix_out = absorb(third, third_slots, state, True)
    else:
        gathered = lax.all_gather(trace_key_value, ("ctx", "tp"), axis=0, tiled=True)
        own_parts = lax.all_gather(suffix_own, "tp", axis=0, tiled=False)
        tp = lax.axis_index("tp")
        suffix_pieces = [own_parts[tp ^ flip] for flip in OWN_ORDER]
        groups = [
            (
                [gathered[at:at + CHUNK_ROWS]],
                [lambda ctx, tp, number=number: number for number in range(at // rows, (at + CHUNK_ROWS) // rows)],
            )
            for at in range(0, gathered.shape[0], CHUNK_ROWS)
        ]

        state = None
        for index, (pieces, slots) in enumerate(groups):
            own_here = suffix_pieces if index == 0 else ()
            state = absorb(pieces, slots, state, index == len(groups) - 1, own_here)
        trace_out, suffix_out = state
    return trace_out, suffix_out[None]


def solution(mesh):
    return jax.shard_map(
        functools.partial(local, mesh.shape["ctx"], mesh.shape["tp"]),
        mesh=mesh,
        in_specs=(
            P(("ctx", "tp"), None),
            P(("ctx", "tp"), None),
            P("ctx", "tp", None),
            P("ctx", "tp", None),
            P("ctx"),
            P("ctx"),
            P("ctx"),
        ),
        out_specs=(P(("ctx", "tp"), None), P("ctx", "tp", None)),
        check_vma=False,
    )
```

```python
import functools

import jax
import jax.numpy as jnp
from jax import lax
from jax.experimental import pallas as pl
from jax.experimental.pallas import tpu as pltpu
from jax.sharding import PartitionSpec as P

QUERY_HEADS = 40
KEY_VALUE_HEADS = 8
HEAD_SIZE = 128
GROUP = QUERY_HEADS // KEY_VALUE_HEADS
PAIR = 2 * HEAD_SIZE
LOG2E = 1.4426950408889634
SCALE = HEAD_SIZE ** (-0.5) * LOG2E
MASKED = -1e30
CHUNK_ROWS = 1024


def dot_t(a, b):
    return lax.dot_general(a, b, (((1,), (1,)), ((), ())), preferred_element_type=jnp.float32)


def dot(a, b):
    return lax.dot_general(a, b, (((1,), (0,)), ((), ())), preferred_element_type=jnp.float32)


def attend_kernel(slots, tp_size, first_call, last_call, *refs):
    refs = list(refs)
    prefix_ref, del_start_ref, del_end_ref, tq, sq = refs[:5]
    del refs[:5]
    k_aug_ref = refs.pop()
    outs, refs = (refs[-2:], refs[:-2]) if last_call else (refs[-3:], refs[:-3])
    if not first_call:
        top_in, denominator_in, sum_in = refs[-3:]
        del refs[-3:]
    pieces = refs

    rows = tq.shape[0]
    half = GROUP * rows
    ctx = lax.axis_index("ctx").astype(jnp.int32)
    tp = lax.axis_index("tp").astype(jnp.int32)
    first_position = (ctx * tp_size + tp) * rows
    prefix, del_start, del_end = prefix_ref[0], del_start_ref[0], del_end_ref[0]
    lane = lax.broadcasted_iota(jnp.int32, (rows, HEAD_SIZE), 1)
    row = lax.broadcasted_iota(jnp.int32, (rows, HEAD_SIZE), 0)
    q_trace_aug = jnp.where(lane == row, 1.0, 0.0).astype(jnp.bfloat16)
    q_suffix_aug = jnp.where((lane == rows) | (lane == rows + 1 + row), 1.0, 0.0).astype(jnp.bfloat16)
    q_aug = jnp.concatenate([q_trace_aug] * GROUP + [q_suffix_aug] * GROUP, axis=0)
    for index, slot in enumerate(slots):
        kind, block = slot(ctx, tp)
        position = block * rows + row
        if kind == "trace":
            hidden_trace = (lane < rows) & (position > first_position + lane)
            hidden_suffix = (lane == rows) & (
                (position >= prefix) | ((position >= del_start) & (position < del_end))
            )
            hidden = hidden_trace | hidden_suffix
        else:
            hidden = (lane < rows) | ((lane > rows) & (position > tp * rows + (lane - rows - 1)))
        k_aug_ref[index * rows:(index + 1) * rows, :] = jnp.where(hidden, MASKED, 0.0).astype(jnp.bfloat16)
    total = rows * len(slots)
    ones = jnp.ones((total, HEAD_SIZE), jnp.bfloat16)

    def columns(index):
        return slice(index * HEAD_SIZE, (index + 1) * HEAD_SIZE)

    def stacked(index):
        return jnp.concatenate([piece[:, columns(index)] for piece in pieces], axis=0)

    def scores_of(g):
        query = jnp.concatenate(
            [ref[:, columns(g * GROUP + j)] for ref in (tq, sq) for j in range(GROUP)], axis=0
        )
        query = jnp.concatenate([query, q_aug], axis=1)
        return dot_t(query, jnp.concatenate([stacked(2 * g), k_aug_ref[...]], axis=1))

    def absorb_head(g, scores):
        top = jnp.broadcast_to(jnp.max(scores, axis=1, keepdims=True), (2 * half, HEAD_SIZE))
        if not first_call:
            old_top = top_in[g]
            top = jnp.maximum(old_top, top)
        shifted = scores - jnp.concatenate([top] * (total // HEAD_SIZE), axis=1)
        weights = jnp.exp2(shifted * SCALE).astype(jnp.bfloat16)
        both = dot(weights, jnp.concatenate([stacked(2 * g + 1), ones], axis=1))
        summed, denominator = both[:, :HEAD_SIZE], both[:, HEAD_SIZE:]
        if not first_call:
            rescale = jnp.exp2((old_top - top) * SCALE)
            summed = summed + sum_in[g] * rescale
            denominator = denominator + denominator_in[g] * rescale
        if last_call:
            inverse = pl.reciprocal(denominator, approx=True)
            inverse = inverse * (2.0 - denominator * inverse)
            result = (summed * inverse).astype(jnp.bfloat16)
            for j in range(GROUP):
                outs[0][:, columns(g * GROUP + j)] = result[j * rows:(j + 1) * rows]
                outs[1][:, columns(g * GROUP + j)] = result[half + j * rows:half + (j + 1) * rows]
        else:
            for out, state in zip(outs, (top, denominator, summed)):
                out[g] = state

    ahead = scores_of(0)
    for g in range(KEY_VALUE_HEADS):
        now, ahead = ahead, scores_of(g + 1) if g + 1 < KEY_VALUE_HEADS else None
        absorb_head(g, now)


def attend(spans, tq, sq, pieces, slots, tp_size, carry, last_call):
    first_call = carry is None
    rows = tq.shape[0]
    smem = pl.BlockSpec(memory_space=pltpu.SMEM)
    vmem = pl.BlockSpec(memory_space=pltpu.VMEM)
    operands = [*spans, tq, sq, *pieces]
    if not first_call:
        operands += list(carry)
    if last_call:
        out_shape = [jax.ShapeDtypeStruct(tq.shape, jnp.bfloat16)] * 2
    else:
        state = (KEY_VALUE_HEADS, 2 * GROUP * rows, HEAD_SIZE)
        out_shape = [jax.ShapeDtypeStruct(state, jnp.float32)] * 3
    all_rows = sum(p.shape[0] for p in pieces)
    flops = 2 * 2 * QUERY_HEADS * rows * all_rows * PAIR * 2
    return pl.pallas_call(
        functools.partial(attend_kernel, slots, tp_size, first_call, last_call),
        out_shape=out_shape,
        in_specs=[smem] * 3 + [vmem] * (len(operands) - 3),
        out_specs=[vmem] * len(out_shape),
        scratch_shapes=[pltpu.VMEM((all_rows, HEAD_SIZE), jnp.bfloat16)],
        compiler_params=pltpu.CompilerParams(vmem_limit_bytes=32 * 1024 * 1024),
        cost_estimate=pl.CostEstimate(
            flops=flops, bytes_accessed=all_rows * 4096, transcendentals=2 * QUERY_HEADS * rows * all_rows
        ),
    )(*operands)


def swap(array, axis, bit, size):
    return lax.ppermute(array, axis, [(i, i ^ bit) for i in range(size)])


def after(array, *others):
    return lax.optimization_barrier((array, *others))[0]


def local(ctx_size, tp_size, trace_q, trace_key_value, suffix_q, suffix_key_value, prefix_len, del_start, del_end):
    rows = trace_q.shape[0]
    spans = (prefix_len, del_start, del_end)
    sq = suffix_q[0]
    suffix_own = suffix_key_value[0]

    core = lambda a: swap(a, "tp", 1, tp_size)
    across_y = lambda a: swap(a, "tp", 2, tp_size)
    across_x = lambda a: swap(a, "ctx", 1, ctx_size)
    along_z = lambda a, shift: lax.ppermute(
        a, "ctx", [(i, (i + 2 * shift) % ctx_size) for i in range(ctx_size)]
    )

    across_both = lambda a: lax.ppermute(
        a,
        ("ctx", "tp"),
        [(i * tp_size + j, (i ^ 1) * tp_size + (j ^ 2)) for i in range(ctx_size) for j in range(tp_size)],
    )

    def slot(place, c):
        if isinstance(place, int):
            return lambda ctx, tp: ("suffix", tp ^ place ^ c)
        shift, x, y = place
        return lambda ctx, tp: (
            "trace",
            (((ctx + ctx_size - 2 * shift) % ctx_size) ^ x) * tp_size + (tp ^ (2 * y + c)),
        )

    def absorb(pieces, slots, state, last_call=False):
        return attend(spans, trace_q, sq, pieces, slots, tp_size, state, last_call)

    def absorb_both(mine, sibling, places, state, last_call=False):
        slots = [slot(place, c) for c in (0, 1) for place in places]
        return absorb(mine + sibling, slots, state, last_call)

    if ctx_size == 8 and tp_size == 4:
        barrier = lax.optimization_barrier
        up, down = along_z(trace_key_value, 1), along_z(trace_key_value, 3)
        own_x, own_d = across_x(trace_key_value), across_both(trace_key_value)
        own = jnp.concatenate([trace_key_value, suffix_own], axis=0)
        own_y = across_y(own)
        up, down, own_x, own_d = barrier((up, down, own_x, own_d))

        up_two = along_z(jnp.concatenate([up, own_d], axis=0), 1)
        down_d = along_z(own_d, 3)
        near = jnp.concatenate([up, down], axis=0)
        near_x, near_y = across_x(near), across_y(near)
        plane = jnp.concatenate([own, own_y, own_x, own_d], axis=0)
        here = [(0, 0, 0), 0, (0, 0, 1), 2, (0, 1, 0), (0, 1, 1)]
        state = absorb_both([plane], [core(plane)], here, None)

        near_x, near_y, state = barrier((near_x, near_y, state))
        sides = jnp.concatenate([near, near_x, near_y], axis=0)
        sides_core = core(sides)
        far, up_d = up_two[:rows], up_two[rows:]
        far_x, far_y, far_d = across_x(far), across_y(far), along_z(up_d, 1)
        mixed = jnp.concatenate([up_two, down_d], axis=0)
        mixed_core = core(mixed)
        here = [(z, x, y) for x, y in ((0, 0), (1, 0), (0, 1)) for z in (1, 3)]
        state = absorb_both([sides], [sides_core], here, state)

        far_x, far_y, far_d, state = barrier((far_x, far_y, far_d, state))
        rest = jnp.concatenate([far_x, far_y, far_d], axis=0)
        here = [(2, 0, 0), (1, 1, 1), (3, 1, 1), (2, 1, 0), (2, 0, 1), (2, 1, 1)]
        trace_out, suffix_out = absorb_both([mixed, rest], [mixed_core, core(rest)], here, state, True)
    else:
        gathered = lax.all_gather(trace_key_value, ("ctx", "tp"), axis=0, tiled=True)
        suffix_all = lax.all_gather(suffix_own, "tp", axis=0, tiled=True)
        state = None
        for at in range(0, gathered.shape[0], CHUNK_ROWS):
            last_call = at + CHUNK_ROWS >= gathered.shape[0]
            pieces = [gathered[at:at + CHUNK_ROWS]]
            slots = [
                lambda ctx, tp, block=block: ("trace", block)
                for block in range(at // rows, min(at + CHUNK_ROWS, gathered.shape[0]) // rows)
            ]
            if at == 0:
                pieces.append(suffix_all)
                slots += [lambda ctx, tp, block=block: ("suffix", block) for block in range(tp_size)]
            state = absorb(pieces, slots, state, last_call)
        trace_out, suffix_out = state
    return trace_out, suffix_out[None]


def solution(mesh):
    return jax.shard_map(
        functools.partial(local, mesh.shape["ctx"], mesh.shape["tp"]),
        mesh=mesh,
        in_specs=(
            P(("ctx", "tp"), None),
            P(("ctx", "tp"), None),
            P("ctx", "tp", None),
            P("ctx", "tp", None),
            P("ctx"),
            P("ctx"),
            P("ctx"),
        ),
        out_specs=(P(("ctx", "tp"), None), P("ctx", "tp", None)),
        check_vma=False,
    )
```

```python
import functools

import jax
import jax.numpy as jnp
from jax import lax
from jax.experimental import pallas as pl
from jax.experimental.pallas import tpu as pltpu
from jax.sharding import PartitionSpec as P

QUERY_HEADS = 40
KEY_VALUE_HEADS = 8
HEAD_SIZE = 128
GROUP = QUERY_HEADS // KEY_VALUE_HEADS
PAIR = 2 * HEAD_SIZE
LOG2E = 1.4426950408889634
SCALE = HEAD_SIZE ** (-0.5) * LOG2E
MASKED = -1e30
CHUNK_ROWS = 1024


def dot_t(a, b):
    return lax.dot_general(a, b, (((1,), (1,)), ((), ())), preferred_element_type=jnp.float32)


def dot(a, b):
    return lax.dot_general(a, b, (((1,), (0,)), ((), ())), preferred_element_type=jnp.float32)


def attend_kernel(slots, tp_size, first_call, last_call, *refs):
    refs = list(refs)
    spans, tq, sq = refs[:3]
    del refs[:3]
    k_aug_ref = refs.pop()
    outs, refs = (refs[-2:], refs[:-2]) if last_call else (refs[-3:], refs[:-3])
    if not first_call:
        top_in, denominator_in, sum_in = refs[-3:]
        del refs[-3:]
    pieces = refs

    rows = tq.shape[0]
    half = GROUP * rows
    ctx = lax.axis_index("ctx").astype(jnp.int32)
    tp = lax.axis_index("tp").astype(jnp.int32)
    first_position = (ctx * tp_size + tp) * rows
    prefix, del_start, del_end = spans[0:1], spans[1:2], spans[2:3]
    lane = lax.broadcasted_iota(jnp.int32, (rows, HEAD_SIZE), 1)
    row = lax.broadcasted_iota(jnp.int32, (rows, HEAD_SIZE), 0)
    q_trace_aug = jnp.where(lane == row, 1.0, 0.0).astype(jnp.bfloat16)
    q_suffix_aug = jnp.where((lane == rows) | (lane == rows + 1 + row), 1.0, 0.0).astype(jnp.bfloat16)
    q_aug = jnp.concatenate([q_trace_aug] * GROUP + [q_suffix_aug] * GROUP, axis=0)
    for index, slot in enumerate(slots):
        kind, block = slot(ctx, tp)
        position = block * rows + row
        if kind == "trace":
            hidden_trace = (lane < rows) & (position > first_position + lane)
            hidden_suffix = (lane == rows) & (
                (position >= prefix) | ((position >= del_start) & (position < del_end))
            )
            hidden = hidden_trace | hidden_suffix
        else:
            hidden = (lane < rows) | ((lane > rows) & (position > tp * rows + (lane - rows - 1)))
        k_aug_ref[index * rows:(index + 1) * rows, :] = jnp.where(hidden, MASKED, 0.0).astype(jnp.bfloat16)
    total = rows * len(slots)
    ones = jnp.ones((total, HEAD_SIZE), jnp.bfloat16)

    def columns(index):
        return slice(index * HEAD_SIZE, (index + 1) * HEAD_SIZE)

    def stacked(index):
        return jnp.concatenate([piece[:, columns(index)] for piece in pieces], axis=0)

    def scores_of(g):
        query = jnp.concatenate(
            [ref[:, columns(g * GROUP + j)] for ref in (tq, sq) for j in range(GROUP)], axis=0
        )
        query = jnp.concatenate([query, q_aug], axis=1)
        return dot_t(query, jnp.concatenate([stacked(2 * g), k_aug_ref[...]], axis=1))

    def absorb_head(g, scores):
        top = jnp.broadcast_to(jnp.max(scores, axis=1, keepdims=True), (2 * half, HEAD_SIZE))
        if not first_call:
            old_top = top_in[g]
            top = jnp.maximum(old_top, top)
        shifted = scores - jnp.concatenate([top] * (total // HEAD_SIZE), axis=1)
        weights = jnp.exp2(shifted * SCALE).astype(jnp.bfloat16)
        both = dot(weights, jnp.concatenate([stacked(2 * g + 1), ones], axis=1))
        summed, denominator = both[:, :HEAD_SIZE], both[:, HEAD_SIZE:]
        if not first_call:
            rescale = jnp.exp2((old_top - top) * SCALE)
            summed = summed + sum_in[g] * rescale
            denominator = denominator + denominator_in[g] * rescale
        if last_call:
            inverse = pl.reciprocal(denominator, approx=True)
            inverse = inverse * (2.0 - denominator * inverse)
            result = (summed * inverse).astype(jnp.bfloat16)
            for j in range(GROUP):
                outs[0][:, columns(g * GROUP + j)] = result[j * rows:(j + 1) * rows]
                outs[1][:, columns(g * GROUP + j)] = result[half + j * rows:half + (j + 1) * rows]
        else:
            for out, state in zip(outs, (top, denominator, summed)):
                out[g] = state

    ahead = scores_of(0)
    for g in range(KEY_VALUE_HEADS):
        now, ahead = ahead, scores_of(g + 1) if g + 1 < KEY_VALUE_HEADS else None
        absorb_head(g, now)


def attend(spans, tq, sq, pieces, slots, tp_size, carry, last_call):
    first_call = carry is None
    rows = tq.shape[0]
    vmem = pl.BlockSpec(memory_space=pltpu.VMEM)
    operands = [spans, tq, sq, *pieces]
    if not first_call:
        operands += list(carry)
    if last_call:
        out_shape = [jax.ShapeDtypeStruct(tq.shape, jnp.bfloat16)] * 2
    else:
        state = (KEY_VALUE_HEADS, 2 * GROUP * rows, HEAD_SIZE)
        out_shape = [jax.ShapeDtypeStruct(state, jnp.float32)] * 3
    all_rows = sum(p.shape[0] for p in pieces)
    flops = 2 * 2 * QUERY_HEADS * rows * all_rows * PAIR * 2
    return pl.pallas_call(
        functools.partial(attend_kernel, slots, tp_size, first_call, last_call),
        out_shape=out_shape,
        in_specs=[vmem] * len(operands),
        out_specs=[vmem] * len(out_shape),
        scratch_shapes=[pltpu.VMEM((all_rows, HEAD_SIZE), jnp.bfloat16)],
        compiler_params=pltpu.CompilerParams(vmem_limit_bytes=32 * 1024 * 1024),
        cost_estimate=pl.CostEstimate(
            flops=flops, bytes_accessed=all_rows * 4096, transcendentals=2 * QUERY_HEADS * rows * all_rows
        ),
    )(*operands)


def swap(array, axis, bit, size):
    return lax.ppermute(array, axis, [(i, i ^ bit) for i in range(size)])


def after(array, *others):
    return lax.optimization_barrier((array, *others))[0]


def local(ctx_size, tp_size, trace_q, trace_key_value, suffix_q, suffix_key_value, prefix_len, del_start, del_end):
    rows = trace_q.shape[0]
    spans = jnp.broadcast_to(jnp.stack([prefix_len, del_start, del_end]), (3, HEAD_SIZE))
    sq = suffix_q[0]
    suffix_own = suffix_key_value[0]

    core = lambda a: swap(a, "tp", 1, tp_size)
    across_y = lambda a: swap(a, "tp", 2, tp_size)
    across_x = lambda a: swap(a, "ctx", 1, ctx_size)
    along_z = lambda a, shift: lax.ppermute(
        a, "ctx", [(i, (i + 2 * shift) % ctx_size) for i in range(ctx_size)]
    )

    across_both = lambda a: lax.ppermute(
        a,
        ("ctx", "tp"),
        [(i * tp_size + j, (i ^ 1) * tp_size + (j ^ 2)) for i in range(ctx_size) for j in range(tp_size)],
    )

    def slot(place, c):
        if isinstance(place, int):
            return lambda ctx, tp: ("suffix", tp ^ place ^ c)
        shift, x, y = place
        return lambda ctx, tp: (
            "trace",
            (((ctx + ctx_size - 2 * shift) % ctx_size) ^ x) * tp_size + (tp ^ (2 * y + c)),
        )

    def absorb(pieces, slots, state, last_call=False):
        return attend(spans, trace_q, sq, pieces, slots, tp_size, state, last_call)

    def absorb_both(mine, sibling, places, state, last_call=False):
        slots = [slot(place, c) for c in (0, 1) for place in places]
        return absorb(mine + sibling, slots, state, last_call)

    if ctx_size == 8 and tp_size == 4:
        barrier = lax.optimization_barrier
        up, down = along_z(trace_key_value, 1), along_z(trace_key_value, 3)
        own_x, own_y = across_x(trace_key_value), across_y(trace_key_value)
        own_d = across_both(trace_key_value)
        up, down, own_x, own_y, own_d, spans = barrier((up, down, own_x, own_y, own_d, spans))

        near_x = across_x(jnp.concatenate([up, down], axis=0))
        near_y = across_y(jnp.concatenate([up, down, suffix_own], axis=0))
        up_two = along_z(jnp.concatenate([up, own_d], axis=0), 1)
        down_d = along_z(own_d, 3)
        plane = jnp.concatenate([trace_key_value, own_x, own_y, own_d, up, down, suffix_own], axis=0)
        plane_core = core(plane)
        cut = 6 * rows
        here = [(0, 0, 0), (0, 1, 0), (0, 0, 1), (0, 1, 1), (1, 0, 0), (3, 0, 0)]
        state = absorb_both([plane[:cut]], [plane_core[:cut]], here, None)

        near_x, near_y, state = barrier((near_x, near_y, state))
        sides = jnp.concatenate([near_x, near_y], axis=0)
        sides_core = core(sides)
        far, up_d = up_two[:rows], up_two[rows:]
        far_x, far_y, far_d = across_x(far), across_y(far), along_z(up_d, 1)
        mixed = jnp.concatenate([up_two, down_d], axis=0)
        mixed_core = core(mixed)
        here = [0, (1, 1, 0), (3, 1, 0), (1, 0, 1), (3, 0, 1), 2]
        state = absorb_both([plane[cut:], sides], [plane_core[cut:], sides_core], here, state)

        far_x, far_y, far_d, state = barrier((far_x, far_y, far_d, state))
        rest = jnp.concatenate([far_x, far_y, far_d], axis=0)
        here = [(2, 0, 0), (1, 1, 1), (3, 1, 1), (2, 1, 0), (2, 0, 1), (2, 1, 1)]
        trace_out, suffix_out = absorb_both([mixed, rest], [mixed_core, core(rest)], here, state, True)
    else:
        gathered = lax.all_gather(trace_key_value, ("ctx", "tp"), axis=0, tiled=True)
        suffix_all = lax.all_gather(suffix_own, "tp", axis=0, tiled=True)
        state = None
        for at in range(0, gathered.shape[0], CHUNK_ROWS):
            last_call = at + CHUNK_ROWS >= gathered.shape[0]
            pieces = [gathered[at:at + CHUNK_ROWS]]
            slots = [
                lambda ctx, tp, block=block: ("trace", block)
                for block in range(at // rows, min(at + CHUNK_ROWS, gathered.shape[0]) // rows)
            ]
            if at == 0:
                pieces.append(suffix_all)
                slots += [lambda ctx, tp, block=block: ("suffix", block) for block in range(tp_size)]
            state = absorb(pieces, slots, state, last_call)
        trace_out, suffix_out = state
    return trace_out, suffix_out[None]


def solution(mesh):
    return jax.shard_map(
        functools.partial(local, mesh.shape["ctx"], mesh.shape["tp"]),
        mesh=mesh,
        in_specs=(
            P(("ctx", "tp"), None),
            P(("ctx", "tp"), None),
            P("ctx", "tp", None),
            P("ctx", "tp", None),
            P("ctx"),
            P("ctx"),
            P("ctx"),
        ),
        out_specs=(P(("ctx", "tp"), None), P("ctx", "tp", None)),
        check_vma=False,
    )
```

```python
import functools

import jax
import jax.numpy as jnp
from jax import lax
from jax.experimental import pallas as pl
from jax.experimental.pallas import tpu as pltpu
from jax.sharding import PartitionSpec as P

QUERY_HEADS = 40
KEY_VALUE_HEADS = 8
HEAD_SIZE = 128
GROUP = QUERY_HEADS // KEY_VALUE_HEADS
PAIR = 2 * HEAD_SIZE
LOG2E = 1.4426950408889634
SCALE = HEAD_SIZE ** (-0.5) * LOG2E
MASKED = -1e30
CHUNK_ROWS = 1024


def dot_t(a, b):
    return lax.dot_general(a, b, (((1,), (1,)), ((), ())), preferred_element_type=jnp.float32)


def dot(a, b):
    return lax.dot_general(a, b, (((1,), (0,)), ((), ())), preferred_element_type=jnp.float32)


def attend_kernel(slots, tp_size, first_call, last_call, *refs):
    refs = list(refs)
    spans, tq, sq = refs[:3]
    del refs[:3]
    k_aug_ref = refs.pop()
    outs, refs = (refs[-2:], refs[:-2]) if last_call else (refs[-3:], refs[:-3])
    if not first_call:
        top_in, denominator_in, sum_in = refs[-3:]
        del refs[-3:]
    pieces = refs

    rows = tq.shape[0]
    half = GROUP * rows
    ctx = lax.axis_index("ctx").astype(jnp.int32)
    tp = lax.axis_index("tp").astype(jnp.int32)
    first_position = (ctx * tp_size + tp) * rows
    prefix, del_start, del_end = spans[0:1], spans[1:2], spans[2:3]
    lane = lax.broadcasted_iota(jnp.int32, (rows, HEAD_SIZE), 1)
    row = lax.broadcasted_iota(jnp.int32, (rows, HEAD_SIZE), 0)
    q_trace_aug = jnp.where(lane == row, 1.0, 0.0).astype(jnp.bfloat16)
    q_suffix_aug = jnp.where((lane == rows) | (lane == rows + 1 + row), 1.0, 0.0).astype(jnp.bfloat16)
    q_aug = jnp.concatenate([q_trace_aug] * GROUP + [q_suffix_aug] * GROUP, axis=0)
    for index, slot in enumerate(slots):
        kind, block = slot(ctx, tp)
        position = block * rows + row
        if kind == "trace":
            hidden_trace = (lane < rows) & (position > first_position + lane)
            hidden_suffix = (lane == rows) & (
                (position >= prefix) | ((position >= del_start) & (position < del_end))
            )
            hidden = hidden_trace | hidden_suffix
        else:
            hidden = (lane < rows) | ((lane > rows) & (position > tp * rows + (lane - rows - 1)))
        k_aug_ref[index * rows:(index + 1) * rows, :] = jnp.where(hidden, MASKED, 0.0).astype(jnp.bfloat16)
    total = rows * len(slots)
    ones = jnp.ones((total, HEAD_SIZE), jnp.bfloat16)

    def columns(index):
        return slice(index * HEAD_SIZE, (index + 1) * HEAD_SIZE)

    def stacked(index):
        return jnp.concatenate([piece[:, columns(index)] for piece in pieces], axis=0)

    def scores_of(g):
        query = jnp.concatenate(
            [ref[:, columns(g * GROUP + j)] for ref in (tq, sq) for j in range(GROUP)], axis=0
        )
        query = jnp.concatenate([query, q_aug], axis=1)
        return dot_t(query, jnp.concatenate([stacked(2 * g), k_aug_ref[...]], axis=1))

    def absorb_head(g, scores):
        top = jnp.broadcast_to(jnp.max(scores, axis=1, keepdims=True), (2 * half, HEAD_SIZE))
        if not first_call:
            old_top = top_in[g]
            top = jnp.maximum(old_top, top)
        shifted = scores - jnp.concatenate([top] * (total // HEAD_SIZE), axis=1)
        weights = jnp.exp2(shifted * SCALE).astype(jnp.bfloat16)
        both = dot(weights, jnp.concatenate([stacked(2 * g + 1), ones], axis=1))
        summed, denominator = both[:, :HEAD_SIZE], both[:, HEAD_SIZE:]
        if not first_call:
            rescale = jnp.exp2((old_top - top) * SCALE)
            summed = summed + sum_in[g] * rescale
            denominator = denominator + denominator_in[g] * rescale
        if last_call:
            inverse = pl.reciprocal(denominator, approx=True)
            inverse = inverse * (2.0 - denominator * inverse)
            result = (summed * inverse).astype(jnp.bfloat16)
            for j in range(GROUP):
                outs[0][:, columns(g * GROUP + j)] = result[j * rows:(j + 1) * rows]
                outs[1][:, columns(g * GROUP + j)] = result[half + j * rows:half + (j + 1) * rows]
        else:
            for out, state in zip(outs, (top, denominator, summed)):
                out[g] = state

    ahead = scores_of(0)
    for g in range(KEY_VALUE_HEADS):
        now, ahead = ahead, scores_of(g + 1) if g + 1 < KEY_VALUE_HEADS else None
        absorb_head(g, now)


def attend(spans, tq, sq, pieces, slots, tp_size, carry, last_call):
    first_call = carry is None
    rows = tq.shape[0]
    vmem = pl.BlockSpec(memory_space=pltpu.VMEM)
    operands = [spans, tq, sq, *pieces]
    if not first_call:
        operands += list(carry)
    if last_call:
        out_shape = [jax.ShapeDtypeStruct(tq.shape, jnp.bfloat16)] * 2
    else:
        state = (KEY_VALUE_HEADS, 2 * GROUP * rows, HEAD_SIZE)
        out_shape = [jax.ShapeDtypeStruct(state, jnp.float32)] * 3
    all_rows = sum(p.shape[0] for p in pieces)
    flops = 2 * 2 * QUERY_HEADS * rows * all_rows * PAIR * 2
    return pl.pallas_call(
        functools.partial(attend_kernel, slots, tp_size, first_call, last_call),
        out_shape=out_shape,
        in_specs=[vmem] * len(operands),
        out_specs=[vmem] * len(out_shape),
        scratch_shapes=[pltpu.VMEM((all_rows, HEAD_SIZE), jnp.bfloat16)],
        compiler_params=pltpu.CompilerParams(vmem_limit_bytes=32 * 1024 * 1024),
        cost_estimate=pl.CostEstimate(
            flops=flops, bytes_accessed=all_rows * 4096, transcendentals=2 * QUERY_HEADS * rows * all_rows
        ),
    )(*operands)


def swap(array, axis, bit, size):
    return lax.ppermute(array, axis, [(i, i ^ bit) for i in range(size)])


def after(array, *others):
    return lax.optimization_barrier((array, *others))[0]


def local(ctx_size, tp_size, trace_q, trace_key_value, suffix_q, suffix_key_value, prefix_len, del_start, del_end):
    rows = trace_q.shape[0]
    spans = jnp.broadcast_to(jnp.stack([prefix_len, del_start, del_end]), (3, HEAD_SIZE))
    sq = suffix_q[0]
    suffix_own = suffix_key_value[0]

    core = lambda a: swap(a, "tp", 1, tp_size)
    across_y = lambda a: swap(a, "tp", 2, tp_size)
    across_x = lambda a: swap(a, "ctx", 1, ctx_size)
    along_z = lambda a, shift: lax.ppermute(
        a, "ctx", [(i, (i + 2 * shift) % ctx_size) for i in range(ctx_size)]
    )

    across_both = lambda a: lax.ppermute(
        a,
        ("ctx", "tp"),
        [(i * tp_size + j, (i ^ 1) * tp_size + (j ^ 2)) for i in range(ctx_size) for j in range(tp_size)],
    )

    def slot(place, c):
        if isinstance(place, int):
            return lambda ctx, tp: ("suffix", tp ^ place ^ c)
        shift, x, y = place
        return lambda ctx, tp: (
            "trace",
            (((ctx + ctx_size - 2 * shift) % ctx_size) ^ x) * tp_size + (tp ^ (2 * y + c)),
        )

    def absorb(pieces, slots, state, last_call=False):
        return attend(spans, trace_q, sq, pieces, slots, tp_size, state, last_call)

    def absorb_both(mine, sibling, places, state, last_call=False):
        slots = [slot(place, c) for c in (0, 1) for place in places]
        return absorb(mine + sibling, slots, state, last_call)

    if ctx_size == 8 and tp_size == 4:
        barrier = lax.optimization_barrier
        up, down = along_z(trace_key_value, 1), along_z(trace_key_value, 3)
        own_x, own_y = across_x(trace_key_value), across_y(trace_key_value)
        own_d = across_both(trace_key_value)
        up, down, own_x, own_y, own_d, spans = barrier((up, down, own_x, own_y, own_d, spans))

        near_x = across_x(jnp.concatenate([up, down], axis=0))
        near_y = across_y(jnp.concatenate([up, down, suffix_own], axis=0))
        up_two = along_z(jnp.concatenate([up, own_d], axis=0), 1)
        down_d = along_z(own_d, 3)
        plane = jnp.concatenate([trace_key_value, own_x, own_y, own_d, up, down, suffix_own], axis=0)
        plane_core = core(plane)
        near_x, near_y, up_two, plane, plane_core = barrier((near_x, near_y, up_two, plane, plane_core))
        sides = jnp.concatenate([near_x, near_y], axis=0)
        sides_core = core(sides)
        far, up_d = up_two[:rows], up_two[rows:]
        far_x, far_y, far_d = across_x(far), across_y(far), along_z(up_d, 1)
        mixed = jnp.concatenate([up_two, down_d], axis=0)
        mixed_core = core(mixed)
        cut = 6 * rows
        here = [(0, 0, 0), (0, 1, 0), (0, 0, 1), (0, 1, 1), (1, 0, 0), (3, 0, 0)]
        state = absorb_both([plane[:cut]], [plane_core[:cut]], here, None)
        here = [0, (1, 1, 0), (3, 1, 0), (1, 0, 1), (3, 0, 1), 2]
        state = absorb_both([plane[cut:], sides], [plane_core[cut:], sides_core], here, state)

        far_x, far_y, far_d, state = barrier((far_x, far_y, far_d, state))
        rest = jnp.concatenate([far_x, far_y, far_d], axis=0)
        here = [(2, 0, 0), (1, 1, 1), (3, 1, 1), (2, 1, 0), (2, 0, 1), (2, 1, 1)]
        trace_out, suffix_out = absorb_both([mixed, rest], [mixed_core, core(rest)], here, state, True)
    else:
        gathered = lax.all_gather(trace_key_value, ("ctx", "tp"), axis=0, tiled=True)
        suffix_all = lax.all_gather(suffix_own, "tp", axis=0, tiled=True)
        state = None
        for at in range(0, gathered.shape[0], CHUNK_ROWS):
            last_call = at + CHUNK_ROWS >= gathered.shape[0]
            pieces = [gathered[at:at + CHUNK_ROWS]]
            slots = [
                lambda ctx, tp, block=block: ("trace", block)
                for block in range(at // rows, min(at + CHUNK_ROWS, gathered.shape[0]) // rows)
            ]
            if at == 0:
                pieces.append(suffix_all)
                slots += [lambda ctx, tp, block=block: ("suffix", block) for block in range(tp_size)]
            state = absorb(pieces, slots, state, last_call)
        trace_out, suffix_out = state
    return trace_out, suffix_out[None]


def solution(mesh):
    return jax.shard_map(
        functools.partial(local, mesh.shape["ctx"], mesh.shape["tp"]),
        mesh=mesh,
        in_specs=(
            P(("ctx", "tp"), None),
            P(("ctx", "tp"), None),
            P("ctx", "tp", None),
            P("ctx", "tp", None),
            P("ctx"),
            P("ctx"),
            P("ctx"),
        ),
        out_specs=(P(("ctx", "tp"), None), P("ctx", "tp", None)),
        check_vma=False,
    )
```

```python
import functools

import jax
import jax.numpy as jnp
from jax import lax
from jax.experimental import pallas as pl
from jax.experimental.pallas import tpu as pltpu
from jax.sharding import PartitionSpec as P

QUERY_HEADS = 40
KEY_VALUE_HEADS = 8
HEAD_SIZE = 128
GROUP = QUERY_HEADS // KEY_VALUE_HEADS
PAIR = 2 * HEAD_SIZE
LOG2E = 1.4426950408889634
SCALE = HEAD_SIZE ** (-0.5) * LOG2E
MASKED = -1e30
CHUNK_ROWS = 1024


def dot_t(a, b):
    return lax.dot_general(a, b, (((1,), (1,)), ((), ())), preferred_element_type=jnp.float32)


def dot(a, b):
    return lax.dot_general(a, b, (((1,), (0,)), ((), ())), preferred_element_type=jnp.float32)


def attend_kernel(slots, ranges, tp_size, first_call, last_call, *refs):
    refs = list(refs)
    spans, tq, sq = refs[:3]
    del refs[:3]
    k_aug_ref = refs.pop()
    outs, refs = (refs[-2:], refs[:-2]) if last_call else (refs[-3:], refs[:-3])
    if not first_call:
        top_in, denominator_in, sum_in = refs[-3:]
        del refs[-3:]
    pieces = refs

    rows = tq.shape[0]
    half = GROUP * rows
    ctx = lax.axis_index("ctx").astype(jnp.int32)
    tp = lax.axis_index("tp").astype(jnp.int32)
    first_position = (ctx * tp_size + tp) * rows
    prefix, del_start, del_end = spans[0:1], spans[1:2], spans[2:3]
    lane = lax.broadcasted_iota(jnp.int32, (rows, HEAD_SIZE), 1)
    row = lax.broadcasted_iota(jnp.int32, (rows, HEAD_SIZE), 0)
    q_trace_aug = jnp.where(lane == row, 1.0, 0.0).astype(jnp.bfloat16)
    q_suffix_aug = jnp.where((lane == rows) | (lane == rows + 1 + row), 1.0, 0.0).astype(jnp.bfloat16)
    q_aug = jnp.concatenate([q_trace_aug] * GROUP + [q_suffix_aug] * GROUP, axis=0)
    for index, slot in enumerate(slots):
        kind, block = slot(ctx, tp)
        position = block * rows + row
        if kind == "trace":
            hidden_trace = (lane < rows) & (position > first_position + lane)
            hidden_suffix = (lane == rows) & (
                (position >= prefix) | ((position >= del_start) & (position < del_end))
            )
            hidden = hidden_trace | hidden_suffix
        else:
            hidden = (lane < rows) | ((lane > rows) & (position > tp * rows + (lane - rows - 1)))
        k_aug_ref[index * rows:(index + 1) * rows, :] = jnp.where(hidden, MASKED, 0.0).astype(jnp.bfloat16)
    filled, total = rows * len(slots), k_aug_ref.shape[0]
    if filled < total:
        k_aug_ref[filled:total, :] = jnp.full((total - filled, HEAD_SIZE), MASKED, jnp.bfloat16)
        padding = [jnp.zeros((total - filled, HEAD_SIZE), jnp.bfloat16)]
    else:
        padding = []
    ones = jnp.ones((total, HEAD_SIZE), jnp.bfloat16)

    def columns(index):
        return slice(index * HEAD_SIZE, (index + 1) * HEAD_SIZE)

    def stacked(index):
        parts = [piece[start:stop, columns(index)] for piece, (start, stop) in zip(pieces, ranges)]
        return jnp.concatenate(parts + padding, axis=0)

    def scores_of(g):
        query = jnp.concatenate(
            [ref[:, columns(g * GROUP + j)] for ref in (tq, sq) for j in range(GROUP)], axis=0
        )
        query = jnp.concatenate([query, q_aug], axis=1)
        return dot_t(query, jnp.concatenate([stacked(2 * g), k_aug_ref[...]], axis=1))

    def absorb_head(g, scores):
        top = jnp.broadcast_to(jnp.max(scores, axis=1, keepdims=True), (2 * half, HEAD_SIZE))
        if not first_call:
            old_top = top_in[g]
            top = jnp.maximum(old_top, top)
        shifted = scores - jnp.concatenate([top] * (total // HEAD_SIZE), axis=1)
        weights = jnp.exp2(shifted * SCALE).astype(jnp.bfloat16)
        both = dot(weights, jnp.concatenate([stacked(2 * g + 1), ones], axis=1))
        summed, denominator = both[:, :HEAD_SIZE], both[:, HEAD_SIZE:]
        if not first_call:
            rescale = jnp.exp2((old_top - top) * SCALE)
            summed = summed + sum_in[g] * rescale
            denominator = denominator + denominator_in[g] * rescale
        if last_call:
            inverse = pl.reciprocal(denominator, approx=True)
            inverse = inverse * (2.0 - denominator * inverse)
            result = (summed * inverse).astype(jnp.bfloat16)
            for j in range(GROUP):
                outs[0][:, columns(g * GROUP + j)] = result[j * rows:(j + 1) * rows]
                outs[1][:, columns(g * GROUP + j)] = result[half + j * rows:half + (j + 1) * rows]
        else:
            for out, state in zip(outs, (top, denominator, summed)):
                out[g] = state

    ahead = scores_of(0)
    for g in range(KEY_VALUE_HEADS):
        now, ahead = ahead, scores_of(g + 1) if g + 1 < KEY_VALUE_HEADS else None
        absorb_head(g, now)


def attend(spans, tq, sq, pieces, slots, tp_size, carry, last_call):
    first_call = carry is None
    rows = tq.shape[0]
    vmem = pl.BlockSpec(memory_space=pltpu.VMEM)
    operands = [spans, tq, sq, *(piece for piece, _, _ in pieces)]
    if not first_call:
        operands += list(carry)
    if last_call:
        out_shape = [jax.ShapeDtypeStruct(tq.shape, jnp.bfloat16)] * 2
    else:
        state = (KEY_VALUE_HEADS, 2 * GROUP * rows, HEAD_SIZE)
        out_shape = [jax.ShapeDtypeStruct(state, jnp.float32)] * 3
    ranges = tuple((first * rows, last * rows) for _, first, last in pieces)
    all_rows = pl.cdiv(sum(stop - start for start, stop in ranges), HEAD_SIZE) * HEAD_SIZE
    flops = 2 * 2 * QUERY_HEADS * rows * all_rows * PAIR * 2
    return pl.pallas_call(
        functools.partial(attend_kernel, slots, ranges, tp_size, first_call, last_call),
        out_shape=out_shape,
        in_specs=[vmem] * len(operands),
        out_specs=[vmem] * len(out_shape),
        scratch_shapes=[pltpu.VMEM((all_rows, HEAD_SIZE), jnp.bfloat16)],
        compiler_params=pltpu.CompilerParams(vmem_limit_bytes=32 * 1024 * 1024),
        cost_estimate=pl.CostEstimate(
            flops=flops, bytes_accessed=all_rows * 4096, transcendentals=2 * QUERY_HEADS * rows * all_rows
        ),
    )(*operands)


def swap(array, axis, bit, size):
    return lax.ppermute(array, axis, [(i, i ^ bit) for i in range(size)])


def after(array, *others):
    return lax.optimization_barrier((array, *others))[0]


def local(ctx_size, tp_size, trace_q, trace_key_value, suffix_q, suffix_key_value, prefix_len, del_start, del_end):
    rows = trace_q.shape[0]
    spans = jnp.broadcast_to(jnp.stack([prefix_len, del_start, del_end]), (3, HEAD_SIZE))
    sq = suffix_q[0]
    suffix_own = suffix_key_value[0]

    core = lambda a: swap(a, "tp", 1, tp_size)
    across_y = lambda a: swap(a, "tp", 2, tp_size)
    across_x = lambda a: swap(a, "ctx", 1, ctx_size)
    along_z = lambda a, shift: lax.ppermute(
        a, "ctx", [(i, (i + 2 * shift) % ctx_size) for i in range(ctx_size)]
    )

    across_both = lambda a: lax.ppermute(
        a,
        ("ctx", "tp"),
        [(i * tp_size + j, (i ^ 1) * tp_size + (j ^ 2)) for i in range(ctx_size) for j in range(tp_size)],
    )

    def slot(place, c):
        if isinstance(place, int):
            return lambda ctx, tp: ("suffix", tp ^ place ^ c)
        shift, x, y = place
        return lambda ctx, tp: (
            "trace",
            (((ctx + ctx_size - 2 * shift) % ctx_size) ^ x) * tp_size + (tp ^ (2 * y + c)),
        )

    def slots_of(places, c=0):
        return [slot(place, c) for place in places]

    def absorb(pieces, slots, state, last_call=False):
        return attend(spans, trace_q, sq, pieces, slots, tp_size, state, last_call)

    if ctx_size == 8 and tp_size == 4:
        barrier = lax.optimization_barrier
        up, down = along_z(trace_key_value, 1), along_z(trace_key_value, 3)
        own_x, own_y = across_x(trace_key_value), across_y(trace_key_value)
        own_d = across_both(trace_key_value)
        up, down, own_x, own_y, own_d, spans = barrier((up, down, own_x, own_y, own_d, spans))

        near = jnp.concatenate([up, down], axis=0)
        up_two, down_d = along_z(jnp.concatenate([up, own_d], axis=0), 1), along_z(own_d, 3)
        near_x, near_y = across_x(near), across_y(near)
        plane = jnp.concatenate([trace_key_value, own_x, own_y, own_d, up, down, suffix_own], axis=0)
        here = [(0, 0, 0), (0, 1, 0), (0, 0, 1), (0, 1, 1), (1, 0, 0), (3, 0, 0)]
        state = absorb([(plane, 0, 7)], slots_of(here + [0]), None)

        near_x, near_y, up_two, down_d, state = barrier((near_x, near_y, up_two, down_d, state))
        far, up_d = up_two[:rows], up_two[rows:]
        far_y = across_y(jnp.concatenate([far, suffix_own], axis=0))
        far_x, far_d = across_x(far), along_z(up_d, 1)
        sides = jnp.concatenate([plane, near_x, near_y, up_d, down_d, far], axis=0)
        sibling = core(sides)
        near_here = [(1, 1, 0), (3, 1, 0), (1, 0, 1), (3, 0, 1), (1, 1, 1), (3, 1, 1)]
        state = absorb([(sides, 7, 13), (sibling, 0, 6)], slots_of(near_here) + slots_of(here, 1), state)

        far_x, far_y, far_d, state = barrier((far_x, far_y, far_d, state))
        rest = jnp.concatenate([far_x, far_y, far_d], axis=0)
        rest_sibling = core(rest)
        state = absorb(
            [(sides, 13, 14), (sibling, 7, 14)], slots_of([(2, 0, 0)]) + slots_of(near_here + [(2, 0, 0)], 1), state
        )
        here = [(2, 1, 0), (2, 0, 1), 2, (2, 1, 1)]
        trace_out, suffix_out = absorb(
            [(rest, 0, 4), (rest_sibling, 0, 4), (sibling, 6, 7)],
            slots_of(here) + slots_of(here + [0], 1),
            state,
            True,
        )
    else:
        gathered = lax.all_gather(trace_key_value, ("ctx", "tp"), axis=0, tiled=True)
        suffix_all = lax.all_gather(suffix_own, "tp", axis=0, tiled=True)
        state = None
        for at in range(0, gathered.shape[0], CHUNK_ROWS):
            last_call = at + CHUNK_ROWS >= gathered.shape[0]
            pieces = [(gathered[at:at + CHUNK_ROWS], 0, min(CHUNK_ROWS, gathered.shape[0] - at) // rows)]
            slots = [
                lambda ctx, tp, block=block: ("trace", block)
                for block in range(at // rows, min(at + CHUNK_ROWS, gathered.shape[0]) // rows)
            ]
            if at == 0:
                pieces.append((suffix_all, 0, tp_size))
                slots += [lambda ctx, tp, block=block: ("suffix", block) for block in range(tp_size)]
            state = absorb(pieces, slots, state, last_call)
        trace_out, suffix_out = state
    return trace_out, suffix_out[None]


def solution(mesh):
    return jax.shard_map(
        functools.partial(local, mesh.shape["ctx"], mesh.shape["tp"]),
        mesh=mesh,
        in_specs=(
            P(("ctx", "tp"), None),
            P(("ctx", "tp"), None),
            P("ctx", "tp", None),
            P("ctx", "tp", None),
            P("ctx"),
            P("ctx"),
            P("ctx"),
        ),
        out_specs=(P(("ctx", "tp"), None), P("ctx", "tp", None)),
        check_vma=False,
    )
```

```python
import functools

import jax
import jax.numpy as jnp
from jax import lax
from jax.experimental import pallas as pl
from jax.experimental.pallas import tpu as pltpu
from jax.sharding import PartitionSpec as P

QUERY_HEADS = 40
KEY_VALUE_HEADS = 8
HEAD_SIZE = 128
GROUP = QUERY_HEADS // KEY_VALUE_HEADS
PAIR = 2 * HEAD_SIZE
LOG2E = 1.4426950408889634
SCALE = HEAD_SIZE ** (-0.5) * LOG2E
MASKED = -1e30
CHUNK_ROWS = 1024


def dot_t(a, b):
    return lax.dot_general(a, b, (((1,), (1,)), ((), ())), preferred_element_type=jnp.float32)


def dot(a, b):
    return lax.dot_general(a, b, (((1,), (0,)), ((), ())), preferred_element_type=jnp.float32)


def attend_kernel(slots, ranges, tp_size, first_call, last_call, *refs):
    refs = list(refs)
    spans, tq, sq = refs[:3]
    del refs[:3]
    k_aug_ref = refs.pop()
    outs, refs = (refs[-2:], refs[:-2]) if last_call else (refs[-3:], refs[:-3])
    if not first_call:
        top_in, denominator_in, sum_in = refs[-3:]
        del refs[-3:]
    pieces = refs

    rows = tq.shape[0]
    half = GROUP * rows
    ctx = lax.axis_index("ctx").astype(jnp.int32)
    tp = lax.axis_index("tp").astype(jnp.int32)
    first_position = (ctx * tp_size + tp) * rows
    prefix, del_start, del_end = spans[0:1], spans[1:2], spans[2:3]
    lane = lax.broadcasted_iota(jnp.int32, (rows, HEAD_SIZE), 1)
    row = lax.broadcasted_iota(jnp.int32, (rows, HEAD_SIZE), 0)
    q_trace_aug = jnp.where(lane == row, 1.0, 0.0).astype(jnp.bfloat16)
    q_suffix_aug = jnp.where((lane == rows) | (lane == rows + 1 + row), 1.0, 0.0).astype(jnp.bfloat16)
    q_aug = jnp.concatenate([q_trace_aug] * GROUP + [q_suffix_aug] * GROUP, axis=0)
    for index, slot in enumerate(slots):
        kind, block = slot(ctx, tp)
        position = block * rows + row
        if kind == "trace":
            hidden_trace = (lane < rows) & (position > first_position + lane)
            hidden_suffix = (lane == rows) & (
                (position >= prefix) | ((position >= del_start) & (position < del_end))
            )
            hidden = hidden_trace | hidden_suffix
        else:
            hidden = (lane < rows) | ((lane > rows) & (position > tp * rows + (lane - rows - 1)))
        k_aug_ref[index * rows:(index + 1) * rows, :] = jnp.where(hidden, MASKED, 0.0).astype(jnp.bfloat16)
    filled, total = rows * len(slots), k_aug_ref.shape[0]
    if filled < total:
        k_aug_ref[filled:total, :] = jnp.full((total - filled, HEAD_SIZE), MASKED, jnp.bfloat16)
        padding = [jnp.zeros((total - filled, HEAD_SIZE), jnp.bfloat16)]
    else:
        padding = []
    ones = jnp.ones((total, HEAD_SIZE), jnp.bfloat16)

    def columns(index):
        return slice(index * HEAD_SIZE, (index + 1) * HEAD_SIZE)

    def stacked(index):
        parts = [piece[start:stop, columns(index)] for piece, (start, stop) in zip(pieces, ranges)]
        return jnp.concatenate(parts + padding, axis=0)

    def scores_of(g):
        query = jnp.concatenate(
            [ref[:, columns(g * GROUP + j)] for ref in (tq, sq) for j in range(GROUP)], axis=0
        )
        query = jnp.concatenate([query, q_aug], axis=1)
        return dot_t(query, jnp.concatenate([stacked(2 * g), k_aug_ref[...]], axis=1))

    def absorb_head(g, scores):
        top = jnp.broadcast_to(jnp.max(scores, axis=1, keepdims=True), (2 * half, HEAD_SIZE))
        if not first_call:
            old_top = top_in[g]
            top = jnp.maximum(old_top, top)
        shifted = scores - jnp.concatenate([top] * (total // HEAD_SIZE), axis=1)
        weights = jnp.exp2(shifted * SCALE).astype(jnp.bfloat16)
        both = dot(weights, jnp.concatenate([stacked(2 * g + 1), ones], axis=1))
        summed, denominator = both[:, :HEAD_SIZE], both[:, HEAD_SIZE:]
        if not first_call:
            rescale = jnp.exp2((old_top - top) * SCALE)
            summed = summed + sum_in[g] * rescale
            denominator = denominator + denominator_in[g] * rescale
        if last_call:
            inverse = pl.reciprocal(denominator, approx=True)
            inverse = inverse * (2.0 - denominator * inverse)
            result = (summed * inverse).astype(jnp.bfloat16)
            for j in range(GROUP):
                outs[0][:, columns(g * GROUP + j)] = result[j * rows:(j + 1) * rows]
                outs[1][:, columns(g * GROUP + j)] = result[half + j * rows:half + (j + 1) * rows]
        else:
            for out, state in zip(outs, (top, denominator, summed)):
                out[g] = state

    ahead = scores_of(0)
    for g in range(KEY_VALUE_HEADS):
        now, ahead = ahead, scores_of(g + 1) if g + 1 < KEY_VALUE_HEADS else None
        absorb_head(g, now)


def attend(spans, tq, sq, pieces, slots, tp_size, carry, last_call):
    first_call = carry is None
    rows = tq.shape[0]
    vmem = pl.BlockSpec(memory_space=pltpu.VMEM)
    operands = [spans, tq, sq, *(piece for piece, _, _ in pieces)]
    if not first_call:
        operands += list(carry)
    if last_call:
        out_shape = [jax.ShapeDtypeStruct(tq.shape, jnp.bfloat16)] * 2
    else:
        state = (KEY_VALUE_HEADS, 2 * GROUP * rows, HEAD_SIZE)
        out_shape = [jax.ShapeDtypeStruct(state, jnp.float32)] * 3
    ranges = tuple((first * rows, last * rows) for _, first, last in pieces)
    all_rows = pl.cdiv(sum(stop - start for start, stop in ranges), HEAD_SIZE) * HEAD_SIZE
    flops = 2 * 2 * QUERY_HEADS * rows * all_rows * PAIR * 2
    return pl.pallas_call(
        functools.partial(attend_kernel, slots, ranges, tp_size, first_call, last_call),
        out_shape=out_shape,
        in_specs=[vmem] * len(operands),
        out_specs=[vmem] * len(out_shape),
        scratch_shapes=[pltpu.VMEM((all_rows, HEAD_SIZE), jnp.bfloat16)],
        compiler_params=pltpu.CompilerParams(vmem_limit_bytes=32 * 1024 * 1024),
        cost_estimate=pl.CostEstimate(
            flops=flops, bytes_accessed=all_rows * 4096, transcendentals=2 * QUERY_HEADS * rows * all_rows
        ),
    )(*operands)


def swap(array, axis, bit, size):
    return lax.ppermute(array, axis, [(i, i ^ bit) for i in range(size)])


def after(array, *others):
    return lax.optimization_barrier((array, *others))[0]


def local(ctx_size, tp_size, trace_q, trace_key_value, suffix_q, suffix_key_value, prefix_len, del_start, del_end):
    rows = trace_q.shape[0]
    spans = jnp.broadcast_to(jnp.stack([prefix_len, del_start, del_end]), (3, HEAD_SIZE))
    sq = suffix_q[0]
    suffix_own = suffix_key_value[0]

    core = lambda a: swap(a, "tp", 1, tp_size)
    across_y = lambda a: swap(a, "tp", 2, tp_size)
    across_x = lambda a: swap(a, "ctx", 1, ctx_size)
    along_z = lambda a, flip: swap(a, "ctx", 2 * flip, ctx_size)

    across_both = lambda a: lax.ppermute(
        a,
        ("ctx", "tp"),
        [(i * tp_size + j, (i ^ 1) * tp_size + (j ^ 2)) for i in range(ctx_size) for j in range(tp_size)],
    )

    def slot(place, c):
        if isinstance(place, int):
            return lambda ctx, tp: ("suffix", tp ^ place ^ c)
        z, x, y = place
        return lambda ctx, tp: (
            "trace",
            (ctx ^ (2 * z + x)) * tp_size + (tp ^ (2 * y + c)),
        )

    def slots_of(places, c=0):
        return [slot(place, c) for place in places]

    def absorb(pieces, slots, state, last_call=False):
        return attend(spans, trace_q, sq, pieces, slots, tp_size, state, last_call)

    if ctx_size == 8 and tp_size == 4:
        barrier = lax.optimization_barrier
        next_z, third_z = along_z(trace_key_value, 1), along_z(trace_key_value, 3)
        own_x, own_y = across_x(trace_key_value), across_y(trace_key_value)
        own_d = across_both(trace_key_value)
        next_z, third_z, own_x, own_y, own_d, spans = barrier((next_z, third_z, own_x, own_y, own_d, spans))

        near = jnp.concatenate([next_z, third_z], axis=0)
        far_and_next_d, third_d = along_z(jnp.concatenate([third_z, own_d], axis=0), 1), along_z(own_d, 3)
        near_x, near_y = across_x(near), across_y(near)
        plane = jnp.concatenate([trace_key_value, own_x, own_y, own_d, near, suffix_own], axis=0)
        here = [(0, 0, 0), (0, 1, 0), (0, 0, 1), (0, 1, 1), (1, 0, 0), (3, 0, 0), 0]
        state = absorb([(plane, 0, 7)], slots_of(here), None)

        near_x, near_y, far_and_next_d, third_d, state = barrier((near_x, near_y, far_and_next_d, third_d, state))
        far = far_and_next_d[:rows]
        far_y = across_y(jnp.concatenate([far, suffix_own], axis=0))
        far_x, far_d = across_x(far), along_z(third_d, 1)
        sides = jnp.concatenate([plane, near_x, near_y, far_and_next_d, third_d], axis=0)
        sibling = core(sides)
        near_here = [(1, 1, 0), (3, 1, 0), (1, 0, 1), (3, 0, 1), (2, 0, 0), (1, 1, 1), (3, 1, 1)]
        state = absorb([(sides, 7, 14), (sibling, 0, 5)], slots_of(near_here) + slots_of(here[:5], 1), state)

        far_x, far_y, far_d, state = barrier((far_x, far_y, far_d, state))
        rest = jnp.concatenate([far_x, far_y, far_d], axis=0)
        rest_sibling = core(rest)
        state = absorb([(sibling, 5, 14)], slots_of(here[5:] + near_here, 1), state)
        here = [(2, 1, 0), (2, 0, 1), 2, (2, 1, 1)]
        trace_out, suffix_out = absorb(
            [(rest, 0, 4), (rest_sibling, 0, 4)], slots_of(here) + slots_of(here, 1), state, True
        )
    else:
        gathered = lax.all_gather(trace_key_value, ("ctx", "tp"), axis=0, tiled=True)
        suffix_all = lax.all_gather(suffix_own, "tp", axis=0, tiled=True)
        state = None
        for at in range(0, gathered.shape[0], CHUNK_ROWS):
            last_call = at + CHUNK_ROWS >= gathered.shape[0]
            pieces = [(gathered[at:at + CHUNK_ROWS], 0, min(CHUNK_ROWS, gathered.shape[0] - at) // rows)]
            slots = [
                lambda ctx, tp, block=block: ("trace", block)
                for block in range(at // rows, min(at + CHUNK_ROWS, gathered.shape[0]) // rows)
            ]
            if at == 0:
                pieces.append((suffix_all, 0, tp_size))
                slots += [lambda ctx, tp, block=block: ("suffix", block) for block in range(tp_size)]
            state = absorb(pieces, slots, state, last_call)
        trace_out, suffix_out = state
    return trace_out, suffix_out[None]


def solution(mesh):
    return jax.shard_map(
        functools.partial(local, mesh.shape["ctx"], mesh.shape["tp"]),
        mesh=mesh,
        in_specs=(
            P(("ctx", "tp"), None),
            P(("ctx", "tp"), None),
            P("ctx", "tp", None),
            P("ctx", "tp", None),
            P("ctx"),
            P("ctx"),
            P("ctx"),
        ),
        out_specs=(P(("ctx", "tp"), None), P("ctx", "tp", None)),
        check_vma=False,
    )
```

```python
import functools

import jax
import jax.numpy as jnp
from jax import lax
from jax.experimental import pallas as pl
from jax.experimental.pallas import tpu as pltpu
from jax.sharding import PartitionSpec as P

QUERY_HEADS = 40
KEY_VALUE_HEADS = 8
HEAD_SIZE = 128
GROUP = QUERY_HEADS // KEY_VALUE_HEADS
PAIR = 2 * HEAD_SIZE
LOG2E = 1.4426950408889634
SCALE = HEAD_SIZE ** (-0.5) * LOG2E
MASKED = -1e30
CHUNK_ROWS = 1024


def dot_t(a, b):
    return lax.dot_general(a, b, (((1,), (1,)), ((), ())), preferred_element_type=jnp.float32)


def dot(a, b):
    return lax.dot_general(a, b, (((1,), (0,)), ((), ())), preferred_element_type=jnp.float32)


def attend_kernel(slots, ranges, tp_size, first_call, last_call, *refs):
    refs = list(refs)
    spans, tq, sq = refs[:3]
    del refs[:3]
    k_aug_ref = refs.pop()
    outs, refs = (refs[-2:], refs[:-2]) if last_call else (refs[-3:], refs[:-3])
    if not first_call:
        top_in, denominator_in, sum_in = refs[-3:]
        del refs[-3:]
    pieces = refs

    rows = tq.shape[0]
    half = GROUP * rows
    ctx = lax.axis_index("ctx").astype(jnp.int32)
    tp = lax.axis_index("tp").astype(jnp.int32)
    first_position = (ctx * tp_size + tp) * rows
    prefix, del_start, del_end = spans[0:1], spans[1:2], spans[2:3]
    lane = lax.broadcasted_iota(jnp.int32, (rows, HEAD_SIZE), 1)
    row = lax.broadcasted_iota(jnp.int32, (rows, HEAD_SIZE), 0)
    q_trace_aug = jnp.where(lane == row, 1.0, 0.0).astype(jnp.bfloat16)
    q_suffix_aug = jnp.where((lane == rows) | (lane == rows + 1 + row), 1.0, 0.0).astype(jnp.bfloat16)
    q_aug = jnp.concatenate([q_trace_aug] * GROUP + [q_suffix_aug] * GROUP, axis=0)
    for index, slot in enumerate(slots):
        kind, block = slot(ctx, tp)
        position = block * rows + row
        if kind == "trace":
            hidden_trace = (lane < rows) & (position > first_position + lane)
            hidden_suffix = (lane == rows) & (
                (position >= prefix) | ((position >= del_start) & (position < del_end))
            )
            hidden = hidden_trace | hidden_suffix
        else:
            hidden = (lane < rows) | ((lane > rows) & (position > tp * rows + (lane - rows - 1)))
        k_aug_ref[index * rows:(index + 1) * rows, :] = jnp.where(hidden, MASKED, 0.0).astype(jnp.bfloat16)
    filled, total = rows * len(slots), k_aug_ref.shape[0]
    if filled < total:
        k_aug_ref[filled:total, :] = jnp.full((total - filled, HEAD_SIZE), MASKED, jnp.bfloat16)
        padding = [jnp.zeros((total - filled, HEAD_SIZE), jnp.bfloat16)]
    else:
        padding = []
    ones = jnp.ones((total, HEAD_SIZE), jnp.bfloat16)

    def columns(index):
        return slice(index * HEAD_SIZE, (index + 1) * HEAD_SIZE)

    def stacked(index):
        parts = [piece[start:stop, columns(index)] for piece, (start, stop) in zip(pieces, ranges)]
        return jnp.concatenate(parts + padding, axis=0)

    def scores_of(g):
        query = jnp.concatenate(
            [ref[:, columns(g * GROUP + j)] for ref in (tq, sq) for j in range(GROUP)], axis=0
        )
        query = jnp.concatenate([query, q_aug], axis=1)
        return dot_t(query, jnp.concatenate([stacked(2 * g), k_aug_ref[...]], axis=1))

    def absorb_head(g, scores):
        top = jnp.broadcast_to(jnp.max(scores, axis=1, keepdims=True), (2 * half, HEAD_SIZE))
        if not first_call:
            old_top = top_in[g]
            top = jnp.maximum(old_top, top)
        shifted = scores - jnp.concatenate([top] * (total // HEAD_SIZE), axis=1)
        weights = jnp.exp2(shifted * SCALE).astype(jnp.bfloat16)
        both = dot(weights, jnp.concatenate([stacked(2 * g + 1), ones], axis=1))
        summed, denominator = both[:, :HEAD_SIZE], both[:, HEAD_SIZE:]
        if not first_call:
            rescale = jnp.exp2((old_top - top) * SCALE)
            summed = summed + sum_in[g] * rescale
            denominator = denominator + denominator_in[g] * rescale
        if last_call:
            inverse = pl.reciprocal(denominator, approx=True)
            inverse = inverse * (2.0 - denominator * inverse)
            result = (summed * inverse).astype(jnp.bfloat16)
            for j in range(GROUP):
                outs[0][:, columns(g * GROUP + j)] = result[j * rows:(j + 1) * rows]
                outs[1][:, columns(g * GROUP + j)] = result[half + j * rows:half + (j + 1) * rows]
        else:
            for out, state in zip(outs, (top, denominator, summed)):
                out[g] = state

    ahead = scores_of(0)
    for g in range(KEY_VALUE_HEADS):
        now, ahead = ahead, scores_of(g + 1) if g + 1 < KEY_VALUE_HEADS else None
        absorb_head(g, now)


def attend(spans, tq, sq, pieces, slots, tp_size, carry, last_call):
    first_call = carry is None
    rows = tq.shape[0]
    vmem = pl.BlockSpec(memory_space=pltpu.VMEM)
    operands = [spans, tq, sq, *(piece for piece, _, _ in pieces)]
    if not first_call:
        operands += list(carry)
    if last_call:
        out_shape = [jax.ShapeDtypeStruct(tq.shape, jnp.bfloat16)] * 2
    else:
        state = (KEY_VALUE_HEADS, 2 * GROUP * rows, HEAD_SIZE)
        out_shape = [jax.ShapeDtypeStruct(state, jnp.float32)] * 3
    ranges = tuple((first * rows, last * rows) for _, first, last in pieces)
    all_rows = pl.cdiv(sum(stop - start for start, stop in ranges), HEAD_SIZE) * HEAD_SIZE
    flops = 2 * 2 * QUERY_HEADS * rows * all_rows * PAIR * 2
    return pl.pallas_call(
        functools.partial(attend_kernel, slots, ranges, tp_size, first_call, last_call),
        out_shape=out_shape,
        in_specs=[vmem] * len(operands),
        out_specs=[vmem] * len(out_shape),
        scratch_shapes=[pltpu.VMEM((all_rows, HEAD_SIZE), jnp.bfloat16)],
        compiler_params=pltpu.CompilerParams(vmem_limit_bytes=32 * 1024 * 1024),
        cost_estimate=pl.CostEstimate(
            flops=flops, bytes_accessed=all_rows * 4096, transcendentals=2 * QUERY_HEADS * rows * all_rows
        ),
    )(*operands)


def swap(array, axis, bit, size):
    return lax.ppermute(array, axis, [(i, i ^ bit) for i in range(size)])


def after(array, *others):
    return lax.optimization_barrier((array, *others))[0]


def local(ctx_size, tp_size, trace_q, trace_key_value, suffix_q, suffix_key_value, prefix_len, del_start, del_end):
    rows = trace_q.shape[0]
    spans = jnp.broadcast_to(jnp.stack([prefix_len, del_start, del_end]), (3, HEAD_SIZE))
    sq = suffix_q[0]
    suffix_own = suffix_key_value[0]

    core = lambda a: swap(a, "tp", 1, tp_size)
    across_y = lambda a: swap(a, "tp", 2, tp_size)
    across_x = lambda a: swap(a, "ctx", 1, ctx_size)
    along_z = lambda a, flip: swap(a, "ctx", 2 * flip, ctx_size)

    across_both = lambda a: lax.ppermute(
        a,
        ("ctx", "tp"),
        [(i * tp_size + j, (i ^ 1) * tp_size + (j ^ 2)) for i in range(ctx_size) for j in range(tp_size)],
    )

    def slot(place, c):
        if isinstance(place, int):
            return lambda ctx, tp: ("suffix", tp ^ place ^ c)
        z, x, y = place
        return lambda ctx, tp: (
            "trace",
            (ctx ^ (2 * z + x)) * tp_size + (tp ^ (2 * y + c)),
        )

    def slots_of(places, c=0):
        return [slot(place, c) for place in places]

    def absorb(pieces, slots, state, last_call=False):
        return attend(spans, trace_q, sq, pieces, slots, tp_size, state, last_call)

    if ctx_size == 8 and tp_size == 4:
        barrier = lax.optimization_barrier
        next_z, third_z = along_z(trace_key_value, 1), along_z(trace_key_value, 3)
        own_x, own_y = across_x(trace_key_value), across_y(trace_key_value)
        own_d = across_both(trace_key_value)
        next_z, third_z, own_x, own_y, own_d, spans = barrier((next_z, third_z, own_x, own_y, own_d, spans))

        near = jnp.concatenate([next_z, third_z], axis=0)
        far, third_d = along_z(third_z, 1), along_z(own_d, 3)
        near_x, near_y = across_x(near), across_y(near)
        plane = jnp.concatenate([trace_key_value, own_x, own_y, own_d, near, suffix_own], axis=0)
        here = [(0, 0, 0), (0, 1, 0), (0, 0, 1), (0, 1, 1), (1, 0, 0), (3, 0, 0), 0]
        state = absorb([(plane, 0, 7)], slots_of(here), None)

        near_x, near_y, far, third_d, state = barrier((near_x, near_y, far, third_d, state))
        far_y = across_y(jnp.concatenate([far, suffix_own], axis=0))
        far_and_next_d = along_z(jnp.concatenate([third_d, own_d], axis=0), 1)
        far_x = across_x(far)
        sides = jnp.concatenate([plane, near_x, near_y, far, third_d], axis=0)
        sibling = core(sides)
        near_here = [(1, 1, 0), (3, 1, 0), (1, 0, 1), (3, 0, 1), (2, 0, 0), (3, 1, 1)]
        state = absorb([(sides, 7, 13), (sibling, 0, 6)], slots_of(near_here) + slots_of(here[:6], 1), state)

        far_x, far_y, far_and_next_d, state = barrier((far_x, far_y, far_and_next_d, state))
        rest = jnp.concatenate([far_x, far_y, far_and_next_d], axis=0)
        rest_sibling = core(rest)
        rest_here = [(2, 1, 0), (2, 0, 1), 2, (2, 1, 1), (1, 1, 1)]
        state = absorb(
            [(sibling, 6, 13), (rest, 0, 5)], slots_of(here[6:] + near_here, 1) + slots_of(rest_here), state
        )
        trace_out, suffix_out = absorb([(rest_sibling, 0, 5)], slots_of(rest_here, 1), state, True)
    else:
        gathered = lax.all_gather(trace_key_value, ("ctx", "tp"), axis=0, tiled=True)
        suffix_all = lax.all_gather(suffix_own, "tp", axis=0, tiled=True)
        state = None
        for at in range(0, gathered.shape[0], CHUNK_ROWS):
            last_call = at + CHUNK_ROWS >= gathered.shape[0]
            pieces = [(gathered[at:at + CHUNK_ROWS], 0, min(CHUNK_ROWS, gathered.shape[0] - at) // rows)]
            slots = [
                lambda ctx, tp, block=block: ("trace", block)
                for block in range(at // rows, min(at + CHUNK_ROWS, gathered.shape[0]) // rows)
            ]
            if at == 0:
                pieces.append((suffix_all, 0, tp_size))
                slots += [lambda ctx, tp, block=block: ("suffix", block) for block in range(tp_size)]
            state = absorb(pieces, slots, state, last_call)
        trace_out, suffix_out = state
    return trace_out, suffix_out[None]


def solution(mesh):
    return jax.shard_map(
        functools.partial(local, mesh.shape["ctx"], mesh.shape["tp"]),
        mesh=mesh,
        in_specs=(
            P(("ctx", "tp"), None),
            P(("ctx", "tp"), None),
            P("ctx", "tp", None),
            P("ctx", "tp", None),
            P("ctx"),
            P("ctx"),
            P("ctx"),
        ),
        out_specs=(P(("ctx", "tp"), None), P("ctx", "tp", None)),
        check_vma=False,
    )
```

```python
import functools

import jax
import jax.numpy as jnp
from jax import lax
from jax.experimental import pallas as pl
from jax.experimental.pallas import tpu as pltpu
from jax.sharding import PartitionSpec as P

QUERY_HEADS = 40
KEY_VALUE_HEADS = 8
HEAD_SIZE = 128
GROUP = QUERY_HEADS // KEY_VALUE_HEADS
PAIR = 2 * HEAD_SIZE
LOG2E = 1.4426950408889634
SCALE = HEAD_SIZE ** (-0.5) * LOG2E
MASKED = -1e30
CHUNK_ROWS = 1024
COST_FACTOR = 10


def dot_t(a, b):
    return lax.dot_general(a, b, (((1,), (1,)), ((), ())), preferred_element_type=jnp.float32)


def dot(a, b):
    return lax.dot_general(a, b, (((1,), (0,)), ((), ())), preferred_element_type=jnp.float32)


def attend_kernel(slots, ranges, tp_size, first_call, last_call, *refs):
    refs = list(refs)
    spans, tq, sq = refs[:3]
    del refs[:3]
    k_aug_ref = refs.pop()
    outs, refs = (refs[-2:], refs[:-2]) if last_call else (refs[-3:], refs[:-3])
    if not first_call:
        top_in, denominator_in, sum_in = refs[-3:]
        del refs[-3:]
    pieces = refs

    rows = tq.shape[0]
    half = GROUP * rows
    ctx = lax.axis_index("ctx").astype(jnp.int32)
    tp = lax.axis_index("tp").astype(jnp.int32)
    first_position = (ctx * tp_size + tp) * rows
    prefix, del_start, del_end = spans[0:1], spans[1:2], spans[2:3]
    lane = lax.broadcasted_iota(jnp.int32, (rows, HEAD_SIZE), 1)
    row = lax.broadcasted_iota(jnp.int32, (rows, HEAD_SIZE), 0)
    q_trace_aug = jnp.where(lane == row, 1.0, 0.0).astype(jnp.bfloat16)
    q_suffix_aug = jnp.where((lane == rows) | (lane == rows + 1 + row), 1.0, 0.0).astype(jnp.bfloat16)
    q_aug = jnp.concatenate([q_trace_aug] * GROUP + [q_suffix_aug] * GROUP, axis=0)
    for index, slot in enumerate(slots):
        kind, block = slot(ctx, tp)
        position = block * rows + row
        if kind == "trace":
            hidden_trace = (lane < rows) & (position > first_position + lane)
            hidden_suffix = (lane == rows) & (
                (position >= prefix) | ((position >= del_start) & (position < del_end))
            )
            hidden = hidden_trace | hidden_suffix
        else:
            hidden = (lane < rows) | ((lane > rows) & (position > tp * rows + (lane - rows - 1)))
        k_aug_ref[index * rows:(index + 1) * rows, :] = jnp.where(hidden, MASKED, 0.0).astype(jnp.bfloat16)
    filled, total = rows * len(slots), k_aug_ref.shape[0]
    if filled < total:
        k_aug_ref[filled:total, :] = jnp.full((total - filled, HEAD_SIZE), MASKED, jnp.bfloat16)
        padding = [jnp.zeros((total - filled, HEAD_SIZE), jnp.bfloat16)]
    else:
        padding = []
    ones = jnp.ones((total, HEAD_SIZE), jnp.bfloat16)

    def columns(index):
        return slice(index * HEAD_SIZE, (index + 1) * HEAD_SIZE)

    def stacked(index):
        parts = [piece[start:stop, columns(index)] for piece, (start, stop) in zip(pieces, ranges)]
        return jnp.concatenate(parts + padding, axis=0)

    def scores_of(g):
        query = jnp.concatenate(
            [ref[:, columns(g * GROUP + j)] for ref in (tq, sq) for j in range(GROUP)], axis=0
        )
        query = jnp.concatenate([query, q_aug], axis=1)
        return dot_t(query, jnp.concatenate([stacked(2 * g), k_aug_ref[...]], axis=1))

    def absorb_head(g, scores):
        top = jnp.broadcast_to(jnp.max(scores, axis=1, keepdims=True), (2 * half, HEAD_SIZE))
        if not first_call:
            old_top = top_in[g]
            top = jnp.maximum(old_top, top)
        shifted = scores - jnp.concatenate([top] * (total // HEAD_SIZE), axis=1)
        weights = jnp.exp2(shifted * SCALE).astype(jnp.bfloat16)
        both = dot(weights, jnp.concatenate([stacked(2 * g + 1), ones], axis=1))
        summed, denominator = both[:, :HEAD_SIZE], both[:, HEAD_SIZE:]
        if not first_call:
            rescale = jnp.exp2((old_top - top) * SCALE)
            summed = summed + sum_in[g] * rescale
            denominator = denominator + denominator_in[g] * rescale
        if last_call:
            inverse = pl.reciprocal(denominator, approx=True)
            inverse = inverse * (2.0 - denominator * inverse)
            result = (summed * inverse).astype(jnp.bfloat16)
            for j in range(GROUP):
                outs[0][:, columns(g * GROUP + j)] = result[j * rows:(j + 1) * rows]
                outs[1][:, columns(g * GROUP + j)] = result[half + j * rows:half + (j + 1) * rows]
        else:
            for out, state in zip(outs, (top, denominator, summed)):
                out[g] = state

    ahead = scores_of(0)
    for g in range(KEY_VALUE_HEADS):
        now, ahead = ahead, scores_of(g + 1) if g + 1 < KEY_VALUE_HEADS else None
        absorb_head(g, now)


def attend(spans, tq, sq, pieces, slots, tp_size, carry, last_call):
    first_call = carry is None
    rows = tq.shape[0]
    vmem = pl.BlockSpec(memory_space=pltpu.VMEM)
    operands = [spans, tq, sq, *(piece for piece, _, _ in pieces)]
    if not first_call:
        operands += list(carry)
    if last_call:
        out_shape = [jax.ShapeDtypeStruct(tq.shape, jnp.bfloat16)] * 2
    else:
        state = (KEY_VALUE_HEADS, 2 * GROUP * rows, HEAD_SIZE)
        out_shape = [jax.ShapeDtypeStruct(state, jnp.float32)] * 3
    ranges = tuple((first * rows, last * rows) for _, first, last in pieces)
    all_rows = pl.cdiv(sum(stop - start for start, stop in ranges), HEAD_SIZE) * HEAD_SIZE
    flops = 2 * 2 * QUERY_HEADS * rows * all_rows * PAIR * 2
    return pl.pallas_call(
        functools.partial(attend_kernel, slots, ranges, tp_size, first_call, last_call),
        out_shape=out_shape,
        in_specs=[vmem] * len(operands),
        out_specs=[vmem] * len(out_shape),
        scratch_shapes=[pltpu.VMEM((all_rows, HEAD_SIZE), jnp.bfloat16)],
        compiler_params=pltpu.CompilerParams(vmem_limit_bytes=32 * 1024 * 1024),
        cost_estimate=pl.CostEstimate(
            flops=COST_FACTOR * flops, bytes_accessed=all_rows * 4096, transcendentals=2 * QUERY_HEADS * rows * all_rows
        ),
    )(*operands)


def swap(array, axis, bit, size):
    return lax.ppermute(array, axis, [(i, i ^ bit) for i in range(size)])


def after(array, *others):
    return lax.optimization_barrier((array, *others))[0]


def local(ctx_size, tp_size, trace_q, trace_key_value, suffix_q, suffix_key_value, prefix_len, del_start, del_end):
    rows = trace_q.shape[0]
    spans = jnp.broadcast_to(jnp.stack([prefix_len, del_start, del_end]), (3, HEAD_SIZE))
    sq = suffix_q[0]
    suffix_own = suffix_key_value[0]

    core = lambda a: swap(a, "tp", 1, tp_size)
    across_y = lambda a: swap(a, "tp", 2, tp_size)
    across_x = lambda a: swap(a, "ctx", 1, ctx_size)
    along_z = lambda a, flip: swap(a, "ctx", 2 * flip, ctx_size)

    across_both = lambda a: lax.ppermute(
        a,
        ("ctx", "tp"),
        [(i * tp_size + j, (i ^ 1) * tp_size + (j ^ 2)) for i in range(ctx_size) for j in range(tp_size)],
    )

    def slot(place, c):
        if isinstance(place, int):
            return lambda ctx, tp: ("suffix", tp ^ place ^ c)
        z, x, y = place
        return lambda ctx, tp: (
            "trace",
            (ctx ^ (2 * z + x)) * tp_size + (tp ^ (2 * y + c)),
        )

    def slots_of(places, c=0):
        return [slot(place, c) for place in places]

    def absorb(pieces, slots, state, last_call=False):
        return attend(spans, trace_q, sq, pieces, slots, tp_size, state, last_call)

    if ctx_size == 8 and tp_size == 4:
        barrier = lax.optimization_barrier
        next_z, third_z = along_z(trace_key_value, 1), along_z(trace_key_value, 3)
        own_x, own_y = across_x(trace_key_value), across_y(trace_key_value)
        own_d = across_both(trace_key_value)
        next_z, third_z, own_x, own_y, own_d, spans = barrier((next_z, third_z, own_x, own_y, own_d, spans))

        near = jnp.concatenate([next_z, third_z], axis=0)
        far, third_d = along_z(third_z, 1), along_z(own_d, 3)
        near_x, near_y = across_x(near), across_y(near)
        plane = jnp.concatenate([trace_key_value, own_x, own_y, own_d, near, suffix_own], axis=0)
        here = [(0, 0, 0), (0, 1, 0), (0, 0, 1), (0, 1, 1), (1, 0, 0), (3, 0, 0), 0]
        state = absorb([(plane, 0, 7)], slots_of(here), None)
        plane, state = barrier((plane, state))
        plane_sibling = core(plane)

        near_x, near_y, far, third_d, state = barrier((near_x, near_y, far, third_d, state))
        far_y = across_y(jnp.concatenate([far, suffix_own], axis=0))
        far_and_next_d = along_z(jnp.concatenate([third_d, own_d], axis=0), 1)
        far_x = across_x(far)
        sides = jnp.concatenate([near_x, near_y, far, third_d], axis=0)
        near_here = [(1, 1, 0), (3, 1, 0), (1, 0, 1), (3, 0, 1), (2, 0, 0), (3, 1, 1)]
        state = absorb([(sides, 0, 6), (plane_sibling, 0, 6)], slots_of(near_here) + slots_of(here[:6], 1), state)
        sides, state = barrier((sides, state))
        sides_sibling = core(sides)

        far_x, far_y, far_and_next_d, state = barrier((far_x, far_y, far_and_next_d, state))
        rest = jnp.concatenate([far_x, far_y, far_and_next_d], axis=0)
        rest_sibling = core(rest)
        rest_here = [(2, 1, 0), (2, 0, 1), 2, (2, 1, 1), (1, 1, 1)]
        state = absorb(
            [(plane_sibling, 6, 7), (sides_sibling, 0, 6), (rest, 0, 5)],
            slots_of(here[6:] + near_here, 1) + slots_of(rest_here),
            state,
        )
        trace_out, suffix_out = absorb([(rest_sibling, 0, 5)], slots_of(rest_here, 1), state, True)
    else:
        gathered = lax.all_gather(trace_key_value, ("ctx", "tp"), axis=0, tiled=True)
        suffix_all = lax.all_gather(suffix_own, "tp", axis=0, tiled=True)
        state = None
        for at in range(0, gathered.shape[0], CHUNK_ROWS):
            last_call = at + CHUNK_ROWS >= gathered.shape[0]
            pieces = [(gathered[at:at + CHUNK_ROWS], 0, min(CHUNK_ROWS, gathered.shape[0] - at) // rows)]
            slots = [
                lambda ctx, tp, block=block: ("trace", block)
                for block in range(at // rows, min(at + CHUNK_ROWS, gathered.shape[0]) // rows)
            ]
            if at == 0:
                pieces.append((suffix_all, 0, tp_size))
                slots += [lambda ctx, tp, block=block: ("suffix", block) for block in range(tp_size)]
            state = absorb(pieces, slots, state, last_call)
        trace_out, suffix_out = state
    return trace_out, suffix_out[None]


def solution(mesh):
    return jax.shard_map(
        functools.partial(local, mesh.shape["ctx"], mesh.shape["tp"]),
        mesh=mesh,
        in_specs=(
            P(("ctx", "tp"), None),
            P(("ctx", "tp"), None),
            P("ctx", "tp", None),
            P("ctx", "tp", None),
            P("ctx"),
            P("ctx"),
            P("ctx"),
        ),
        out_specs=(P(("ctx", "tp"), None), P("ctx", "tp", None)),
        check_vma=False,
    )
```

```python
import functools

import jax
import jax.numpy as jnp
from jax import lax
from jax.experimental import pallas as pl
from jax.experimental.pallas import tpu as pltpu
from jax.sharding import PartitionSpec as P

QUERY_HEADS = 40
KEY_VALUE_HEADS = 8
HEAD_SIZE = 128
GROUP = QUERY_HEADS // KEY_VALUE_HEADS
PAIR = 2 * HEAD_SIZE
LOG2E = 1.4426950408889634
SCALE = HEAD_SIZE ** (-0.5) * LOG2E
MASKED = -1e30
CHUNK_ROWS = 1024
COST_FACTOR = 10


def dot_t(a, b):
    return lax.dot_general(a, b, (((1,), (1,)), ((), ())), preferred_element_type=jnp.float32)


def dot(a, b):
    return lax.dot_general(a, b, (((1,), (0,)), ((), ())), preferred_element_type=jnp.float32)


def attend_kernel(slots, ranges, tp_size, first_call, last_call, *refs):
    refs = list(refs)
    spans, tq, sq = refs[:3]
    del refs[:3]
    k_aug_ref = refs.pop()
    outs, refs = (refs[-2:], refs[:-2]) if last_call else (refs[-3:], refs[:-3])
    if not first_call:
        top_in, denominator_in, sum_in = refs[-3:]
        del refs[-3:]
    pieces = refs

    rows = tq.shape[0]
    half = GROUP * rows
    ctx = lax.axis_index("ctx").astype(jnp.int32)
    tp = lax.axis_index("tp").astype(jnp.int32)
    first_position = (ctx * tp_size + tp) * rows
    prefix, del_start, del_end = spans[0:1], spans[1:2], spans[2:3]
    lane = lax.broadcasted_iota(jnp.int32, (rows, HEAD_SIZE), 1)
    row = lax.broadcasted_iota(jnp.int32, (rows, HEAD_SIZE), 0)
    q_trace_aug = jnp.where(lane == row, 1.0, 0.0).astype(jnp.bfloat16)
    q_suffix_aug = jnp.where((lane == rows) | (lane == rows + 1 + row), 1.0, 0.0).astype(jnp.bfloat16)
    q_aug = jnp.concatenate([q_trace_aug] * GROUP + [q_suffix_aug] * GROUP, axis=0)
    for index, slot in enumerate(slots):
        kind, block = slot(ctx, tp)
        position = block * rows + row
        if kind == "trace":
            hidden_trace = (lane < rows) & (position > first_position + lane)
            hidden_suffix = (lane == rows) & (
                (position >= prefix) | ((position >= del_start) & (position < del_end))
            )
            hidden = hidden_trace | hidden_suffix
        else:
            hidden = (lane < rows) | ((lane > rows) & (position > tp * rows + (lane - rows - 1)))
        k_aug_ref[index * rows:(index + 1) * rows, :] = jnp.where(hidden, MASKED, 0.0).astype(jnp.bfloat16)
    filled, total = rows * len(slots), k_aug_ref.shape[0]
    if filled < total:
        k_aug_ref[filled:total, :] = jnp.full((total - filled, HEAD_SIZE), MASKED, jnp.bfloat16)
        padding = [jnp.zeros((total - filled, HEAD_SIZE), jnp.bfloat16)]
    else:
        padding = []
    ones = jnp.ones((total, HEAD_SIZE), jnp.bfloat16)

    def columns(index):
        return slice(index * HEAD_SIZE, (index + 1) * HEAD_SIZE)

    def stacked(index):
        parts = [piece[start:stop, columns(index)] for piece, (start, stop) in zip(pieces, ranges)]
        return jnp.concatenate(parts + padding, axis=0)

    def scores_of(g):
        query = jnp.concatenate(
            [ref[:, columns(g * GROUP + j)] for ref in (tq, sq) for j in range(GROUP)], axis=0
        )
        query = jnp.concatenate([query, q_aug], axis=1)
        return dot_t(query, jnp.concatenate([stacked(2 * g), k_aug_ref[...]], axis=1))

    def absorb_head(g, scores):
        top = jnp.broadcast_to(jnp.max(scores, axis=1, keepdims=True), (2 * half, HEAD_SIZE))
        if not first_call:
            old_top = top_in[g]
            top = jnp.maximum(old_top, top)
        shifted = scores - jnp.concatenate([top] * (total // HEAD_SIZE), axis=1)
        weights = jnp.exp2(shifted * SCALE).astype(jnp.bfloat16)
        both = dot(weights, jnp.concatenate([stacked(2 * g + 1), ones], axis=1))
        summed, denominator = both[:, :HEAD_SIZE], both[:, HEAD_SIZE:]
        if not first_call:
            rescale = jnp.exp2((old_top - top) * SCALE)
            summed = summed + sum_in[g] * rescale
            denominator = denominator + denominator_in[g] * rescale
        if last_call:
            inverse = pl.reciprocal(denominator, approx=True)
            inverse = inverse * (2.0 - denominator * inverse)
            result = (summed * inverse).astype(jnp.bfloat16)
            for j in range(GROUP):
                outs[0][:, columns(g * GROUP + j)] = result[j * rows:(j + 1) * rows]
                outs[1][:, columns(g * GROUP + j)] = result[half + j * rows:half + (j + 1) * rows]
        else:
            for out, state in zip(outs, (top, denominator, summed)):
                out[g] = state

    ahead = scores_of(0)
    for g in range(KEY_VALUE_HEADS):
        now, ahead = ahead, scores_of(g + 1) if g + 1 < KEY_VALUE_HEADS else None
        absorb_head(g, now)


def attend(spans, tq, sq, pieces, slots, tp_size, carry, last_call):
    first_call = carry is None
    rows = tq.shape[0]
    vmem = pl.BlockSpec(memory_space=pltpu.VMEM)
    operands = [spans, tq, sq, *(piece for piece, _, _ in pieces)]
    if not first_call:
        operands += list(carry)
    if last_call:
        out_shape = [jax.ShapeDtypeStruct(tq.shape, jnp.bfloat16)] * 2
    else:
        state = (KEY_VALUE_HEADS, 2 * GROUP * rows, HEAD_SIZE)
        out_shape = [jax.ShapeDtypeStruct(state, jnp.float32)] * 3
    ranges = tuple((first * rows, last * rows) for _, first, last in pieces)
    all_rows = pl.cdiv(sum(stop - start for start, stop in ranges), HEAD_SIZE) * HEAD_SIZE
    flops = 2 * 2 * QUERY_HEADS * rows * all_rows * PAIR * 2
    return pl.pallas_call(
        functools.partial(attend_kernel, slots, ranges, tp_size, first_call, last_call),
        out_shape=out_shape,
        in_specs=[vmem] * len(operands),
        out_specs=[vmem] * len(out_shape),
        scratch_shapes=[pltpu.VMEM((all_rows, HEAD_SIZE), jnp.bfloat16)],
        compiler_params=pltpu.CompilerParams(vmem_limit_bytes=32 * 1024 * 1024),
        cost_estimate=pl.CostEstimate(
            flops=COST_FACTOR * flops, bytes_accessed=all_rows * 4096, transcendentals=2 * QUERY_HEADS * rows * all_rows
        ),
    )(*operands)


def swap(array, axis, bit, size):
    return lax.ppermute(array, axis, [(i, i ^ bit) for i in range(size)])


def after(array, *others):
    return lax.optimization_barrier((array, *others))[0]


def local(ctx_size, tp_size, trace_q, trace_key_value, suffix_q, suffix_key_value, prefix_len, del_start, del_end):
    rows = trace_q.shape[0]
    spans = jnp.broadcast_to(jnp.stack([prefix_len, del_start, del_end]), (3, HEAD_SIZE))
    sq = suffix_q[0]
    suffix_own = suffix_key_value[0]

    core = lambda a: swap(a, "tp", 1, tp_size)
    across_y = lambda a: swap(a, "tp", 2, tp_size)
    across_x = lambda a: swap(a, "ctx", 1, ctx_size)
    along_z = lambda a, flip: swap(a, "ctx", 2 * flip, ctx_size)

    across_both = lambda a: lax.ppermute(
        a,
        ("ctx", "tp"),
        [(i * tp_size + j, (i ^ 1) * tp_size + (j ^ 2)) for i in range(ctx_size) for j in range(tp_size)],
    )

    def slot(place, c):
        if isinstance(place, int):
            return lambda ctx, tp: ("suffix", tp ^ place ^ c)
        z, x, y = place
        return lambda ctx, tp: (
            "trace",
            (ctx ^ (2 * z + x)) * tp_size + (tp ^ (2 * y + c)),
        )

    def slots_of(places, c=0):
        return [slot(place, c) for place in places]

    def absorb(pieces, slots, state, last_call=False):
        return attend(spans, trace_q, sq, pieces, slots, tp_size, state, last_call)

    if ctx_size == 8 and tp_size == 4:
        barrier = lax.optimization_barrier
        next_z, third_z = along_z(trace_key_value, 1), along_z(trace_key_value, 3)
        own_x, own_y = across_x(trace_key_value), across_y(trace_key_value)
        own_d = across_both(trace_key_value)
        next_z, third_z, own_x, own_y, own_d, spans = barrier((next_z, third_z, own_x, own_y, own_d, spans))

        near = jnp.concatenate([next_z, third_z], axis=0)
        far, third_d = along_z(third_z, 1), along_z(own_d, 3)
        near_x, near_y = across_x(near), across_y(near)
        plane = jnp.concatenate([trace_key_value, own_x, own_y, own_d, near, suffix_own], axis=0)
        here = [(0, 0, 0), (0, 1, 0), (0, 0, 1), (0, 1, 1), (1, 0, 0), (3, 0, 0), 0]
        state = absorb([(plane, 0, 7)], slots_of(here), None)
        plane, state = barrier((plane, state))
        plane_sibling = core(plane)

        near_x, near_y, far, third_d, state = barrier((near_x, near_y, far, third_d, state))
        far_y = across_y(jnp.concatenate([far, suffix_own], axis=0))
        far_x = across_x(jnp.concatenate([far, near_y[:rows]], axis=0))
        far_d = along_z(third_d, 1)
        sides = jnp.concatenate([near_x, near_y, far, third_d], axis=0)
        near_here = [(1, 1, 0), (3, 1, 0), (1, 0, 1), (3, 0, 1), (2, 0, 0), (3, 1, 1)]
        state = absorb([(sides, 0, 6), (plane_sibling, 0, 6)], slots_of(near_here) + slots_of(here[:6], 1), state)
        sides, state = barrier((sides, state))
        sides_sibling = core(sides)

        far_x, far_y, far_d, state = barrier((far_x, far_y, far_d, state))
        rest = jnp.concatenate([far_x, far_y, far_d], axis=0)
        rest_sibling = core(rest)
        rest_here = [(2, 1, 0), (1, 1, 1), (2, 0, 1), 2, (2, 1, 1)]
        state = absorb(
            [(plane_sibling, 6, 7), (sides_sibling, 0, 6), (rest, 0, 5)],
            slots_of(here[6:] + near_here, 1) + slots_of(rest_here),
            state,
        )
        trace_out, suffix_out = absorb([(rest_sibling, 0, 5)], slots_of(rest_here, 1), state, True)
    else:
        gathered = lax.all_gather(trace_key_value, ("ctx", "tp"), axis=0, tiled=True)
        suffix_all = lax.all_gather(suffix_own, "tp", axis=0, tiled=True)
        state = None
        for at in range(0, gathered.shape[0], CHUNK_ROWS):
            last_call = at + CHUNK_ROWS >= gathered.shape[0]
            pieces = [(gathered[at:at + CHUNK_ROWS], 0, min(CHUNK_ROWS, gathered.shape[0] - at) // rows)]
            slots = [
                lambda ctx, tp, block=block: ("trace", block)
                for block in range(at // rows, min(at + CHUNK_ROWS, gathered.shape[0]) // rows)
            ]
            if at == 0:
                pieces.append((suffix_all, 0, tp_size))
                slots += [lambda ctx, tp, block=block: ("suffix", block) for block in range(tp_size)]
            state = absorb(pieces, slots, state, last_call)
        trace_out, suffix_out = state
    return trace_out, suffix_out[None]


def solution(mesh):
    return jax.shard_map(
        functools.partial(local, mesh.shape["ctx"], mesh.shape["tp"]),
        mesh=mesh,
        in_specs=(
            P(("ctx", "tp"), None),
            P(("ctx", "tp"), None),
            P("ctx", "tp", None),
            P("ctx", "tp", None),
            P("ctx"),
            P("ctx"),
            P("ctx"),
        ),
        out_specs=(P(("ctx", "tp"), None), P("ctx", "tp", None)),
        check_vma=False,
    )
```

```python
import functools

import jax
import jax.numpy as jnp
from jax import lax
from jax.experimental import pallas as pl
from jax.experimental.pallas import tpu as pltpu
from jax.sharding import PartitionSpec as P

QUERY_HEADS = 40
KEY_VALUE_HEADS = 8
HEAD_SIZE = 128
GROUP = QUERY_HEADS // KEY_VALUE_HEADS
PAIR = 2 * HEAD_SIZE
LOG2E = 1.4426950408889634
SCALE = HEAD_SIZE ** (-0.5) * LOG2E
MASKED = -1e30
CHUNK_ROWS = 1024
COST_FACTOR = 10


def dot_t(a, b):
    return lax.dot_general(a, b, (((1,), (1,)), ((), ())), preferred_element_type=jnp.float32)


def dot(a, b):
    return lax.dot_general(a, b, (((1,), (0,)), ((), ())), preferred_element_type=jnp.float32)


def attend_kernel(slots, ranges, tp_size, first_call, last_call, *refs):
    refs = list(refs)
    spans, tq, sq = refs[:3]
    del refs[:3]
    if last_call:
        stage, sems = refs[-2:]
        del refs[-2:]
    k_aug_ref = refs.pop()
    outs, refs = (refs[-2:], refs[:-2]) if last_call else (refs[-3:], refs[:-3])
    if not first_call:
        top_in, denominator_in, sum_in = refs[-3:]
        del refs[-3:]
    pieces = refs

    rows = tq.shape[0]
    half = GROUP * rows
    ctx = lax.axis_index("ctx").astype(jnp.int32)
    tp = lax.axis_index("tp").astype(jnp.int32)
    first_position = (ctx * tp_size + tp) * rows
    prefix, del_start, del_end = spans[0:1], spans[1:2], spans[2:3]
    lane = lax.broadcasted_iota(jnp.int32, (rows, HEAD_SIZE), 1)
    row = lax.broadcasted_iota(jnp.int32, (rows, HEAD_SIZE), 0)
    q_trace_aug = jnp.where(lane == row, 1.0, 0.0).astype(jnp.bfloat16)
    q_suffix_aug = jnp.where((lane == rows) | (lane == rows + 1 + row), 1.0, 0.0).astype(jnp.bfloat16)
    q_aug = jnp.concatenate([q_trace_aug] * GROUP + [q_suffix_aug] * GROUP, axis=0)
    for index, slot in enumerate(slots):
        kind, block = slot(ctx, tp)
        position = block * rows + row
        if kind == "trace":
            hidden_trace = (lane < rows) & (position > first_position + lane)
            hidden_suffix = (lane == rows) & (
                (position >= prefix) | ((position >= del_start) & (position < del_end))
            )
            hidden = hidden_trace | hidden_suffix
        else:
            hidden = (lane < rows) | ((lane > rows) & (position > tp * rows + (lane - rows - 1)))
        k_aug_ref[index * rows:(index + 1) * rows, :] = jnp.where(hidden, MASKED, 0.0).astype(jnp.bfloat16)
    filled, total = rows * len(slots), k_aug_ref.shape[0]
    if filled < total:
        k_aug_ref[filled:total, :] = jnp.full((total - filled, HEAD_SIZE), MASKED, jnp.bfloat16)
        padding = [jnp.zeros((total - filled, HEAD_SIZE), jnp.bfloat16)]
    else:
        padding = []
    ones = jnp.ones((total, HEAD_SIZE), jnp.bfloat16)

    def columns(index):
        return slice(index * HEAD_SIZE, (index + 1) * HEAD_SIZE)

    def stacked(index):
        parts = [piece[start:stop, columns(index)] for piece, (start, stop) in zip(pieces, ranges)]
        return jnp.concatenate(parts + padding, axis=0)

    def scores_of(g):
        query = jnp.concatenate(
            [ref[:, columns(g * GROUP + j)] for ref in (tq, sq) for j in range(GROUP)], axis=0
        )
        query = jnp.concatenate([query, q_aug], axis=1)
        return dot_t(query, jnp.concatenate([stacked(2 * g), k_aug_ref[...]], axis=1))

    def absorb_head(g, scores):
        top = jnp.broadcast_to(jnp.max(scores, axis=1, keepdims=True), (2 * half, HEAD_SIZE))
        if not first_call:
            old_top = top_in[g]
            top = jnp.maximum(old_top, top)
        shifted = scores - jnp.concatenate([top] * (total // HEAD_SIZE), axis=1)
        weights = jnp.exp2(shifted * SCALE).astype(jnp.bfloat16)
        both = dot(weights, jnp.concatenate([stacked(2 * g + 1), ones], axis=1))
        summed, denominator = both[:, :HEAD_SIZE], both[:, HEAD_SIZE:]
        if not first_call:
            rescale = jnp.exp2((old_top - top) * SCALE)
            summed = summed + sum_in[g] * rescale
            denominator = denominator + denominator_in[g] * rescale
        if last_call:
            inverse = pl.reciprocal(denominator, approx=True)
            inverse = inverse * (2.0 - denominator * inverse)
            result = (summed * inverse).astype(jnp.bfloat16)
            for side in range(2):
                for j in range(GROUP):
                    start = (side * GROUP + j) * rows
                    stage[side, :, columns(g * GROUP + j)] = result[start:start + rows]
                output_copy(side, g).start()
        else:
            for out, state in zip(outs, (top, denominator, summed)):
                out[g] = state

    def output_copy(side, g):
        group = pl.ds(g * GROUP * HEAD_SIZE, GROUP * HEAD_SIZE)
        return pltpu.make_async_copy(stage.at[side, :, group], outs[side].at[:, group], sems.at[side, g])

    ahead = scores_of(0)
    for g in range(KEY_VALUE_HEADS):
        now, ahead = ahead, scores_of(g + 1) if g + 1 < KEY_VALUE_HEADS else None
        absorb_head(g, now)
    if last_call:
        for g in range(KEY_VALUE_HEADS):
            for side in range(2):
                output_copy(side, g).wait()


def attend(spans, tq, sq, pieces, slots, tp_size, carry, last_call):
    first_call = carry is None
    rows = tq.shape[0]
    vmem = pl.BlockSpec(memory_space=pltpu.VMEM)
    operands = [spans, tq, sq, *(piece for piece, _, _ in pieces)]
    if not first_call:
        operands += list(carry)
    if last_call:
        out_shape = [jax.ShapeDtypeStruct(tq.shape, jnp.bfloat16)] * 2
        out_specs = [pl.BlockSpec(memory_space=pl.ANY)] * 2
        scratch = [pltpu.VMEM((2, *tq.shape), jnp.bfloat16), pltpu.SemaphoreType.DMA((2, KEY_VALUE_HEADS))]
    else:
        state = (KEY_VALUE_HEADS, 2 * GROUP * rows, HEAD_SIZE)
        out_shape = [jax.ShapeDtypeStruct(state, jnp.float32)] * 3
        out_specs = [vmem] * 3
        scratch = []
    ranges = tuple((first * rows, last * rows) for _, first, last in pieces)
    all_rows = pl.cdiv(sum(stop - start for start, stop in ranges), HEAD_SIZE) * HEAD_SIZE
    flops = 2 * 2 * QUERY_HEADS * rows * all_rows * PAIR * 2
    return pl.pallas_call(
        functools.partial(attend_kernel, slots, ranges, tp_size, first_call, last_call),
        out_shape=out_shape,
        in_specs=[vmem] * len(operands),
        out_specs=out_specs,
        scratch_shapes=[pltpu.VMEM((all_rows, HEAD_SIZE), jnp.bfloat16), *scratch],
        compiler_params=pltpu.CompilerParams(vmem_limit_bytes=32 * 1024 * 1024),
        cost_estimate=pl.CostEstimate(
            flops=COST_FACTOR * flops, bytes_accessed=all_rows * 4096, transcendentals=2 * QUERY_HEADS * rows * all_rows
        ),
    )(*operands)


def swap(array, axis, bit, size):
    return lax.ppermute(array, axis, [(i, i ^ bit) for i in range(size)])


def after(array, *others):
    return lax.optimization_barrier((array, *others))[0]


def local(ctx_size, tp_size, trace_q, trace_key_value, suffix_q, suffix_key_value, prefix_len, del_start, del_end):
    rows = trace_q.shape[0]
    spans = jnp.broadcast_to(jnp.stack([prefix_len, del_start, del_end]), (3, HEAD_SIZE))
    sq = suffix_q[0]
    suffix_own = suffix_key_value[0]

    core = lambda a: swap(a, "tp", 1, tp_size)
    across_y = lambda a: swap(a, "tp", 2, tp_size)
    across_x = lambda a: swap(a, "ctx", 1, ctx_size)
    along_z = lambda a, flip: swap(a, "ctx", 2 * flip, ctx_size)

    across_both = lambda a: lax.ppermute(
        a,
        ("ctx", "tp"),
        [(i * tp_size + j, (i ^ 1) * tp_size + (j ^ 2)) for i in range(ctx_size) for j in range(tp_size)],
    )

    def slot(place, c):
        if isinstance(place, int):
            return lambda ctx, tp: ("suffix", tp ^ place ^ c)
        z, x, y = place
        return lambda ctx, tp: (
            "trace",
            (ctx ^ (2 * z + x)) * tp_size + (tp ^ (2 * y + c)),
        )

    def slots_of(places, c=0):
        return [slot(place, c) for place in places]

    def absorb(pieces, slots, state, last_call=False):
        return attend(spans, trace_q, sq, pieces, slots, tp_size, state, last_call)

    if ctx_size == 8 and tp_size == 4:
        barrier = lax.optimization_barrier
        next_z, third_z = along_z(trace_key_value, 1), along_z(trace_key_value, 3)
        own_x, own_y = across_x(trace_key_value), across_y(trace_key_value)
        own_d = across_both(trace_key_value)
        own_d, third_z, next_z, own_y, own_x, spans = barrier((own_d, third_z, next_z, own_y, own_x, spans))

        near = jnp.concatenate([next_z, third_z], axis=0)
        far, third_d = along_z(third_z, 1), along_z(own_d, 3)
        near_x, near_y = across_x(near), across_y(near)
        plane = jnp.concatenate([trace_key_value, own_x, own_y, own_d, near, suffix_own], axis=0)
        here = [(0, 0, 0), (0, 1, 0), (0, 0, 1), (0, 1, 1), (1, 0, 0), (3, 0, 0), 0]
        state = absorb([(plane, 0, 7)], slots_of(here), None)
        plane, state = barrier((plane, state))
        plane_sibling = core(plane)

        near_x, near_y, far, third_d, state = barrier((near_x, near_y, far, third_d, state))
        far_y = across_y(jnp.concatenate([far, suffix_own], axis=0))
        far_x = across_x(jnp.concatenate([far, near_y[:rows]], axis=0))
        far_d = along_z(third_d, 1)
        sides = jnp.concatenate([near_x, near_y, far, third_d], axis=0)
        near_here = [(1, 1, 0), (3, 1, 0), (1, 0, 1), (3, 0, 1), (2, 0, 0), (3, 1, 1)]
        state = absorb([(sides, 0, 6), (plane_sibling, 0, 6)], slots_of(near_here) + slots_of(here[:6], 1), state)
        sides, state = barrier((sides, state))
        sides_sibling = core(sides)

        far_x, far_y, far_d, state = barrier((far_x, far_y, far_d, state))
        rest = jnp.concatenate([far_x, far_y, far_d], axis=0)
        rest_sibling = core(rest)
        rest_here = [(2, 1, 0), (1, 1, 1), (2, 0, 1), 2, (2, 1, 1)]
        state = absorb(
            [(plane_sibling, 6, 7), (sides_sibling, 0, 6), (rest, 0, 5)],
            slots_of(here[6:] + near_here, 1) + slots_of(rest_here),
            state,
        )
        trace_out, suffix_out = absorb([(rest_sibling, 0, 5)], slots_of(rest_here, 1), state, True)
    else:
        gathered = lax.all_gather(trace_key_value, ("ctx", "tp"), axis=0, tiled=True)
        suffix_all = lax.all_gather(suffix_own, "tp", axis=0, tiled=True)
        state = None
        for at in range(0, gathered.shape[0], CHUNK_ROWS):
            last_call = at + CHUNK_ROWS >= gathered.shape[0]
            pieces = [(gathered[at:at + CHUNK_ROWS], 0, min(CHUNK_ROWS, gathered.shape[0] - at) // rows)]
            slots = [
                lambda ctx, tp, block=block: ("trace", block)
                for block in range(at // rows, min(at + CHUNK_ROWS, gathered.shape[0]) // rows)
            ]
            if at == 0:
                pieces.append((suffix_all, 0, tp_size))
                slots += [lambda ctx, tp, block=block: ("suffix", block) for block in range(tp_size)]
            state = absorb(pieces, slots, state, last_call)
        trace_out, suffix_out = state
    return trace_out, suffix_out[None]


def solution(mesh):
    return jax.shard_map(
        functools.partial(local, mesh.shape["ctx"], mesh.shape["tp"]),
        mesh=mesh,
        in_specs=(
            P(("ctx", "tp"), None),
            P(("ctx", "tp"), None),
            P("ctx", "tp", None),
            P("ctx", "tp", None),
            P("ctx"),
            P("ctx"),
            P("ctx"),
        ),
        out_specs=(P(("ctx", "tp"), None), P("ctx", "tp", None)),
        check_vma=False,
    )
```

```python
import functools

import jax
import jax.numpy as jnp
from jax import lax
from jax.experimental import pallas as pl
from jax.experimental.pallas import tpu as pltpu
from jax.sharding import PartitionSpec as P

QUERY_HEADS = 40
KEY_VALUE_HEADS = 8
HEAD_SIZE = 128
GROUP = QUERY_HEADS // KEY_VALUE_HEADS
PAIR = 2 * HEAD_SIZE
LOG2E = 1.4426950408889634
SCALE = HEAD_SIZE ** (-0.5) * LOG2E
MASKED = -1e30
CHUNK_ROWS = 1024
COST_FACTOR = 10


def dot_t(a, b):
    return lax.dot_general(a, b, (((1,), (1,)), ((), ())), preferred_element_type=jnp.float32)


def dot(a, b):
    return lax.dot_general(a, b, (((1,), (0,)), ((), ())), preferred_element_type=jnp.float32)


def attend_kernel(slots, ranges, tp_size, first_call, last_call, *refs):
    refs = list(refs)
    spans, tq, sq = refs[:3]
    del refs[:3]
    if last_call:
        stage, sems = refs[-2:]
        del refs[-2:]
    k_aug_ref = refs.pop()
    outs, refs = (refs[-2:], refs[:-2]) if last_call else (refs[-3:], refs[:-3])
    if not first_call:
        top_in, denominator_in, sum_in = refs[-3:]
        del refs[-3:]
    pieces = refs

    rows = tq.shape[0]
    half = GROUP * rows
    ctx = lax.axis_index("ctx").astype(jnp.int32)
    tp = lax.axis_index("tp").astype(jnp.int32)
    first_position = (ctx * tp_size + tp) * rows
    prefix, del_start, del_end = spans[0:1], spans[1:2], spans[2:3]
    lane = lax.broadcasted_iota(jnp.int32, (rows, HEAD_SIZE), 1)
    row = lax.broadcasted_iota(jnp.int32, (rows, HEAD_SIZE), 0)
    q_trace_aug = jnp.where(lane == row, 1.0, 0.0).astype(jnp.bfloat16)
    q_suffix_aug = jnp.where((lane == rows) | (lane == rows + 1 + row), 1.0, 0.0).astype(jnp.bfloat16)
    q_aug = jnp.concatenate([q_trace_aug] * GROUP + [q_suffix_aug] * GROUP, axis=0)
    for index, slot in enumerate(slots):
        kind, block = slot(ctx, tp)
        position = block * rows + row
        if kind == "trace":
            hidden_trace = (lane < rows) & (position > first_position + lane)
            hidden_suffix = (lane == rows) & (
                (position >= prefix) | ((position >= del_start) & (position < del_end))
            )
            hidden = hidden_trace | hidden_suffix
        else:
            hidden = (lane < rows) | ((lane > rows) & (position > tp * rows + (lane - rows - 1)))
        k_aug_ref[index * rows:(index + 1) * rows, :] = jnp.where(hidden, MASKED, 0.0).astype(jnp.bfloat16)
    filled, total = rows * len(slots), k_aug_ref.shape[0]
    if filled < total:
        k_aug_ref[filled:total, :] = jnp.full((total - filled, HEAD_SIZE), MASKED, jnp.bfloat16)
        padding = [jnp.zeros((total - filled, HEAD_SIZE), jnp.bfloat16)]
    else:
        padding = []
    ones = jnp.ones((total, HEAD_SIZE), jnp.bfloat16)

    def columns(index):
        return slice(index * HEAD_SIZE, (index + 1) * HEAD_SIZE)

    def stacked(index):
        parts = [piece[start:stop, columns(index)] for piece, (start, stop) in zip(pieces, ranges)]
        return jnp.concatenate(parts + padding, axis=0)

    def scores_of(g):
        query = jnp.concatenate(
            [ref[:, columns(g * GROUP + j)] for ref in (tq, sq) for j in range(GROUP)], axis=0
        )
        query = jnp.concatenate([query, q_aug], axis=1)
        return dot_t(query, jnp.concatenate([stacked(2 * g), k_aug_ref[...]], axis=1))

    def absorb_head(g, scores):
        top = jnp.broadcast_to(jnp.max(scores, axis=1, keepdims=True), (2 * half, HEAD_SIZE))
        if not first_call:
            old_top = top_in[g]
            top = jnp.maximum(old_top, top)
        shifted = scores - jnp.concatenate([top] * (total // HEAD_SIZE), axis=1)
        weights = jnp.exp2(shifted * SCALE).astype(jnp.bfloat16)
        both = dot(weights, jnp.concatenate([stacked(2 * g + 1), ones], axis=1))
        summed, denominator = both[:, :HEAD_SIZE], both[:, HEAD_SIZE:]
        if not first_call:
            rescale = jnp.exp2((old_top - top) * SCALE)
            summed = summed + sum_in[g] * rescale
            denominator = denominator + denominator_in[g] * rescale
        if last_call:
            inverse = pl.reciprocal(denominator, approx=True)
            inverse = inverse * (2.0 - denominator * inverse)
            result = (summed * inverse).astype(jnp.bfloat16)
            for side in range(2):
                for j in range(GROUP):
                    start = (side * GROUP + j) * rows
                    stage[side, :, columns(g * GROUP + j)] = result[start:start + rows]
                output_copy(side, g).start()
        else:
            for out, state in zip(outs, (top, denominator, summed)):
                out[g] = state

    def output_copy(side, g):
        group = pl.ds(g * GROUP * HEAD_SIZE, GROUP * HEAD_SIZE)
        return pltpu.make_async_copy(stage.at[side, :, group], outs[side].at[:, group], sems.at[side, g])

    ahead = scores_of(0)
    for g in range(KEY_VALUE_HEADS):
        now, ahead = ahead, scores_of(g + 1) if g + 1 < KEY_VALUE_HEADS else None
        absorb_head(g, now)
    if last_call:
        for g in range(KEY_VALUE_HEADS):
            for side in range(2):
                output_copy(side, g).wait()


def attend(spans, tq, sq, pieces, slots, tp_size, carry, last_call):
    first_call = carry is None
    rows = tq.shape[0]
    vmem = pl.BlockSpec(memory_space=pltpu.VMEM)
    operands = [spans, tq, sq, *(piece for piece, _, _ in pieces)]
    if not first_call:
        operands += list(carry)
    if last_call:
        out_shape = [jax.ShapeDtypeStruct(tq.shape, jnp.bfloat16)] * 2
        out_specs = [pl.BlockSpec(memory_space=pl.ANY)] * 2
        scratch = [pltpu.VMEM((2, *tq.shape), jnp.bfloat16), pltpu.SemaphoreType.DMA((2, KEY_VALUE_HEADS))]
    else:
        state = (KEY_VALUE_HEADS, 2 * GROUP * rows, HEAD_SIZE)
        out_shape = [jax.ShapeDtypeStruct(state, jnp.float32)] * 3
        out_specs = [vmem] * 3
        scratch = []
    ranges = tuple((first * rows, last * rows) for _, first, last in pieces)
    all_rows = pl.cdiv(sum(stop - start for start, stop in ranges), HEAD_SIZE) * HEAD_SIZE
    flops = 2 * 2 * QUERY_HEADS * rows * all_rows * PAIR * 2
    return pl.pallas_call(
        functools.partial(attend_kernel, slots, ranges, tp_size, first_call, last_call),
        out_shape=out_shape,
        in_specs=[vmem] * len(operands),
        out_specs=out_specs,
        scratch_shapes=[pltpu.VMEM((all_rows, HEAD_SIZE), jnp.bfloat16), *scratch],
        compiler_params=pltpu.CompilerParams(vmem_limit_bytes=32 * 1024 * 1024),
        cost_estimate=pl.CostEstimate(
            flops=COST_FACTOR * flops, bytes_accessed=all_rows * 4096, transcendentals=2 * QUERY_HEADS * rows * all_rows
        ),
    )(*operands)


def swap(array, axis, bit, size):
    return lax.ppermute(array, axis, [(i, i ^ bit) for i in range(size)])


def after(array, *others):
    return lax.optimization_barrier((array, *others))[0]


def local(ctx_size, tp_size, trace_q, trace_key_value, suffix_q, suffix_key_value, prefix_len, del_start, del_end):
    rows = trace_q.shape[0]
    spans = jnp.broadcast_to(jnp.stack([prefix_len, del_start, del_end]), (3, HEAD_SIZE))
    sq = suffix_q[0]
    suffix_own = suffix_key_value[0]

    core = lambda a: swap(a, "tp", 1, tp_size)
    across_y = lambda a: swap(a, "tp", 2, tp_size)
    across_x = lambda a: swap(a, "ctx", 1, ctx_size)
    along_z = lambda a, flip: swap(a, "ctx", 2 * flip, ctx_size)

    across_both = lambda a: lax.ppermute(
        a,
        ("ctx", "tp"),
        [(i * tp_size + j, (i ^ 1) * tp_size + (j ^ 2)) for i in range(ctx_size) for j in range(tp_size)],
    )

    def slot(place, c):
        if isinstance(place, int):
            return lambda ctx, tp: ("suffix", tp ^ place ^ c)
        z, x, y = place
        return lambda ctx, tp: (
            "trace",
            (ctx ^ (2 * z + x)) * tp_size + (tp ^ (2 * y + c)),
        )

    def slots_of(places, c=0):
        return [slot(place, c) for place in places]

    def absorb(pieces, slots, state, last_call=False):
        return attend(spans, trace_q, sq, pieces, slots, tp_size, state, last_call)

    if ctx_size == 8 and tp_size == 4:
        barrier = lax.optimization_barrier
        next_z, third_z = along_z(trace_key_value, 1), along_z(trace_key_value, 3)
        own_x, own_y = across_x(trace_key_value), across_y(trace_key_value)
        own_d = across_both(trace_key_value)
        own_d, third_z, next_z, own_y, own_x, spans = barrier((own_d, third_z, next_z, own_y, own_x, spans))

        near = jnp.concatenate([next_z, third_z], axis=0)
        far, third_d = along_z(third_z, 1), along_z(own_d, 3)
        near_x, near_y = across_x(near), across_y(near)
        far_x, far_y = across_x(far), across_y(jnp.concatenate([far, suffix_own], axis=0))
        plane = jnp.concatenate([trace_key_value, own_x, own_y, own_d, near, suffix_own], axis=0)
        here = [(0, 0, 0), (0, 1, 0), (0, 0, 1), (0, 1, 1), (1, 0, 0), (3, 0, 0), 0]
        plane, far = barrier((plane, far))
        state = absorb([(plane, 0, 7)], slots_of(here), None)

        near_x, plane, state = barrier((near_x, plane, state))
        plane_sibling = core(plane)
        near_y, state = barrier((near_y, state))
        next_d, far_d = across_x(near_y[:rows]), along_z(third_d, 1)
        sides = jnp.concatenate([near_x, near_y, far, third_d], axis=0)
        near_here = [(1, 1, 0), (3, 1, 0), (1, 0, 1), (3, 0, 1), (2, 0, 0), (3, 1, 1)]
        state = absorb([(sides, 0, 6), (plane_sibling, 0, 6)], slots_of(near_here) + slots_of(here[:6], 1), state)
        sides_sibling = core(sides)

        far_x, next_d, far_y, far_d, state = barrier((far_x, next_d, far_y, far_d, state))
        rest = jnp.concatenate([far_x, next_d, far_y, far_d], axis=0)
        rest_sibling = core(rest)
        rest_here = [(2, 1, 0), (1, 1, 1), (2, 0, 1), 2, (2, 1, 1)]
        state = absorb(
            [(plane_sibling, 6, 7), (sides_sibling, 0, 6), (rest, 0, 5)],
            slots_of(here[6:] + near_here, 1) + slots_of(rest_here),
            state,
        )
        trace_out, suffix_out = absorb([(rest_sibling, 0, 5)], slots_of(rest_here, 1), state, True)
    else:
        gathered = lax.all_gather(trace_key_value, ("ctx", "tp"), axis=0, tiled=True)
        suffix_all = lax.all_gather(suffix_own, "tp", axis=0, tiled=True)
        state = None
        for at in range(0, gathered.shape[0], CHUNK_ROWS):
            last_call = at + CHUNK_ROWS >= gathered.shape[0]
            pieces = [(gathered[at:at + CHUNK_ROWS], 0, min(CHUNK_ROWS, gathered.shape[0] - at) // rows)]
            slots = [
                lambda ctx, tp, block=block: ("trace", block)
                for block in range(at // rows, min(at + CHUNK_ROWS, gathered.shape[0]) // rows)
            ]
            if at == 0:
                pieces.append((suffix_all, 0, tp_size))
                slots += [lambda ctx, tp, block=block: ("suffix", block) for block in range(tp_size)]
            state = absorb(pieces, slots, state, last_call)
        trace_out, suffix_out = state
    return trace_out, suffix_out[None]


def solution(mesh):
    return jax.shard_map(
        functools.partial(local, mesh.shape["ctx"], mesh.shape["tp"]),
        mesh=mesh,
        in_specs=(
            P(("ctx", "tp"), None),
            P(("ctx", "tp"), None),
            P("ctx", "tp", None),
            P("ctx", "tp", None),
            P("ctx"),
            P("ctx"),
            P("ctx"),
        ),
        out_specs=(P(("ctx", "tp"), None), P("ctx", "tp", None)),
        check_vma=False,
    )
```

```python
import functools

import jax
import jax.numpy as jnp
from jax import lax
from jax.experimental import pallas as pl
from jax.experimental.pallas import tpu as pltpu
from jax.sharding import PartitionSpec as P

QUERY_HEADS = 40
KEY_VALUE_HEADS = 8
HEAD_SIZE = 128
GROUP = QUERY_HEADS // KEY_VALUE_HEADS
PAIR = 2 * HEAD_SIZE
LOG2E = 1.4426950408889634
SCALE = HEAD_SIZE ** (-0.5) * LOG2E
MASKED = -1e30
CHUNK_ROWS = 1024
COST_FACTOR = 10


def dot_t(a, b):
    return lax.dot_general(a, b, (((1,), (1,)), ((), ())), preferred_element_type=jnp.float32)


def dot(a, b):
    return lax.dot_general(a, b, (((1,), (0,)), ((), ())), preferred_element_type=jnp.float32)


def attend_kernel(slots, ranges, tp_size, first_call, last_call, *refs):
    refs = list(refs)
    spans, tq, sq = refs[:3]
    del refs[:3]
    if last_call:
        stage, sems = refs[-2:]
        del refs[-2:]
    k_aug_ref = refs.pop()
    outs, refs = (refs[-2:], refs[:-2]) if last_call else (refs[-3:], refs[:-3])
    if not first_call:
        top_in, denominator_in, sum_in = refs[-3:]
        del refs[-3:]
    pieces = refs

    rows = tq.shape[0]
    half = GROUP * rows
    ctx = lax.axis_index("ctx").astype(jnp.int32)
    tp = lax.axis_index("tp").astype(jnp.int32)
    first_position = (ctx * tp_size + tp) * rows
    prefix, del_start, del_end = spans[0:1], spans[1:2], spans[2:3]
    lane = lax.broadcasted_iota(jnp.int32, (rows, HEAD_SIZE), 1)
    row = lax.broadcasted_iota(jnp.int32, (rows, HEAD_SIZE), 0)
    q_trace_aug = jnp.where(lane == row, 1.0, 0.0).astype(jnp.bfloat16)
    q_suffix_aug = jnp.where((lane == rows) | (lane == rows + 1 + row), 1.0, 0.0).astype(jnp.bfloat16)
    q_aug = jnp.concatenate([q_trace_aug] * GROUP + [q_suffix_aug] * GROUP, axis=0)
    for index, slot in enumerate(slots):
        kind, block = slot(ctx, tp)
        position = block * rows + row
        if kind == "trace":
            hidden_trace = (lane < rows) & (position > first_position + lane)
            hidden_suffix = (lane == rows) & (
                (position >= prefix) | ((position >= del_start) & (position < del_end))
            )
            hidden = hidden_trace | hidden_suffix
        else:
            hidden = (lane < rows) | ((lane > rows) & (position > tp * rows + (lane - rows - 1)))
        k_aug_ref[index * rows:(index + 1) * rows, :] = jnp.where(hidden, MASKED, 0.0).astype(jnp.bfloat16)
    filled, total = rows * len(slots), k_aug_ref.shape[0]
    if filled < total:
        k_aug_ref[filled:total, :] = jnp.full((total - filled, HEAD_SIZE), MASKED, jnp.bfloat16)
        padding = [jnp.zeros((total - filled, HEAD_SIZE), jnp.bfloat16)]
    else:
        padding = []
    ones = jnp.ones((total, HEAD_SIZE), jnp.bfloat16)

    def columns(index):
        return slice(index * HEAD_SIZE, (index + 1) * HEAD_SIZE)

    def stacked(index):
        parts = [piece[start:stop, columns(index)] for piece, (start, stop) in zip(pieces, ranges)]
        return jnp.concatenate(parts + padding, axis=0)

    def scores_of(g):
        query = jnp.concatenate(
            [ref[:, columns(g * GROUP + j)] for ref in (tq, sq) for j in range(GROUP)], axis=0
        )
        query = jnp.concatenate([query, q_aug], axis=1)
        return dot_t(query, jnp.concatenate([stacked(2 * g), k_aug_ref[...]], axis=1))

    def absorb_head(g, scores):
        top = jnp.broadcast_to(jnp.max(scores, axis=1, keepdims=True), (2 * half, HEAD_SIZE))
        if not first_call:
            old_top = top_in[g]
            top = jnp.maximum(old_top, top)
        shifted = scores - jnp.concatenate([top] * (total // HEAD_SIZE), axis=1)
        weights = jnp.exp2(shifted * SCALE).astype(jnp.bfloat16)
        both = dot(weights, jnp.concatenate([stacked(2 * g + 1), ones], axis=1))
        summed, denominator = both[:, :HEAD_SIZE], both[:, HEAD_SIZE:]
        if not first_call:
            rescale = jnp.exp2((old_top - top) * SCALE)
            summed = summed + sum_in[g] * rescale
            denominator = denominator + denominator_in[g] * rescale
        if last_call:
            inverse = pl.reciprocal(denominator, approx=True)
            inverse = inverse * (2.0 - denominator * inverse)
            result = (summed * inverse).astype(jnp.bfloat16)
            for side in range(2):
                for j in range(GROUP):
                    start = (side * GROUP + j) * rows
                    stage[side, :, columns(g * GROUP + j)] = result[start:start + rows]
                output_copy(side, g).start()
        else:
            for out, state in zip(outs, (top, denominator, summed)):
                out[g] = state

    def output_copy(side, g):
        group = pl.ds(g * GROUP * HEAD_SIZE, GROUP * HEAD_SIZE)
        return pltpu.make_async_copy(stage.at[side, :, group], outs[side].at[:, group], sems.at[side, g])

    ahead = scores_of(0)
    for g in range(KEY_VALUE_HEADS):
        now, ahead = ahead, scores_of(g + 1) if g + 1 < KEY_VALUE_HEADS else None
        absorb_head(g, now)
    if last_call:
        for g in range(KEY_VALUE_HEADS):
            for side in range(2):
                output_copy(side, g).wait()


def attend(spans, tq, sq, pieces, slots, tp_size, carry, last_call):
    first_call = carry is None
    rows = tq.shape[0]
    vmem = pl.BlockSpec(memory_space=pltpu.VMEM)
    operands = [spans, tq, sq, *(piece for piece, _, _ in pieces)]
    if not first_call:
        operands += list(carry)
    if last_call:
        out_shape = [jax.ShapeDtypeStruct(tq.shape, jnp.bfloat16)] * 2
        out_specs = [pl.BlockSpec(memory_space=pl.ANY)] * 2
        scratch = [pltpu.VMEM((2, *tq.shape), jnp.bfloat16), pltpu.SemaphoreType.DMA((2, KEY_VALUE_HEADS))]
    else:
        state = (KEY_VALUE_HEADS, 2 * GROUP * rows, HEAD_SIZE)
        out_shape = [jax.ShapeDtypeStruct(state, jnp.float32)] * 3
        out_specs = [vmem] * 3
        scratch = []
    ranges = tuple((first * rows, last * rows) for _, first, last in pieces)
    all_rows = pl.cdiv(sum(stop - start for start, stop in ranges), HEAD_SIZE) * HEAD_SIZE
    flops = 2 * 2 * QUERY_HEADS * rows * all_rows * PAIR * 2
    return pl.pallas_call(
        functools.partial(attend_kernel, slots, ranges, tp_size, first_call, last_call),
        out_shape=out_shape,
        in_specs=[vmem] * len(operands),
        out_specs=out_specs,
        scratch_shapes=[pltpu.VMEM((all_rows, HEAD_SIZE), jnp.bfloat16), *scratch],
        compiler_params=pltpu.CompilerParams(vmem_limit_bytes=32 * 1024 * 1024),
        cost_estimate=pl.CostEstimate(
            flops=COST_FACTOR * flops, bytes_accessed=all_rows * 4096, transcendentals=2 * QUERY_HEADS * rows * all_rows
        ),
    )(*operands)


def swap(array, axis, bit, size):
    return lax.ppermute(array, axis, [(i, i ^ bit) for i in range(size)])


def after(array, *others):
    return lax.optimization_barrier((array, *others))[0]


def local(ctx_size, tp_size, trace_q, trace_key_value, suffix_q, suffix_key_value, prefix_len, del_start, del_end):
    rows = trace_q.shape[0]
    spans = jnp.broadcast_to(jnp.stack([prefix_len, del_start, del_end]), (3, HEAD_SIZE))
    sq = suffix_q[0]
    suffix_own = suffix_key_value[0]

    core = lambda a: swap(a, "tp", 1, tp_size)
    across_y = lambda a: swap(a, "tp", 2, tp_size)
    across_x = lambda a: swap(a, "ctx", 1, ctx_size)
    along_z = lambda a, flip: swap(a, "ctx", 2 * flip, ctx_size)

    across_both = lambda a: lax.ppermute(
        a,
        ("ctx", "tp"),
        [(i * tp_size + j, (i ^ 1) * tp_size + (j ^ 2)) for i in range(ctx_size) for j in range(tp_size)],
    )

    def slot(place, c):
        if isinstance(place, int):
            return lambda ctx, tp: ("suffix", tp ^ place ^ c)
        z, x, y = place
        return lambda ctx, tp: (
            "trace",
            (ctx ^ (2 * z + x)) * tp_size + (tp ^ (2 * y + c)),
        )

    def slots_of(places, c=0):
        return [slot(place, c) for place in places]

    def absorb(pieces, slots, state, last_call=False):
        return attend(spans, trace_q, sq, pieces, slots, tp_size, state, last_call)

    if ctx_size == 8 and tp_size == 4:
        barrier = lax.optimization_barrier
        next_z, third_z = along_z(trace_key_value, 1), along_z(trace_key_value, 3)
        own_x, own_y = across_x(trace_key_value), across_y(trace_key_value)
        own_d = across_both(trace_key_value)
        own_d, third_z, next_z, own_y, own_x, spans = barrier((own_d, third_z, next_z, own_y, own_x, spans))

        near = jnp.concatenate([next_z, third_z], axis=0)
        far, third_d = along_z(third_z, 1), along_z(own_d, 3)
        near_x, near_y = across_x(near), across_y(near)
        far_x, far_y = across_x(far), across_y(jnp.concatenate([far, suffix_own], axis=0))
        plane = jnp.concatenate([trace_key_value, own_x, own_y, own_d, near, suffix_own], axis=0)
        here = [(0, 0, 0), (0, 1, 0), (0, 0, 1), (0, 1, 1), (1, 0, 0), (3, 0, 0), 0]
        plane, far = barrier((plane, far))
        state = absorb([(plane, 0, 7)], slots_of(here), None)

        near_y, plane, state = barrier((near_y, plane, state))
        plane_sibling = core(plane)
        near_x, state = barrier((near_x, state))
        next_d, far_d = across_x(near_y[:rows]), along_z(third_d, 1)
        sides = jnp.concatenate([near_x, near_y, far, third_d], axis=0)
        near_here = [(1, 1, 0), (3, 1, 0), (1, 0, 1), (3, 0, 1), (2, 0, 0), (3, 1, 1)]
        state = absorb([(sides, 0, 6), (plane_sibling, 0, 6)], slots_of(near_here) + slots_of(here[:6], 1), state)
        sides_sibling = core(sides)

        far_x, next_d, far_y, far_d, state = barrier((far_x, next_d, far_y, far_d, state))
        rest = jnp.concatenate([far_x, next_d, far_y, far_d], axis=0)
        rest_sibling = core(rest)
        rest_here = [(2, 1, 0), (1, 1, 1), (2, 0, 1), 2, (2, 1, 1)]
        state = absorb(
            [(plane_sibling, 6, 7), (sides_sibling, 0, 6), (rest, 0, 5)],
            slots_of(here[6:] + near_here, 1) + slots_of(rest_here),
            state,
        )
        trace_out, suffix_out = absorb([(rest_sibling, 0, 5)], slots_of(rest_here, 1), state, True)
    else:
        gathered = lax.all_gather(trace_key_value, ("ctx", "tp"), axis=0, tiled=True)
        suffix_all = lax.all_gather(suffix_own, "tp", axis=0, tiled=True)
        state = None
        for at in range(0, gathered.shape[0], CHUNK_ROWS):
            last_call = at + CHUNK_ROWS >= gathered.shape[0]
            pieces = [(gathered[at:at + CHUNK_ROWS], 0, min(CHUNK_ROWS, gathered.shape[0] - at) // rows)]
            slots = [
                lambda ctx, tp, block=block: ("trace", block)
                for block in range(at // rows, min(at + CHUNK_ROWS, gathered.shape[0]) // rows)
            ]
            if at == 0:
                pieces.append((suffix_all, 0, tp_size))
                slots += [lambda ctx, tp, block=block: ("suffix", block) for block in range(tp_size)]
            state = absorb(pieces, slots, state, last_call)
        trace_out, suffix_out = state
    return trace_out, suffix_out[None]


def solution(mesh):
    return jax.shard_map(
        functools.partial(local, mesh.shape["ctx"], mesh.shape["tp"]),
        mesh=mesh,
        in_specs=(
            P(("ctx", "tp"), None),
            P(("ctx", "tp"), None),
            P("ctx", "tp", None),
            P("ctx", "tp", None),
            P("ctx"),
            P("ctx"),
            P("ctx"),
        ),
        out_specs=(P(("ctx", "tp"), None), P("ctx", "tp", None)),
        check_vma=False,
    )
```

```python
import functools

import jax
import jax.numpy as jnp
from jax import lax
from jax.experimental import pallas as pl
from jax.experimental.pallas import tpu as pltpu
from jax.sharding import PartitionSpec as P

QUERY_HEADS = 40
KEY_VALUE_HEADS = 8
HEAD_SIZE = 128
GROUP = QUERY_HEADS // KEY_VALUE_HEADS
PAIR = 2 * HEAD_SIZE
LOG2E = 1.4426950408889634
SCALE = HEAD_SIZE ** (-0.5) * LOG2E
MASKED = -1e30
CHUNK_ROWS = 1024
COST_FACTOR = 10


def dot_t(a, b):
    return lax.dot_general(a, b, (((1,), (1,)), ((), ())), preferred_element_type=jnp.float32)


def dot(a, b):
    return lax.dot_general(a, b, (((1,), (0,)), ((), ())), preferred_element_type=jnp.float32)


def attend_kernel(slots, ranges, tp_size, first_call, last_call, *refs):
    refs = list(refs)
    spans, tq, sq = refs[:3]
    del refs[:3]
    if last_call:
        stage, sems = refs[-2:]
        del refs[-2:]
    k_aug_ref = refs.pop()
    outs, refs = (refs[-2:], refs[:-2]) if last_call else (refs[-3:], refs[:-3])
    if not first_call:
        top_in, denominator_in, sum_in = refs[-3:]
        del refs[-3:]
    pieces = refs

    rows = tq.shape[0]
    half = GROUP * rows
    ctx = lax.axis_index("ctx").astype(jnp.int32)
    tp = lax.axis_index("tp").astype(jnp.int32)
    first_position = (ctx * tp_size + tp) * rows
    prefix, del_start, del_end = spans[0:1], spans[1:2], spans[2:3]
    lane = lax.broadcasted_iota(jnp.int32, (rows, HEAD_SIZE), 1)
    row = lax.broadcasted_iota(jnp.int32, (rows, HEAD_SIZE), 0)
    q_trace_aug = jnp.where(lane == row, 1.0, 0.0).astype(jnp.bfloat16)
    q_suffix_aug = jnp.where((lane == rows) | (lane == rows + 1 + row), 1.0, 0.0).astype(jnp.bfloat16)
    q_aug = jnp.concatenate([q_trace_aug] * GROUP + [q_suffix_aug] * GROUP, axis=0)
    for index, slot in enumerate(slots):
        kind, block = slot(ctx, tp)
        position = block * rows + row
        if kind == "trace":
            hidden_trace = (lane < rows) & (position > first_position + lane)
            hidden_suffix = (lane == rows) & (
                (position >= prefix) | ((position >= del_start) & (position < del_end))
            )
            hidden = hidden_trace | hidden_suffix
        else:
            hidden = (lane < rows) | ((lane > rows) & (position > tp * rows + (lane - rows - 1)))
        k_aug_ref[index * rows:(index + 1) * rows, :] = jnp.where(hidden, MASKED, 0.0).astype(jnp.bfloat16)
    filled, total = rows * len(slots), k_aug_ref.shape[0]
    if filled < total:
        k_aug_ref[filled:total, :] = jnp.full((total - filled, HEAD_SIZE), MASKED, jnp.bfloat16)
        padding = [jnp.zeros((total - filled, HEAD_SIZE), jnp.bfloat16)]
    else:
        padding = []
    ones = jnp.ones((total, HEAD_SIZE), jnp.bfloat16)

    def columns(index):
        return slice(index * HEAD_SIZE, (index + 1) * HEAD_SIZE)

    def stacked(index):
        parts = [piece[start:stop, columns(index)] for piece, (start, stop) in zip(pieces, ranges)]
        return jnp.concatenate(parts + padding, axis=0)

    def scores_of(g):
        query = jnp.concatenate(
            [ref[:, columns(g * GROUP + j)] for ref in (tq, sq) for j in range(GROUP)], axis=0
        )
        query = jnp.concatenate([query, q_aug], axis=1)
        return dot_t(query, jnp.concatenate([stacked(2 * g), k_aug_ref[...]], axis=1))

    def absorb_head(g, scores):
        top = jnp.broadcast_to(jnp.max(scores, axis=1, keepdims=True), (2 * half, HEAD_SIZE))
        if not first_call:
            old_top = top_in[g]
            top = jnp.maximum(old_top, top)
        shifted = scores - jnp.concatenate([top] * (total // HEAD_SIZE), axis=1)
        weights = jnp.exp2(shifted * SCALE).astype(jnp.bfloat16)
        both = dot(weights, jnp.concatenate([stacked(2 * g + 1), ones], axis=1))
        summed, denominator = both[:, :HEAD_SIZE], both[:, HEAD_SIZE:]
        if not first_call:
            rescale = jnp.exp2((old_top - top) * SCALE)
            summed = summed + sum_in[g] * rescale
            denominator = denominator + denominator_in[g] * rescale
        if last_call:
            inverse = pl.reciprocal(denominator, approx=True)
            inverse = inverse * (2.0 - denominator * inverse)
            result = (summed * inverse).astype(jnp.bfloat16)
            for side in range(2):
                for j in range(GROUP):
                    start = (side * GROUP + j) * rows
                    stage[side, :, columns(g * GROUP + j)] = result[start:start + rows]
                output_copy(side, g).start()
        else:
            for out, state in zip(outs, (top, denominator, summed)):
                out[g] = state

    def output_copy(side, g):
        group = pl.ds(g * GROUP * HEAD_SIZE, GROUP * HEAD_SIZE)
        return pltpu.make_async_copy(stage.at[side, :, group], outs[side].at[:, group], sems.at[side, g])

    ahead = scores_of(0)
    for g in range(KEY_VALUE_HEADS):
        now, ahead = ahead, scores_of(g + 1) if g + 1 < KEY_VALUE_HEADS else None
        absorb_head(g, now)
    if last_call:
        for g in range(KEY_VALUE_HEADS):
            for side in range(2):
                output_copy(side, g).wait()


def attend(spans, tq, sq, pieces, slots, tp_size, carry, last_call):
    first_call = carry is None
    rows = tq.shape[0]
    vmem = pl.BlockSpec(memory_space=pltpu.VMEM)
    operands = [spans, tq, sq, *(piece for piece, _, _ in pieces)]
    if not first_call:
        operands += list(carry)
    if last_call:
        out_shape = [jax.ShapeDtypeStruct(tq.shape, jnp.bfloat16)] * 2
        out_specs = [pl.BlockSpec(memory_space=pl.ANY)] * 2
        scratch = [pltpu.VMEM((2, *tq.shape), jnp.bfloat16), pltpu.SemaphoreType.DMA((2, KEY_VALUE_HEADS))]
    else:
        state = (KEY_VALUE_HEADS, 2 * GROUP * rows, HEAD_SIZE)
        out_shape = [jax.ShapeDtypeStruct(state, jnp.float32)] * 3
        out_specs = [vmem] * 3
        scratch = []
    ranges = tuple((first * rows, last * rows) for _, first, last in pieces)
    all_rows = pl.cdiv(sum(stop - start for start, stop in ranges), HEAD_SIZE) * HEAD_SIZE
    flops = 2 * 2 * QUERY_HEADS * rows * all_rows * PAIR * 2
    return pl.pallas_call(
        functools.partial(attend_kernel, slots, ranges, tp_size, first_call, last_call),
        out_shape=out_shape,
        in_specs=[vmem] * len(operands),
        out_specs=out_specs,
        scratch_shapes=[pltpu.VMEM((all_rows, HEAD_SIZE), jnp.bfloat16), *scratch],
        compiler_params=pltpu.CompilerParams(vmem_limit_bytes=32 * 1024 * 1024),
        cost_estimate=pl.CostEstimate(
            flops=COST_FACTOR * flops, bytes_accessed=all_rows * 4096, transcendentals=2 * QUERY_HEADS * rows * all_rows
        ),
    )(*operands)


def swap(array, axis, bit, size):
    return lax.ppermute(array, axis, [(i, i ^ bit) for i in range(size)])


def after(array, *others):
    return lax.optimization_barrier((array, *others))[0]


def local(ctx_size, tp_size, trace_q, trace_key_value, suffix_q, suffix_key_value, prefix_len, del_start, del_end):
    rows = trace_q.shape[0]
    spans = jnp.broadcast_to(jnp.stack([prefix_len, del_start, del_end]), (3, HEAD_SIZE))
    sq = suffix_q[0]
    suffix_own = suffix_key_value[0]

    core = lambda a: swap(a, "tp", 1, tp_size)
    across_y = lambda a: swap(a, "tp", 2, tp_size)
    across_x = lambda a: swap(a, "ctx", 1, ctx_size)
    along_z = lambda a, flip: swap(a, "ctx", 2 * flip, ctx_size)

    across_both = lambda a: lax.ppermute(
        a,
        ("ctx", "tp"),
        [(i * tp_size + j, (i ^ 1) * tp_size + (j ^ 2)) for i in range(ctx_size) for j in range(tp_size)],
    )

    def slot(place, c):
        if isinstance(place, int):
            return lambda ctx, tp: ("suffix", tp ^ place ^ c)
        z, x, y = place
        return lambda ctx, tp: (
            "trace",
            (ctx ^ (2 * z + x)) * tp_size + (tp ^ (2 * y + c)),
        )

    def slots_of(places, c=0):
        return [slot(place, c) for place in places]

    def absorb(pieces, slots, state, last_call=False):
        return attend(spans, trace_q, sq, pieces, slots, tp_size, state, last_call)

    if ctx_size == 8 and tp_size == 4:
        barrier = lax.optimization_barrier
        next_z, third_z = along_z(trace_key_value, 1), along_z(trace_key_value, 3)
        own_x, own_y = across_x(trace_key_value), across_y(trace_key_value)
        own_d = across_both(trace_key_value)
        own_d, third_z, next_z, own_y, own_x, spans = barrier((own_d, third_z, next_z, own_y, own_x, spans))

        near = jnp.concatenate([next_z, third_z], axis=0)
        far, third_d = along_z(third_z, 1), along_z(own_d, 3)
        near_x, near_y = across_x(near), across_y(near)
        far_x, far_y = across_x(far), across_y(jnp.concatenate([far, suffix_own], axis=0))
        plane = jnp.concatenate([trace_key_value, own_x, own_y, own_d, near, suffix_own], axis=0)
        here = [(0, 0, 0), (0, 1, 0), (0, 0, 1), (0, 1, 1), (1, 0, 0), (3, 0, 0), 0]
        plane, far = barrier((plane, far))
        state = absorb([(plane, 0, 7)], slots_of(here), None)

        near_y, plane, state = barrier((near_y, plane, state))
        plane_sibling = core(plane)
        near_x, state = barrier((near_x, state))
        next_d, far_d = across_x(near_y[:rows]), along_z(third_d, 1)
        sides = jnp.concatenate([near_x, near_y, far, third_d], axis=0)
        near_here = [(1, 1, 0), (3, 1, 0), (1, 0, 1), (3, 0, 1), (2, 0, 0), (3, 1, 1)]
        state = absorb([(sides, 0, 6), (plane_sibling, 0, 6)], slots_of(near_here) + slots_of(here[:6], 1), state)
        sides_sibling = core(sides)

        far_x, far_y, far_d, state = barrier((far_x, far_y, far_d, state))
        rest = jnp.concatenate([far_x, far_y, far_d], axis=0)
        rest_sibling = core(rest)
        rest_here = [(2, 1, 0), (2, 0, 1), 2, (2, 1, 1)]
        state = absorb(
            [(plane_sibling, 6, 7), (sides_sibling, 0, 6), (rest, 0, 4)],
            slots_of(here[6:] + near_here, 1) + slots_of(rest_here),
            state,
        )
        next_d, state = barrier((next_d, state))
        last = [(1, 1, 1)]
        trace_out, suffix_out = absorb(
            [(next_d, 0, 1), (rest_sibling, 0, 4), (core(next_d), 0, 1)],
            slots_of(last) + slots_of(rest_here + last, 1),
            state,
            True,
        )
    else:
        gathered = lax.all_gather(trace_key_value, ("ctx", "tp"), axis=0, tiled=True)
        suffix_all = lax.all_gather(suffix_own, "tp", axis=0, tiled=True)
        state = None
        for at in range(0, gathered.shape[0], CHUNK_ROWS):
            last_call = at + CHUNK_ROWS >= gathered.shape[0]
            pieces = [(gathered[at:at + CHUNK_ROWS], 0, min(CHUNK_ROWS, gathered.shape[0] - at) // rows)]
            slots = [
                lambda ctx, tp, block=block: ("trace", block)
                for block in range(at // rows, min(at + CHUNK_ROWS, gathered.shape[0]) // rows)
            ]
            if at == 0:
                pieces.append((suffix_all, 0, tp_size))
                slots += [lambda ctx, tp, block=block: ("suffix", block) for block in range(tp_size)]
            state = absorb(pieces, slots, state, last_call)
        trace_out, suffix_out = state
    return trace_out, suffix_out[None]


def solution(mesh):
    return jax.shard_map(
        functools.partial(local, mesh.shape["ctx"], mesh.shape["tp"]),
        mesh=mesh,
        in_specs=(
            P(("ctx", "tp"), None),
            P(("ctx", "tp"), None),
            P("ctx", "tp", None),
            P("ctx", "tp", None),
            P("ctx"),
            P("ctx"),
            P("ctx"),
        ),
        out_specs=(P(("ctx", "tp"), None), P("ctx", "tp", None)),
        check_vma=False,
    )
```

```python
import functools

import jax
import jax.numpy as jnp
from jax import lax
from jax.experimental import pallas as pl
from jax.experimental.pallas import tpu as pltpu
from jax.sharding import PartitionSpec as P

QUERY_HEADS = 40
KEY_VALUE_HEADS = 8
HEAD_SIZE = 128
GROUP = QUERY_HEADS // KEY_VALUE_HEADS
PAIR = 2 * HEAD_SIZE
LOG2E = 1.4426950408889634
SCALE = HEAD_SIZE ** (-0.5) * LOG2E
MASKED = -1e30
CHUNK_ROWS = 1024
COST_FACTOR = 10


def dot_t(a, b):
    return lax.dot_general(a, b, (((1,), (1,)), ((), ())), preferred_element_type=jnp.float32)


def dot(a, b):
    return lax.dot_general(a, b, (((1,), (0,)), ((), ())), preferred_element_type=jnp.float32)


def attend_kernel(slots, ranges, tp_size, first_call, last_call, *refs):
    refs = list(refs)
    spans, tq, sq = refs[:3]
    del refs[:3]
    if last_call:
        stage, sems = refs[-2:]
        del refs[-2:]
    k_aug_ref = refs.pop()
    outs, refs = (refs[-2:], refs[:-2]) if last_call else (refs[-3:], refs[:-3])
    if not first_call:
        top_in, denominator_in, sum_in = refs[-3:]
        del refs[-3:]
    pieces = refs

    rows = tq.shape[0]
    half = GROUP * rows
    ctx = lax.axis_index("ctx").astype(jnp.int32)
    tp = lax.axis_index("tp").astype(jnp.int32)
    first_position = (ctx * tp_size + tp) * rows
    prefix, del_start, del_end = spans[0:1], spans[1:2], spans[2:3]
    lane = lax.broadcasted_iota(jnp.int32, (rows, HEAD_SIZE), 1)
    row = lax.broadcasted_iota(jnp.int32, (rows, HEAD_SIZE), 0)
    q_trace_aug = jnp.where(lane == row, 1.0, 0.0).astype(jnp.bfloat16)
    q_suffix_aug = jnp.where((lane == rows) | (lane == rows + 1 + row), 1.0, 0.0).astype(jnp.bfloat16)
    q_aug = jnp.concatenate([q_trace_aug] * GROUP + [q_suffix_aug] * GROUP, axis=0)
    for index, slot in enumerate(slots):
        kind, block = slot(ctx, tp)
        position = block * rows + row
        if kind == "trace":
            hidden_trace = (lane < rows) & (position > first_position + lane)
            hidden_suffix = (lane == rows) & (
                (position >= prefix) | ((position >= del_start) & (position < del_end))
            )
            hidden = hidden_trace | hidden_suffix
        else:
            hidden = (lane < rows) | ((lane > rows) & (position > tp * rows + (lane - rows - 1)))
        k_aug_ref[index * rows:(index + 1) * rows, :] = jnp.where(hidden, MASKED, 0.0).astype(jnp.bfloat16)
    filled, total = rows * len(slots), k_aug_ref.shape[0]
    if filled < total:
        k_aug_ref[filled:total, :] = jnp.full((total - filled, HEAD_SIZE), MASKED, jnp.bfloat16)
        padding = [jnp.zeros((total - filled, HEAD_SIZE), jnp.bfloat16)]
    else:
        padding = []
    ones = jnp.ones((total, HEAD_SIZE), jnp.bfloat16)

    def columns(index):
        return slice(index * HEAD_SIZE, (index + 1) * HEAD_SIZE)

    def stacked(index):
        parts = [piece[start:stop, columns(index)] for piece, (start, stop) in zip(pieces, ranges)]
        return jnp.concatenate(parts + padding, axis=0)

    def scores_of(g):
        query = jnp.concatenate(
            [ref[:, columns(g * GROUP + j)] for ref in (tq, sq) for j in range(GROUP)], axis=0
        )
        query = jnp.concatenate([query, q_aug], axis=1)
        return dot_t(query, jnp.concatenate([stacked(2 * g), k_aug_ref[...]], axis=1))

    def absorb_head(g, scores):
        top = jnp.broadcast_to(jnp.max(scores, axis=1, keepdims=True), (2 * half, HEAD_SIZE))
        if not first_call:
            old_top = top_in[g]
            top = jnp.maximum(old_top, top)
        shifted = scores - jnp.concatenate([top] * (total // HEAD_SIZE), axis=1)
        weights = jnp.exp2(shifted * SCALE).astype(jnp.bfloat16)
        both = dot(weights, jnp.concatenate([stacked(2 * g + 1), ones], axis=1))
        summed, denominator = both[:, :HEAD_SIZE], both[:, HEAD_SIZE:]
        if not first_call:
            rescale = jnp.exp2((old_top - top) * SCALE)
            summed = summed + sum_in[g] * rescale
            denominator = denominator + denominator_in[g] * rescale
        if last_call:
            inverse = pl.reciprocal(denominator, approx=True)
            inverse = inverse * (2.0 - denominator * inverse)
            result = (summed * inverse).astype(jnp.bfloat16)
            for side in range(2):
                for j in range(GROUP):
                    start = (side * GROUP + j) * rows
                    stage[side, :, columns(g * GROUP + j)] = result[start:start + rows]
                output_copy(side, g).start()
        else:
            for out, state in zip(outs, (top, denominator, summed)):
                out[g] = state

    def output_copy(side, g):
        group = pl.ds(g * GROUP * HEAD_SIZE, GROUP * HEAD_SIZE)
        return pltpu.make_async_copy(stage.at[side, :, group], outs[side].at[:, group], sems.at[side, g])

    ahead = scores_of(0)
    for g in range(KEY_VALUE_HEADS):
        now, ahead = ahead, scores_of(g + 1) if g + 1 < KEY_VALUE_HEADS else None
        absorb_head(g, now)
    if last_call:
        for g in range(KEY_VALUE_HEADS):
            for side in range(2):
                output_copy(side, g).wait()


def attend(spans, tq, sq, pieces, slots, tp_size, carry, last_call):
    first_call = carry is None
    rows = tq.shape[0]
    vmem = pl.BlockSpec(memory_space=pltpu.VMEM)
    operands = [spans, tq, sq, *(piece for piece, _, _ in pieces)]
    if not first_call:
        operands += list(carry)
    if last_call:
        out_shape = [jax.ShapeDtypeStruct(tq.shape, jnp.bfloat16)] * 2
        out_specs = [pl.BlockSpec(memory_space=pl.ANY)] * 2
        scratch = [pltpu.VMEM((2, *tq.shape), jnp.bfloat16), pltpu.SemaphoreType.DMA((2, KEY_VALUE_HEADS))]
    else:
        state = (KEY_VALUE_HEADS, 2 * GROUP * rows, HEAD_SIZE)
        out_shape = [jax.ShapeDtypeStruct(state, jnp.float32)] * 3
        out_specs = [vmem] * 3
        scratch = []
    ranges = tuple((first * rows, last * rows) for _, first, last in pieces)
    all_rows = pl.cdiv(sum(stop - start for start, stop in ranges), HEAD_SIZE) * HEAD_SIZE
    flops = 2 * 2 * QUERY_HEADS * rows * all_rows * PAIR * 2
    return pl.pallas_call(
        functools.partial(attend_kernel, slots, ranges, tp_size, first_call, last_call),
        out_shape=out_shape,
        in_specs=[vmem] * len(operands),
        out_specs=out_specs,
        scratch_shapes=[pltpu.VMEM((all_rows, HEAD_SIZE), jnp.bfloat16), *scratch],
        compiler_params=pltpu.CompilerParams(vmem_limit_bytes=32 * 1024 * 1024),
        cost_estimate=pl.CostEstimate(
            flops=COST_FACTOR * flops, bytes_accessed=all_rows * 4096, transcendentals=2 * QUERY_HEADS * rows * all_rows
        ),
    )(*operands)


def swap(array, axis, bit, size):
    return lax.ppermute(array, axis, [(i, i ^ bit) for i in range(size)])


def after(array, *others):
    return lax.optimization_barrier((array, *others))[0]


def local(ctx_size, tp_size, trace_q, trace_key_value, suffix_q, suffix_key_value, prefix_len, del_start, del_end):
    rows = trace_q.shape[0]
    spans = jnp.broadcast_to(jnp.stack([prefix_len, del_start, del_end]), (3, HEAD_SIZE))
    sq = suffix_q[0]
    suffix_own = suffix_key_value[0]

    core = lambda a: swap(a, "tp", 1, tp_size)
    across_y = lambda a: swap(a, "tp", 2, tp_size)
    across_x = lambda a: swap(a, "ctx", 1, ctx_size)
    along_z = lambda a, flip: swap(a, "ctx", 2 * flip, ctx_size)

    across_both = lambda a: lax.ppermute(
        a,
        ("ctx", "tp"),
        [(i * tp_size + j, (i ^ 1) * tp_size + (j ^ 2)) for i in range(ctx_size) for j in range(tp_size)],
    )

    def slot(place, c):
        if isinstance(place, int):
            return lambda ctx, tp: ("suffix", tp ^ place ^ c)
        z, x, y = place
        return lambda ctx, tp: (
            "trace",
            (ctx ^ (2 * z + x)) * tp_size + (tp ^ (2 * y + c)),
        )

    def slots_of(places, c=0):
        return [slot(place, c) for place in places]

    def absorb(pieces, slots, state, last_call=False):
        return attend(spans, trace_q, sq, pieces, slots, tp_size, state, last_call)

    if ctx_size == 8 and tp_size == 4:
        barrier = lax.optimization_barrier
        next_z, third_z = along_z(trace_key_value, 1), along_z(trace_key_value, 3)
        own_x, own_y = across_x(trace_key_value), across_y(trace_key_value)
        own_d = across_both(trace_key_value)
        own_d, third_z, next_z, own_y, own_x, spans = barrier((own_d, third_z, next_z, own_y, own_x, spans))

        near = jnp.concatenate([next_z, third_z], axis=0)
        far, third_d = along_z(third_z, 1), along_z(own_d, 3)
        near_x, near_y = across_x(near), across_y(near)
        plane = jnp.concatenate([trace_key_value, own_x, own_y, own_d, near, suffix_own], axis=0)
        here = [(0, 0, 0), (0, 1, 0), (0, 0, 1), (0, 1, 1), (1, 0, 0), (3, 0, 0), 0]
        far_y = across_y(jnp.concatenate([far, suffix_own], axis=0))
        plane, far = barrier((plane, far))
        state = absorb([(plane, 0, 7)], slots_of(here), None)
        plane, state = barrier((plane, state))
        plane_sibling = core(plane)

        near_x, near_y, third_d, state = barrier((near_x, near_y, third_d, state))
        far_x = across_x(jnp.concatenate([far, near_y[:rows]], axis=0))
        far_d = along_z(third_d, 1)
        sides = jnp.concatenate([near_x, near_y, far, third_d], axis=0)
        near_here = [(1, 1, 0), (3, 1, 0), (1, 0, 1), (3, 0, 1), (2, 0, 0), (3, 1, 1)]
        state = absorb([(sides, 0, 6), (plane_sibling, 0, 6)], slots_of(near_here) + slots_of(here[:6], 1), state)
        sides, state = barrier((sides, state))
        sides_sibling = core(sides)

        far_x, far_y, far_d, state = barrier((far_x, far_y, far_d, state))
        rest = jnp.concatenate([far_x, far_y, far_d], axis=0)
        rest_sibling = core(rest)
        rest_here = [(2, 1, 0), (1, 1, 1), (2, 0, 1), 2, (2, 1, 1)]
        state = absorb(
            [(plane_sibling, 6, 7), (sides_sibling, 0, 6), (rest, 0, 5)],
            slots_of(here[6:] + near_here, 1) + slots_of(rest_here),
            state,
        )
        trace_out, suffix_out = absorb([(rest_sibling, 0, 5)], slots_of(rest_here, 1), state, True)
    else:
        gathered = lax.all_gather(trace_key_value, ("ctx", "tp"), axis=0, tiled=True)
        suffix_all = lax.all_gather(suffix_own, "tp", axis=0, tiled=True)
        state = None
        for at in range(0, gathered.shape[0], CHUNK_ROWS):
            last_call = at + CHUNK_ROWS >= gathered.shape[0]
            pieces = [(gathered[at:at + CHUNK_ROWS], 0, min(CHUNK_ROWS, gathered.shape[0] - at) // rows)]
            slots = [
                lambda ctx, tp, block=block: ("trace", block)
                for block in range(at // rows, min(at + CHUNK_ROWS, gathered.shape[0]) // rows)
            ]
            if at == 0:
                pieces.append((suffix_all, 0, tp_size))
                slots += [lambda ctx, tp, block=block: ("suffix", block) for block in range(tp_size)]
            state = absorb(pieces, slots, state, last_call)
        trace_out, suffix_out = state
    return trace_out, suffix_out[None]


def solution(mesh):
    return jax.shard_map(
        functools.partial(local, mesh.shape["ctx"], mesh.shape["tp"]),
        mesh=mesh,
        in_specs=(
            P(("ctx", "tp"), None),
            P(("ctx", "tp"), None),
            P("ctx", "tp", None),
            P("ctx", "tp", None),
            P("ctx"),
            P("ctx"),
            P("ctx"),
        ),
        out_specs=(P(("ctx", "tp"), None), P("ctx", "tp", None)),
        check_vma=False,
    )
```

```python
import functools

import jax
import jax.numpy as jnp
from jax import lax
from jax.experimental import pallas as pl
from jax.experimental.pallas import tpu as pltpu
from jax.sharding import PartitionSpec as P

QUERY_HEADS = 40
KEY_VALUE_HEADS = 8
HEAD_SIZE = 128
GROUP = QUERY_HEADS // KEY_VALUE_HEADS
PAIR = 2 * HEAD_SIZE
LOG2E = 1.4426950408889634
SCALE = HEAD_SIZE ** (-0.5) * LOG2E
MASKED = -1e30
CHUNK_ROWS = 1024
COST_FACTOR = 10


def dot_t(a, b):
    return lax.dot_general(a, b, (((1,), (1,)), ((), ())), preferred_element_type=jnp.float32)


def dot(a, b):
    return lax.dot_general(a, b, (((1,), (0,)), ((), ())), preferred_element_type=jnp.float32)


def attend_kernel(slots, ranges, tp_size, first_call, last_call, *refs):
    refs = list(refs)
    spans, tq, sq = refs[:3]
    del refs[:3]
    if last_call:
        stage, sems = refs[-2:]
        del refs[-2:]
    k_aug_ref = refs.pop()
    outs, refs = (refs[-2:], refs[:-2]) if last_call else (refs[-3:], refs[:-3])
    if not first_call:
        top_in, denominator_in, sum_in = refs[-3:]
        del refs[-3:]
    pieces = refs

    rows = tq.shape[0]
    half = GROUP * rows
    ctx = lax.axis_index("ctx").astype(jnp.int32)
    tp = lax.axis_index("tp").astype(jnp.int32)
    first_position = (ctx * tp_size + tp) * rows
    prefix, del_start, del_end = spans[0:1], spans[1:2], spans[2:3]
    lane = lax.broadcasted_iota(jnp.int32, (rows, HEAD_SIZE), 1)
    row = lax.broadcasted_iota(jnp.int32, (rows, HEAD_SIZE), 0)
    q_trace_aug = jnp.where(lane == row, 1.0, 0.0).astype(jnp.bfloat16)
    q_suffix_aug = jnp.where((lane == rows) | (lane == rows + 1 + row), 1.0, 0.0).astype(jnp.bfloat16)
    q_aug = jnp.concatenate([q_trace_aug] * GROUP + [q_suffix_aug] * GROUP, axis=0)
    for index, slot in enumerate(slots):
        kind, block = slot(ctx, tp)
        position = block * rows + row
        if kind == "trace":
            hidden_trace = (lane < rows) & (position > first_position + lane)
            hidden_suffix = (lane == rows) & (
                (position >= prefix) | ((position >= del_start) & (position < del_end))
            )
            hidden = hidden_trace | hidden_suffix
        else:
            hidden = (lane < rows) | ((lane > rows) & (position > tp * rows + (lane - rows - 1)))
        k_aug_ref[index * rows:(index + 1) * rows, :] = jnp.where(hidden, MASKED, 0.0).astype(jnp.bfloat16)
    filled, total = rows * len(slots), k_aug_ref.shape[0]
    if filled < total:
        k_aug_ref[filled:total, :] = jnp.full((total - filled, HEAD_SIZE), MASKED, jnp.bfloat16)
        padding = [jnp.zeros((total - filled, HEAD_SIZE), jnp.bfloat16)]
    else:
        padding = []
    ones = jnp.ones((total, HEAD_SIZE), jnp.bfloat16)

    def columns(index):
        return slice(index * HEAD_SIZE, (index + 1) * HEAD_SIZE)

    def stacked(index):
        parts = [piece[start:stop, columns(index)] for piece, (start, stop) in zip(pieces, ranges)]
        return jnp.concatenate(parts + padding, axis=0)

    def scores_of(g):
        query = jnp.concatenate(
            [ref[:, columns(g * GROUP + j)] for ref in (tq, sq) for j in range(GROUP)], axis=0
        )
        query = jnp.concatenate([query, q_aug], axis=1)
        return dot_t(query, jnp.concatenate([stacked(2 * g), k_aug_ref[...]], axis=1))

    def absorb_head(g, scores):
        top = jnp.broadcast_to(jnp.max(scores, axis=1, keepdims=True), (2 * half, HEAD_SIZE))
        if not first_call:
            old_top = top_in[g]
            top = jnp.maximum(old_top, top)
        shifted = scores - jnp.concatenate([top] * (total // HEAD_SIZE), axis=1)
        weights = jnp.exp2(shifted * SCALE).astype(jnp.bfloat16)
        both = dot(weights, jnp.concatenate([stacked(2 * g + 1), ones], axis=1))
        summed, denominator = both[:, :HEAD_SIZE], both[:, HEAD_SIZE:]
        if not first_call:
            rescale = jnp.exp2((old_top - top) * SCALE)
            summed = summed + sum_in[g] * rescale
            denominator = denominator + denominator_in[g] * rescale
        if last_call:
            inverse = pl.reciprocal(denominator, approx=True)
            inverse = inverse * (2.0 - denominator * inverse)
            result = (summed * inverse).astype(jnp.bfloat16)
            for side in range(2):
                for j in range(GROUP):
                    start = (side * GROUP + j) * rows
                    stage[side, :, columns(g * GROUP + j)] = result[start:start + rows]
                output_copy(side, g).start()
        else:
            for out, state in zip(outs, (top, denominator, summed)):
                out[g] = state

    def output_copy(side, g):
        group = pl.ds(g * GROUP * HEAD_SIZE, GROUP * HEAD_SIZE)
        return pltpu.make_async_copy(stage.at[side, :, group], outs[side].at[:, group], sems.at[side, g])

    ahead = scores_of(0)
    for g in range(KEY_VALUE_HEADS):
        now, ahead = ahead, scores_of(g + 1) if g + 1 < KEY_VALUE_HEADS else None
        absorb_head(g, now)
    if last_call:
        for g in range(KEY_VALUE_HEADS):
            for side in range(2):
                output_copy(side, g).wait()


def attend(spans, tq, sq, pieces, slots, tp_size, carry, last_call):
    first_call = carry is None
    rows = tq.shape[0]
    vmem = pl.BlockSpec(memory_space=pltpu.VMEM)
    operands = [spans, tq, sq, *(piece for piece, _, _ in pieces)]
    if not first_call:
        operands += list(carry)
    if last_call:
        out_shape = [jax.ShapeDtypeStruct(tq.shape, jnp.bfloat16)] * 2
        out_specs = [pl.BlockSpec(memory_space=pl.ANY)] * 2
        scratch = [pltpu.VMEM((2, *tq.shape), jnp.bfloat16), pltpu.SemaphoreType.DMA((2, KEY_VALUE_HEADS))]
    else:
        state = (KEY_VALUE_HEADS, 2 * GROUP * rows, HEAD_SIZE)
        out_shape = [jax.ShapeDtypeStruct(state, jnp.float32)] * 3
        out_specs = [vmem] * 3
        scratch = []
    ranges = tuple((first * rows, last * rows) for _, first, last in pieces)
    all_rows = pl.cdiv(sum(stop - start for start, stop in ranges), HEAD_SIZE) * HEAD_SIZE
    flops = 2 * 2 * QUERY_HEADS * rows * all_rows * PAIR * 2
    return pl.pallas_call(
        functools.partial(attend_kernel, slots, ranges, tp_size, first_call, last_call),
        out_shape=out_shape,
        in_specs=[vmem] * len(operands),
        out_specs=out_specs,
        scratch_shapes=[pltpu.VMEM((all_rows, HEAD_SIZE), jnp.bfloat16), *scratch],
        compiler_params=pltpu.CompilerParams(vmem_limit_bytes=32 * 1024 * 1024),
        cost_estimate=pl.CostEstimate(
            flops=COST_FACTOR * flops, bytes_accessed=all_rows * 4096, transcendentals=2 * QUERY_HEADS * rows * all_rows
        ),
    )(*operands)


def swap(array, axis, bit, size):
    return lax.ppermute(array, axis, [(i, i ^ bit) for i in range(size)])


def after(array, *others):
    return lax.optimization_barrier((array, *others))[0]


def local(ctx_size, tp_size, trace_q, trace_key_value, suffix_q, suffix_key_value, prefix_len, del_start, del_end):
    rows = trace_q.shape[0]
    spans = jnp.broadcast_to(jnp.stack([prefix_len, del_start, del_end]), (3, HEAD_SIZE))
    sq = suffix_q[0]
    suffix_own = suffix_key_value[0]

    core = lambda a: swap(a, "tp", 1, tp_size)
    across_y = lambda a: swap(a, "tp", 2, tp_size)
    across_x = lambda a: swap(a, "ctx", 1, ctx_size)
    along_z = lambda a, flip: swap(a, "ctx", 2 * flip, ctx_size)

    across_both = lambda a: lax.ppermute(
        a,
        ("ctx", "tp"),
        [(i * tp_size + j, (i ^ 1) * tp_size + (j ^ 2)) for i in range(ctx_size) for j in range(tp_size)],
    )

    def slot(place, c):
        if isinstance(place, int):
            return lambda ctx, tp: ("suffix", tp ^ place ^ c)
        z, x, y = place
        return lambda ctx, tp: (
            "trace",
            (ctx ^ (2 * z + x)) * tp_size + (tp ^ (2 * y + c)),
        )

    def slots_of(places, c=0):
        return [slot(place, c) for place in places]

    def absorb(pieces, slots, state, last_call=False):
        return attend(spans, trace_q, sq, pieces, slots, tp_size, state, last_call)

    if ctx_size == 8 and tp_size == 4:
        barrier = lax.optimization_barrier
        next_z, third_z = along_z(trace_key_value, 1), along_z(trace_key_value, 3)
        own_x, own_y = across_x(trace_key_value), across_y(trace_key_value)
        own_d = across_both(trace_key_value)
        own_d, third_z, next_z, own_y, own_x, spans = barrier((own_d, third_z, next_z, own_y, own_x, spans))

        near = jnp.concatenate([next_z, third_z], axis=0)
        far, third_d = along_z(third_z, 1), along_z(own_d, 3)
        near_x, near_y = across_x(near), across_y(near)
        plane = jnp.concatenate([trace_key_value, own_x, own_y, own_d, near, suffix_own], axis=0)
        here = [(0, 0, 0), (0, 1, 0), (0, 0, 1), (0, 1, 1), (1, 0, 0), (3, 0, 0), 0]
        far_y = across_y(jnp.concatenate([far, suffix_own], axis=0))
        plane, far = barrier((plane, far))
        state = absorb([(plane, 0, 7)], slots_of(here), None)
        near_x, near_y, plane, state = barrier((near_x, near_y, plane, state))
        plane_sibling = core(plane)
        far_x = across_x(jnp.concatenate([far, near_y[:rows]], axis=0))
        third_d, plane_sibling = barrier((third_d, plane_sibling))
        far_d = along_z(third_d, 1)
        sides = jnp.concatenate([near_x, near_y, far, third_d], axis=0)
        near_here = [(1, 1, 0), (3, 1, 0), (1, 0, 1), (3, 0, 1), (2, 0, 0), (3, 1, 1)]
        state = absorb([(sides, 0, 6), (plane_sibling, 0, 6)], slots_of(near_here) + slots_of(here[:6], 1), state)
        sides, state = barrier((sides, state))
        sides_sibling = core(sides)

        far_x, far_y, far_d, state = barrier((far_x, far_y, far_d, state))
        rest = jnp.concatenate([far_x, far_y, far_d], axis=0)
        rest_sibling = core(rest)
        rest_here = [(2, 1, 0), (1, 1, 1), (2, 0, 1), 2, (2, 1, 1)]
        state = absorb(
            [(plane_sibling, 6, 7), (sides_sibling, 0, 6), (rest, 0, 5)],
            slots_of(here[6:] + near_here, 1) + slots_of(rest_here),
            state,
        )
        trace_out, suffix_out = absorb([(rest_sibling, 0, 5)], slots_of(rest_here, 1), state, True)
    else:
        gathered = lax.all_gather(trace_key_value, ("ctx", "tp"), axis=0, tiled=True)
        suffix_all = lax.all_gather(suffix_own, "tp", axis=0, tiled=True)
        state = None
        for at in range(0, gathered.shape[0], CHUNK_ROWS):
            last_call = at + CHUNK_ROWS >= gathered.shape[0]
            pieces = [(gathered[at:at + CHUNK_ROWS], 0, min(CHUNK_ROWS, gathered.shape[0] - at) // rows)]
            slots = [
                lambda ctx, tp, block=block: ("trace", block)
                for block in range(at // rows, min(at + CHUNK_ROWS, gathered.shape[0]) // rows)
            ]
            if at == 0:
                pieces.append((suffix_all, 0, tp_size))
                slots += [lambda ctx, tp, block=block: ("suffix", block) for block in range(tp_size)]
            state = absorb(pieces, slots, state, last_call)
        trace_out, suffix_out = state
    return trace_out, suffix_out[None]


def solution(mesh):
    return jax.shard_map(
        functools.partial(local, mesh.shape["ctx"], mesh.shape["tp"]),
        mesh=mesh,
        in_specs=(
            P(("ctx", "tp"), None),
            P(("ctx", "tp"), None),
            P("ctx", "tp", None),
            P("ctx", "tp", None),
            P("ctx"),
            P("ctx"),
            P("ctx"),
        ),
        out_specs=(P(("ctx", "tp"), None), P("ctx", "tp", None)),
        check_vma=False,
    )
```
